32 devices in a mesh: section: 2 (over core), dp: 16 (over z, y, x).
Axes of the slice: x: 2, y: 2, z: 4, core: 2. Of those that a mesh axis runs over, the one named last changes fastest.
Arguments:
- inputs: bfloat16 [6, 8192, 384], P(None, 'dp'), may hold values from -120 to 120
- series_id: int32 [6, 8192], P(None, 'dp'), may hold values from 0 to 63, as said below
- item_offset: int32 [6, 8192], P(None, 'dp'), may hold values from 0 to 383, as said below
- variate_offset: int32 [6, 8192], P(None, 'dp'), may hold values from 0 to 511, as said below
- cotangent: bfloat16 [6, 8192, 384], P(None, 'dp'), may hold values from -30 to 30
- attention_gain: bfloat16 [2, 384], P('section'), may hold values from 0.099609375 to 1.8984375
- query_weight: bfloat16 [2, 384, 384], P('section'), may hold values from -0.3125 to 0.3125
- key_weight: bfloat16 [2, 384, 384], P('section'), may hold values from -0.3125 to 0.3125
- value_weight: bfloat16 [2, 384, 384], P('section'), may hold values from -0.3125 to 0.3125
- out_weight: bfloat16 [2, 384, 384], P('section'), may hold values from -1.25 to 1.25
- variate_bias: bfloat16 [2, 6, 2], P('section'), may hold values from -3 to 3
- feed_gain: bfloat16 [2, 384], P('section'), may hold values from 0.099609375 to 1.8984375
- gate_weight: bfloat16 [2, 384, 1024], P('section'), may hold values from -0.3125 to 0.3125
- up_weight: bfloat16 [2, 384, 1024], P('section'), may hold values from -0.3125 to 0.3125
- down_weight: bfloat16 [2, 1024, 384], P('section'), may hold values from -0.1875 to 0.1875
Outputs:
- section_output: bfloat16 [2, 6, 8192, 384], P('section', None, 'dp')
- input_grads: float32 [2, 6, 8192, 384], P('section', None, 'dp')
- grad_attention_gain: float32 [2, 384], P('section')
- grad_query: float32 [2, 384, 384], P('section')
- grad_key: float32 [2, 384, 384], P('section')
- grad_value: float32 [2, 384, 384], P('section')
- grad_out: float32 [2, 384, 384], P('section')
- grad_bias: float32 [2, 6, 2], P('section')
- grad_feed_gain: float32 [2, 384], P('section')
- grad_gate: float32 [2, 384, 1024], P('section')
- grad_up: float32 [2, 384, 1024], P('section')
- grad_down: float32 [2, 1024, 384], P('section')
The draws below stay inside these ranges and needn't reach their ends.
Inputs may be any that keep to these rules, and one draw needn't show every extreme that they name: `series_id`: tokens of one variate share a series; in each micro-batch one series, drawn from the seed, holds the first variate of every block of 512 tokens. Each aligned block of 512 tokens holds two items, runs of tokens; the first begins at 0, so a token's item_offset is at most its position in the block. Variates are runs within an item; a token's variate_offset lies between its item_offset and its position in the block.
All inputs are finite; a program needn't handle non-finite values.
Results may differ from the reference program's by a relative error of at most 0.015.
Values may be sent and summed in bfloat16 or wider, within the bound.
No kernel may reach another device: no remote copies, remote signals or barrier semaphores. Data moves between devices by JAX's collectives and lax.ppermute only.
A program may use at most 320 MiB of HBM per device.

```python
import jax
import jax.numpy as jnp
from jax import lax

D = 384
H = 6
HD = 64
FF = 1024
BLOCK = 512
MICRO = 6
TOKENS = 8192
NSER = 64


def layout(key):
    block_total = TOKENS // BLOCK
    cut_points = jax.random.randint(jax.random.fold_in(key, 11), (MICRO, block_total, 1), BLOCK // 4, 3 * BLOCK // 4)
    cut_points = cut_points.at[0, 0, 0].set(3 * BLOCK // 4 - 1)
    position = jnp.arange(BLOCK, dtype=jnp.int32)[None, None, :]
    item_rows = jnp.where(position < cut_points, 0, cut_points)
    lengths = jax.random.randint(jax.random.fold_in(key, 12), (MICRO, block_total, 2), max(BLOCK // 32, 2), BLOCK // 4 + 1)
    lengths = lengths.at[0, 0, 1].set(BLOCK // 4)
    run_length = jnp.where(position < cut_points, lengths[:, :, :1], lengths[:, :, 1:])
    variate_rows = item_rows + (position - item_rows) // run_length * run_length
    drawn = jax.random.randint(jax.random.fold_in(key, 13), (MICRO, block_total, BLOCK), 0, NSER)
    drawn = drawn.at[0, block_total - 1, :].set(NSER - 1)
    series = jnp.take_along_axis(drawn, variate_rows, axis=2)
    common = jax.random.randint(jax.random.fold_in(key, 14), (MICRO, 1, 1), 0, NSER)
    series = jnp.where(variate_rows == 0, common, series)

    def flatten(array):
        return array.reshape(MICRO, TOKENS).astype(jnp.int32)
    return (flatten(series), flatten(item_rows), flatten(variate_rows))


def shared_noise(key):
    noise = jax.random.normal(jax.random.fold_in(key, 21), (MICRO, TOKENS, D), jnp.float32)
    return jnp.clip(noise, -6.0, 6.0)


def per_token(table, series):
    return jnp.take_along_axis(table, series, axis=1)


def draw_series_id(key, part):
    return layout(key)[0]


def draw_item_offset(key, part):
    return layout(key)[1]


def draw_variate_offset(key, part):
    return layout(key)[2]


def draw_inputs(key, part):
    series = layout(key)[0]
    noise = shared_noise(key)
    key = jax.random.fold_in(key, 31)
    key_centre, key_spread = jax.random.split(key, 2)
    centres = jnp.clip(2.0 * jax.random.normal(key_centre, (MICRO, NSER), jnp.float32), -6.0, 6.0)
    spreads = jnp.exp(jax.random.uniform(key_spread, (MICRO, NSER), jnp.float32, jnp.log(0.5), jnp.log(4.0)))
    rising = 1.0 + 2.0 * jnp.arange(TOKENS, dtype=jnp.float32) / (TOKENS - 1)
    values = (per_token(centres, series)[..., None] + per_token(spreads, series)[..., None] * noise) * rising[None, :, None]
    return values.astype(jnp.bfloat16)


def draw_cotangent(key, part):
    series = layout(key)[0]
    noise = shared_noise(key)
    key = jax.random.fold_in(key, 41)
    key_offset, key_weight, key_fresh = jax.random.split(key, 3)
    offsets = jnp.clip(jax.random.normal(key_offset, (MICRO, NSER), jnp.float32), -3.0, 3.0)
    weights = 0.7 * jnp.clip(jax.random.normal(key_weight, (MICRO, NSER), jnp.float32), -3.0, 3.0)
    fresh = jnp.clip(jax.random.normal(key_fresh, (MICRO, TOKENS, D), jnp.float32), -5.0, 5.0)
    return (fresh + per_token(offsets, series)[..., None] + per_token(weights, series)[..., None] * noise).astype(jnp.bfloat16)


def block_scale(key, extent, cuts, smallest, high):
    factor_of = 1.0
    for dim, blocks in cuts:
        heights = jax.random.uniform(jax.random.fold_in(jax.random.fold_in(key, 6), dim), (blocks,), jnp.float32, smallest / len(cuts), high / len(cuts))
        factor_of = factor_of * jnp.repeat(jnp.exp(heights), extent[dim] // blocks).reshape((-1,) + (1,) * (len(extent) - 1 - dim))
    return factor_of


def scatter_about(rng, extent, scale, most, cuts=(), kind=jnp.bfloat16):
    loudness = block_scale(rng, extent, cuts, -0.22, 0.18) if cuts else 1.0
    result = jax.random.normal(rng, extent, jnp.float32) * scale * loudness
    return jnp.minimum(jnp.maximum(result, -most), most).astype(kind)


def setup_inputs(seed: int = 0) -> dict:
    keys = jax.random.split(jax.random.key(seed), 16)
    return {
        "inputs": draw_inputs(jax.random.fold_in(keys[15], 71), 0),
        "series_id": draw_series_id(jax.random.fold_in(keys[15], 71), 0),
        "item_offset": draw_item_offset(jax.random.fold_in(keys[15], 71), 0),
        "variate_offset": draw_variate_offset(jax.random.fold_in(keys[15], 71), 0),
        "cotangent": draw_cotangent(jax.random.fold_in(keys[15], 71), 0),
        "attention_gain": jnp.clip(1.0 + 0.18 * jax.random.normal(keys[5], (2, D), jnp.float32), 0.099609375, 1.8984375).astype(jnp.bfloat16),
        "query_weight": scatter_about(keys[6], (2, D, D), D ** -0.5, 0.3125, ((0, 2),)),
        "key_weight": scatter_about(keys[7], (2, D, D), D ** -0.5, 0.3125, ((0, 2),)),
        "value_weight": scatter_about(keys[8], (2, D, D), D ** -0.5, 0.3125, ((0, 2),)),
        "out_weight": scatter_about(keys[9], (2, D, D), (D // 16) ** -0.5, 1.25, ((0, 2),)),
        "variate_bias": scatter_about(keys[10], (2, H, 2), 1.0, 3.0, ((0, 2),)),
        "feed_gain": jnp.clip(1.0 + 0.18 * jax.random.normal(keys[11], (2, D), jnp.float32), 0.099609375, 1.8984375).astype(jnp.bfloat16),
        "gate_weight": scatter_about(keys[12], (2, D, FF), D ** -0.5, 0.3125, ((0, 2),)),
        "up_weight": scatter_about(keys[13], (2, D, FF), D ** -0.5, 0.3125, ((0, 2),)),
        "down_weight": scatter_about(keys[14], (2, FF, D), FF ** -0.5, 0.1875, ((0, 2),)),
    }


@jax.custom_vjp
def low(v):
    return lax.optimization_barrier(v.astype(jnp.bfloat16)).astype(jnp.float32)

@jax.custom_vjp
def low_back(v):
    return v

def low_keep(v):
    return (low(v), None)

def low_pass(kept, grad):
    return (grad,)

def back_keep(v):
    return (v, None)

def back_low(kept, grad):
    return (low(grad),)
low.defvjp(low_keep, low_pass)
low_back.defvjp(back_keep, back_low)
norm_epsilon = 1e-05
scale_epsilon = 1e-05
masked_score = -1e+30
highest = lax.Precision.HIGHEST

def matmul(left, right):
    return jnp.dot(left, right, precision=highest, preferred_element_type=jnp.float32)

def rms_norm(hidden, gains):
    return hidden * lax.rsqrt(lax.optimization_barrier(jnp.mean(hidden * hidden, axis=-1, keepdims=True)) + norm_epsilon) * gains

def rotary(time_rows):
    half_size = HD // 2
    frequency = 10000.0 ** (-jnp.arange(half_size, dtype=jnp.float32) * (2.0 / HD))
    angles = time_rows.astype(jnp.float32)[:, None] * frequency[None, :]
    return (jnp.cos(angles), jnp.sin(angles))

def turn(values, cosine, sine_part):
    half_size = values.shape[-1] // 2
    lower_half = values[..., :half_size]
    upper_half = values[..., half_size:]
    cosine = cosine[:, None, :]
    sine_part = sine_part[:, None, :]
    return jnp.concatenate([lower_half * cosine - upper_half * sine_part, upper_half * cosine + lower_half * sine_part], axis=-1)

def attend_block(queries, key_rows, value_rows, item_rows, variate_rows, variate_bias):
    scores = jnp.einsum('qhe,khe->hqk', queries, key_rows, precision=highest) * HD ** (-0.5)
    same_variate = variate_rows[:, None] == variate_rows[None, :]
    same_item = item_rows[:, None] == item_rows[None, :]
    bias_term = jnp.where(same_variate[None], variate_bias[:, 0][:, None, None], variate_bias[:, 1][:, None, None])
    scores = low_back(scores + bias_term)
    scores = jnp.where(same_item[None], scores, masked_score)
    peak_score = lax.optimization_barrier(jnp.max(scores, axis=-1, keepdims=True))
    exponent = jnp.exp(scores - peak_score)
    softmax_low = low(exponent / lax.optimization_barrier(jnp.sum(exponent, axis=-1, keepdims=True)))
    return jnp.einsum('hqk,khe->qhe', softmax_low, value_rows, precision=highest)

def layer(hidden, time_rows, item_rows, variate_rows, weights):
    attention_gain, query_weight, key_weight, value_weight, out_weight, variate_bias, feed_gain, gate_weight, up_weight, down_weight = weights
    row_count = hidden.shape[0]
    cosine, sine_part = rotary(time_rows)
    normed = low(rms_norm(hidden, attention_gain))

    def by_heads(matrix):
        return matrix.reshape(row_count, H, HD)
    queries = low(turn(by_heads(low_back(matmul(normed, query_weight))), cosine, sine_part))
    key_rows = low(turn(by_heads(low_back(matmul(normed, key_weight))), cosine, sine_part))
    value_rows = low(by_heads(low_back(matmul(normed, value_weight))))
    block_count = row_count // BLOCK

    def by_block(array):
        return array.reshape((block_count, BLOCK) + array.shape[1:])

    def single_block(pieces):
        return attend_block(pieces[0], pieces[1], pieces[2], pieces[3], pieces[4], variate_bias)
    attended = lax.map(jax.checkpoint(single_block), (by_block(queries), by_block(key_rows), by_block(value_rows), by_block(item_rows), by_block(variate_rows)))
    mixed = low(low_back(attended.reshape(row_count, D)))
    middle = hidden + low_back(matmul(mixed, out_weight))
    normed_feed = low(rms_norm(middle, feed_gain))
    gate_part = low_back(matmul(normed_feed, gate_weight))
    up_part = low_back(matmul(normed_feed, up_weight))
    activated = low(jax.nn.silu(gate_part) * up_part)
    return low(middle + matmul(activated, down_weight))

def standardize(inputs_float, series_all):

    def per_batch(pieces):
        values, series = pieces
        counts = jax.ops.segment_sum(jnp.ones((TOKENS,), jnp.float32), series, NSER)
        entries = jnp.maximum(counts, 1.0) * D
        centre = jax.ops.segment_sum(lax.optimization_barrier(jnp.sum(values, axis=-1)), series, NSER) / entries
        centred = values - centre[series][:, None]
        spread = jax.ops.segment_sum(lax.optimization_barrier(jnp.sum(centred * centred, axis=-1)), series, NSER)
        scaling = jnp.sqrt(spread / entries + scale_epsilon)
        return centred / scaling[series][:, None]
    return lax.map(per_batch, (inputs_float, series_all))

def reference(inputs, series_id, item_offset, variate_offset, cotangent, attention_gain, query_weight, key_weight, value_weight, out_weight, variate_bias, feed_gain, gate_weight, up_weight, down_weight):
    stacked = tuple((weight.astype(jnp.float32) for weight in (attention_gain, query_weight, key_weight, value_weight, out_weight, variate_bias, feed_gain, gate_weight, up_weight, down_weight)))
    position = jnp.arange(TOKENS, dtype=jnp.int32) % BLOCK
    time_all = (position[None, :] - variate_offset).astype(jnp.int32)

    def forward(inputs_float, nudge, weights):
        standard = standardize(inputs_float, series_id)
        section_zero = tuple((weight[0] for weight in weights))
        section_one = tuple((weight[1] for weight in weights))

        def per_batch(pieces):
            standard_rows, nudge_rows, time_rows, item_rows, variate_rows = pieces
            first_out = layer(standard_rows, time_rows, item_rows, variate_rows, section_zero)
            second_in = low_back(first_out + nudge_rows)
            second_out = layer(second_in, time_rows, item_rows, variate_rows, section_one)
            return (first_out, second_out)
        return lax.map(per_batch, (standard, nudge, time_all, item_offset, variate_offset))
    inputs_float = inputs.astype(jnp.float32)
    nudge = jnp.zeros(inputs.shape, jnp.float32)
    (first_out, second_out), pullback = jax.vjp(forward, inputs_float, nudge, stacked)
    input_grad, nudge_grad, weight_grads = pullback((jnp.zeros_like(first_out), cotangent.astype(jnp.float32)))
    section_output = jnp.stack([first_out, second_out]).astype(jnp.bfloat16)
    input_grads = jnp.stack([input_grad, nudge_grad])
    return (section_output, input_grads, weight_grads[0], weight_grads[1], weight_grads[2], weight_grads[3], weight_grads[4], weight_grads[5], weight_grads[6], weight_grads[7], weight_grads[8], weight_grads[9])
```

```python
import functools

import jax
import jax.numpy as jnp
from jax import lax
from jax.experimental import pallas as pl
from jax.experimental.pallas import tpu as pltpu
from jax.sharding import PartitionSpec as P

HD = 64
BLOCK = 512
SER_DEV = 4
LANES = 128
CHUNK = 256

norm_epsilon = 1e-05
scale_epsilon = 1e-05
masked_score = -1e30

f32 = jnp.float32
bf16 = jnp.bfloat16

AS_IS = (((1,), (0,)), ((), ()))
RIGHT_T = (((1,), (1,)), ((), ()))
LEFT_T = (((0,), (0,)), ((), ()))


def dot(left, right, dims=AS_IS):
    return lax.dot_general(left, right, dims, preferred_element_type=f32)


def column(row):
    return jnp.broadcast_to(row.astype(f32), (LANES, row.shape[1])).T


def lane_index(rows):
    return lax.broadcasted_iota(jnp.int32, (rows, LANES), 1)


def swap_halves(x):
    low_half = (lane_index(x.shape[0]) % HD) < HD // 2
    return jnp.where(low_half, pltpu.roll(x, LANES - HD // 2, 1), pltpu.roll(x, HD // 2, 1))


def turn(x, cosine, sine):
    return x * cosine + swap_halves(x) * sine


def turn_back(x, cosine, sine):
    return x * cosine - swap_halves(x) * sine


def inverse_rms(x):
    return lax.rsqrt(jnp.mean(x * x, axis=1, keepdims=True) + norm_epsilon)


def series_hits(sid_col, piece):
    return sid_col == (lane_index(sid_col.shape[0]) + piece * LANES).astype(f32)


def rows_of(hits, per_series):
    return jnp.sum(jnp.where(hits, per_series, 0.0), axis=1, keepdims=True)


def series_of(hits, per_row):
    return jnp.sum(jnp.where(hits, per_row, 0.0), axis=0, keepdims=True)


def stats_body(x_ref, sid_ref, out_ref):
    i = pl.program_id(0)
    x = x_ref[0].astype(f32)
    width = x.shape[1]
    sid_col = column(sid_ref[pl.ds(i, 1), :])
    pieces = out_ref.shape[-1] // LANES
    totals = jnp.sum(x, axis=1, keepdims=True)
    centre = jnp.zeros_like(totals)
    out_ref[0] = jnp.zeros(out_ref.shape[1:], f32)
    for piece in range(pieces):
        hits = series_hits(sid_col, piece)
        count = series_of(hits, 1.0)
        total = series_of(hits, totals)
        centre = centre + rows_of(hits, total / (jnp.maximum(count, 1.0) * width))
        out_ref[0, 0:1, piece * LANES : (piece + 1) * LANES] = count
        out_ref[0, 1:2, piece * LANES : (piece + 1) * LANES] = total
    centred = x - centre
    squares = jnp.sum(centred * centred, axis=1, keepdims=True)
    for piece in range(pieces):
        hits = series_hits(sid_col, piece)
        out_ref[0, 2:3, piece * LANES : (piece + 1) * LANES] = series_of(hits, squares)


def merge_stats(here, there, width):
    count_a, total_a, spread_a = here[:, 0], here[:, 1], here[:, 2]
    count_b, total_b, spread_b = there[:, 0], there[:, 1], there[:, 2]
    count = count_a + count_b
    gap = total_a / (jnp.maximum(count_a, 1.0) * width) - total_b / (
        jnp.maximum(count_b, 1.0) * width
    )
    weight = count_a * count_b * width / jnp.maximum(count, 1.0)
    spread = spread_a + spread_b + gap * gap * weight
    rest = jnp.zeros_like(here[:, 3:])
    return jnp.concatenate(
        [jnp.stack([count, total_a + total_b, spread], axis=1), rest], axis=1
    )


def centre_and_scale(stats, width):
    entries = jnp.maximum(stats[0:1], 1.0) * width
    centre = stats[1:2] / entries
    scaling = jnp.sqrt(stats[2:3] / entries + scale_epsilon)
    return entries, centre, scaling


def load_weights(take_own, own_refs, other_refs, scratch_refs, sems):
    @pl.when(pl.program_id(0) == 0)
    def _():
        @pl.when(take_own)
        def _():
            for k, (src, dst) in enumerate(zip(own_refs, scratch_refs)):
                pltpu.make_async_copy(src, dst, sems.at[k]).start()

        @pl.when(jnp.logical_not(take_own))
        def _():
            for k, (src, dst) in enumerate(zip(other_refs, scratch_refs)):
                pltpu.make_async_copy(src, dst, sems.at[k]).start()

        for k, (src, dst) in enumerate(zip(own_refs, scratch_refs)):
            pltpu.make_async_copy(src, dst, sems.at[k]).wait()


def fill_same(var_row, same_ref):
    rows = same_ref.shape[0]
    var_col = column(var_row)
    row = var_row.astype(f32)
    for piece in range(rows // LANES):
        part = row[:, piece * LANES : (piece + 1) * LANES]
        same_ref[:, piece * LANES : (piece + 1) * LANES] = jnp.where(var_col == part, 1.0, 0.0)


def attention_forward(
    hidden, gains, cosine, sine, item_row, var_row, bias_ref, big_ref, same_ref, sums_ref,
    qkv_ref, prob_ref, inv_ref, mixed_ref,
):
    rows, width = hidden.shape
    pairs = width // LANES
    normed = (hidden * inverse_rms(hidden) * gains).astype(bf16)
    qkv = dot(normed, big_ref[:, : 3 * width])
    for p in range(pairs):
        at = p * LANES
        q = turn(qkv[:, at : at + LANES], cosine, sine)
        k = turn(qkv[:, width + at : width + at + LANES], cosine, sine)
        qkv_ref[0, :, at : at + LANES] = (q * HD**-0.5).astype(bf16)
        qkv_ref[0, :, width + at : width + at + LANES] = k.astype(bf16)
        qkv_ref[0, :, 2 * width + at : 2 * width + at + LANES] = qkv[
            :, 2 * width + at : 2 * width + at + LANES
        ].astype(bf16)
    fill_same(var_row, same_ref)
    lane = lane_index(rows)
    second = jnp.where(column(item_row) > 0.0, 1.0, 0.0)
    item_q = jnp.where(lane == 0, second, jnp.where(lane == 1, 1.0 - second, 0.0)).astype(bf16)
    item_k = jnp.where(
        lane == 0, (1.0 - second) * masked_score, jnp.where(lane == 1, second * masked_score, 0.0)
    ).astype(bf16)
    extra = lax.broadcasted_iota(jnp.int32, (16, rows), 0)
    sums_ref[...] = jnp.ones_like(sums_ref)
    for p in range(pairs):
        at = p * LANES
        q_pair = qkv_ref[0, :, at : at + LANES]
        k_pair = jnp.concatenate([qkv_ref[0, :, width + at : width + at + LANES], item_k], axis=1)
        v_turned = qkv_ref[0, :, 2 * width + at : 2 * width + at + LANES].T
        first_rows = lax.broadcasted_iota(jnp.int32, (LANES, rows), 0) < HD
        attended = None
        for half in range(2):
            head = 2 * p + half
            mine = (lane // HD) == half
            q_aug = jnp.concatenate([jnp.where(mine, q_pair, 0.0).astype(bf16), item_q], axis=1)
            scores = dot(k_pair, q_aug, RIGHT_T)
            scores = scores + same_ref[...] * (bias_ref[2 * head] - bias_ref[2 * head + 1])
            peak = jnp.max(scores, axis=0, keepdims=True)
            prob = jnp.exp(scores - peak).astype(bf16)
            prob_ref[0, head] = prob
            own_rows = first_rows if half == 0 else jnp.logical_not(first_rows)
            v_aug = jnp.concatenate(
                [
                    jnp.where(own_rows, v_turned, 0.0).astype(bf16),
                    jnp.where(extra == half, 1.0, 0.0).astype(bf16),
                ],
                axis=0,
            )
            part = dot(v_aug, prob)
            attended = part if attended is None else attended + part
        inv_a = 1.0 / attended[LANES : LANES + 1]
        inv_b = 1.0 / attended[LANES + 1 : LANES + 2]
        sums_ref[2 * p : 2 * p + 1, :] = inv_a
        sums_ref[2 * p + 1 : 2 * p + 2, :] = inv_b
        mixed_t = attended[:LANES] * jnp.where(first_rows, inv_a, inv_b)
        mixed_ref[0, :, at : at + LANES] = mixed_t.T.astype(bf16)
    inv_ref[0] = sums_ref[...].T
    return hidden + dot(mixed_ref[0], big_ref[:, 3 * width : 4 * width])


def sigmoid(x):
    return 0.5 * jnp.tanh(0.5 * x) + 0.5


def feed_forward(middle, gains, big_ref, down_ref):
    width = middle.shape[1]
    hidden = down_ref.shape[0]
    feed = (middle * inverse_rms(middle) * gains).astype(bf16)
    total = middle
    for at in range(0, hidden, CHUNK):
        gate = dot(feed, big_ref[:, 4 * width + at : 4 * width + at + CHUNK])
        up = dot(feed, big_ref[:, 4 * width + hidden + at : 4 * width + hidden + at + CHUNK])
        active = (gate * sigmoid(gate) * up).astype(bf16)
        total = total + dot(active, down_ref[at : at + CHUNK, :])
    return total.astype(bf16)


def feed_both(middle, gains, grad_low, big_ref, down_ref, gate_acc, up_acc, down_acc, gain_acc, with_result):
    width = middle.shape[1]
    hidden = down_ref.shape[0]
    inverse = inverse_rms(middle)
    feed = (middle * inverse * gains).astype(bf16)
    feed_t = feed.T
    total = middle
    feed_grad = jnp.zeros(middle.shape, f32)
    for at in range(0, hidden, CHUNK):
        gate_w = big_ref[:, 4 * width + at : 4 * width + at + CHUNK]
        up_w = big_ref[:, 4 * width + hidden + at : 4 * width + hidden + at + CHUNK]
        down_w = down_ref[at : at + CHUNK, :]
        gate = dot(feed, gate_w)
        up = dot(feed, up_w)
        act_grad = dot(grad_low, down_w, RIGHT_T)
        gated = sigmoid(gate)
        swish = gate * gated
        active = (swish * up).astype(bf16)
        gate_grad = (act_grad * up * (gated + swish * (1.0 - gated))).astype(bf16)
        up_grad = (act_grad * swish).astype(bf16)
        if with_result:
            total = total + dot(active, down_w)
        feed_grad = feed_grad + dot(gate_grad, gate_w, RIGHT_T) + dot(up_grad, up_w, RIGHT_T)
        gate_acc[:, at : at + CHUNK] += dot(feed_t, gate_grad)
        up_acc[:, at : at + CHUNK] += dot(feed_t, up_grad)
        down_acc[at : at + CHUNK, :] += dot(active, grad_low, LEFT_T)
    scaled = feed_grad * gains
    gain_acc[...] += jnp.sum(feed_grad * middle * inverse, axis=0, keepdims=True)
    middle_grad = (
        grad_low.astype(f32)
        + inverse * scaled
        - middle * (inverse * inverse * inverse) * jnp.mean(scaled * middle, axis=1, keepdims=True)
    )
    return total, middle_grad


def attention_backward(
    middle_grad, hidden, gains, cosine, sine, var_row, big_ref, same_ref,
    qkv_ref, prob_ref, inv_ref, mixed_ref, grads_ref, qkv_acc, out_acc, gain_acc, bias_acc,
):
    rows, width = hidden.shape
    pairs = width // LANES
    inverse = inverse_rms(hidden)
    normed = (hidden * inverse * gains).astype(bf16)
    mix_grad = middle_grad.astype(bf16)
    out_acc[...] += dot(mixed_ref[0], mix_grad, LEFT_T)
    att_grad = dot(mix_grad, big_ref[:, 3 * width : 4 * width], RIGHT_T).astype(bf16)
    fill_same(var_row, same_ref)
    lane = lane_index(rows)
    ones_two = jnp.where(lane < 2, 1.0, 0.0).astype(bf16)
    first_rows = lax.broadcasted_iota(jnp.int32, (LANES, rows), 0) < HD
    for p in range(pairs):
        at = p * LANES
        q_pair = qkv_ref[0, :, at : at + LANES]
        k_turned = qkv_ref[0, :, width + at : width + at + LANES].T
        v_aug = jnp.concatenate(
            [qkv_ref[0, :, 2 * width + at : 2 * width + at + LANES], ones_two], axis=1
        )
        grad_pair = att_grad[:, at : at + LANES].astype(f32)
        product = grad_pair * mixed_ref[0, :, at : at + LANES].astype(f32)
        value_grad = key_grad = query_grad_t = None
        for half in range(2):
            head = 2 * p + half
            mine = (lane // HD) == half
            inv = inv_ref[0, :, head : head + 1]
            inner = jnp.sum(jnp.where(mine, product, 0.0), axis=1, keepdims=True) * inv
            grad_low = jnp.where(mine, grad_pair * inv, 0.0).astype(bf16)
            inner_high = inner.astype(bf16).astype(f32)
            tail = jnp.where(
                lane == 0, -inner_high, jnp.where(lane == 1, inner_high - inner, 0.0)
            ).astype(bf16)
            prob = prob_ref[0, head]
            prob_grad = dot(v_aug, jnp.concatenate([grad_low, tail], axis=1), RIGHT_T)
            score_grad = prob.astype(f32) * prob_grad
            bias_acc[head : head + 1, :] += jnp.sum(
                score_grad * same_ref[...], axis=0, keepdims=True
            )
            score_low = score_grad.astype(bf16)
            own_rows = first_rows if half == 0 else jnp.logical_not(first_rows)
            q_mine = jnp.where(mine, q_pair, 0.0).astype(bf16)
            k_mine = jnp.where(own_rows, k_turned, 0.0).astype(bf16)
            part_v = dot(prob, grad_low)
            part_k = dot(score_low, q_mine)
            part_q = dot(k_mine, score_low)
            value_grad = part_v if value_grad is None else value_grad + part_v
            key_grad = part_k if key_grad is None else key_grad + part_k
            query_grad_t = part_q if query_grad_t is None else query_grad_t + part_q
        query_grad = query_grad_t.T * HD**-0.5
        grads_ref[:, at : at + LANES] = turn_back(query_grad, cosine, sine).astype(bf16)
        grads_ref[:, width + at : width + at + LANES] = turn_back(key_grad, cosine, sine).astype(
            bf16
        )
        grads_ref[:, 2 * width + at : 2 * width + at + LANES] = value_grad.astype(bf16)
    qkv_acc[...] += dot(normed, grads_ref[...], LEFT_T)
    normed_grad = dot(grads_ref[...], big_ref[:, : 3 * width], RIGHT_T)
    scaled = normed_grad * gains
    gain_acc[...] += jnp.sum(normed_grad * hidden * inverse, axis=0, keepdims=True)
    return (
        middle_grad
        + inverse * scaled
        - hidden * (inverse * inverse * inverse) * jnp.mean(scaled * hidden, axis=1, keepdims=True)
    )


def pack(sec, out_ref, tiles):
    half = out_ref.shape[1]
    at = 0
    for tile in tiles:
        rows = tile.shape[0]
        slot = sec if at < half else 1 - sec
        start = at % half
        out_ref[slot, start : start + rows, :] = tile.astype(bf16)
        at += rows


def column_tiles(acc_ref, first=0, width=None):
    width = acc_ref.shape[1] if width is None else width
    return [acc_ref[:, first + at : first + at + LANES] for at in range(0, width, LANES)]


def first_layer_body(
    sec_ref, bias_ref, x_ref, sid_ref, item_ref, var_ref, stats_ref, cos_ref, sin_ref, gain_ref,
    own_big, other_big, own_down, other_down,
    result_ref, hidden_ref, qkv_ref, prob_ref, inv_ref, mixed_ref, middle_ref,
    big_ref, down_ref, same_ref, sums_ref, sems,
):
    i = pl.program_id(0)
    m = 3 * sec_ref[0] + i
    load_weights(
        sec_ref[0] == 0, (own_big, own_down), (other_big, other_down), (big_ref, down_ref), sems
    )
    x = x_ref[0].astype(f32)
    width = x.shape[1]
    _, centre, scaling = centre_and_scale(stats_ref[0], width)
    sid_col = column(sid_ref[pl.ds(m, 1), :])
    centre_rows = scale_rows = 0.0
    for piece in range(stats_ref.shape[-1] // LANES):
        hits = series_hits(sid_col, piece)
        part = slice(piece * LANES, (piece + 1) * LANES)
        centre_rows = centre_rows + rows_of(hits, centre[:, part])
        scale_rows = scale_rows + rows_of(hits, scaling[:, part])
    hidden = (x - centre_rows) / scale_rows
    hidden_ref[0] = hidden
    middle = attention_forward(
        hidden, gain_ref[0:1, :], cos_ref[0], sin_ref[0],
        item_ref[pl.ds(m, 1), :], var_ref[pl.ds(m, 1), :], bias_ref, big_ref, same_ref, sums_ref,
        qkv_ref, prob_ref, inv_ref, mixed_ref,
    )
    middle_ref[0] = middle
    result_ref[0] = feed_forward(middle, gain_ref[1:2, :], big_ref, down_ref)


def second_layer_body(
    sec_ref, bias_ref, h_ref, grad_ref, item_ref, var_ref, cos_ref, sin_ref, gain_ref,
    own_big, other_big, own_down, other_down,
    result_ref, qkv_ref, prob_ref, inv_ref, mixed_ref, middle_grad_ref, pack_ref, small_ref,
    big_ref, down_ref, same_ref, sums_ref, gate_acc, up_acc, down_acc, gain_acc, sems,
):
    i = pl.program_id(0)
    m = 3 * sec_ref[0] + i
    load_weights(
        sec_ref[0] == 1, (own_big, own_down), (other_big, other_down), (big_ref, down_ref), sems
    )

    @pl.when(i == 0)
    def _():
        for acc in (gate_acc, up_acc, down_acc, gain_acc):
            acc[...] = jnp.zeros_like(acc)

    middle = attention_forward(
        h_ref[0].astype(f32), gain_ref[0:1, :], cos_ref[0], sin_ref[0],
        item_ref[pl.ds(m, 1), :], var_ref[pl.ds(m, 1), :], bias_ref, big_ref, same_ref, sums_ref,
        qkv_ref, prob_ref, inv_ref, mixed_ref,
    )
    total, middle_grad = feed_both(
        middle, gain_ref[1:2, :], grad_ref[0], big_ref, down_ref,
        gate_acc, up_acc, down_acc, gain_acc, True,
    )
    result_ref[0] = total.astype(bf16)
    middle_grad_ref[0] = middle_grad
    finish_feed(i, sec_ref[0], pack_ref, small_ref, gate_acc, up_acc, down_acc, gain_acc)


def finish_feed(i, sec, pack_ref, small_ref, gate_acc, up_acc, down_acc, gain_acc):
    @pl.when(i == pl.num_programs(0) - 1)
    def _():
        pack(
            sec, pack_ref,
            column_tiles(gate_acc) + column_tiles(up_acc) + column_tiles(down_acc),
        )
        small_ref[...] = jnp.broadcast_to(gain_acc[...], small_ref.shape)


def feed_backward_body(
    sec_ref, middle_ref, grad_ref, gain_ref, own_big, other_big, own_down, other_down,
    middle_grad_ref, pack_ref, small_ref,
    big_ref, down_ref, gate_acc, up_acc, down_acc, gain_acc, sems,
):
    i = pl.program_id(0)
    load_weights(
        sec_ref[0] == 0, (own_big, own_down), (other_big, other_down), (big_ref, down_ref), sems
    )

    @pl.when(i == 0)
    def _():
        for acc in (gate_acc, up_acc, down_acc, gain_acc):
            acc[...] = jnp.zeros_like(acc)

    _, middle_grad = feed_both(
        middle_ref[0], gain_ref[1:2, :], grad_ref[0], big_ref, down_ref,
        gate_acc, up_acc, down_acc, gain_acc, False,
    )
    middle_grad_ref[0] = middle_grad
    finish_feed(i, sec_ref[0], pack_ref, small_ref, gate_acc, up_acc, down_acc, gain_acc)


def attention_backward_body(
    layer, sec_ref, middle_grad_ref, h_ref, qkv_ref, prob_ref, inv_ref, mixed_ref, sid_ref, var_ref,
    cos_ref, sin_ref, gain_ref, own_big, other_big,
    grad_ref, series_ref, pack_ref, small_ref,
    big_ref, same_ref, grads_ref, qkv_acc, out_acc, gain_acc, bias_acc, sems,
):
    i = pl.program_id(0)
    m = 3 * sec_ref[0] + i
    width = h_ref.shape[2]
    attention_part = pl.ds(0, 4 * width)
    load_weights(
        sec_ref[0] == layer, (own_big.at[:, attention_part],), (other_big.at[:, attention_part],),
        (big_ref,), sems,
    )

    @pl.when(i == 0)
    def _():
        for acc in (qkv_acc, out_acc, gain_acc, bias_acc):
            acc[...] = jnp.zeros_like(acc)

    hidden = h_ref[0].astype(f32)
    hidden_grad = attention_backward(
        middle_grad_ref[0], hidden, gain_ref[0:1, :], cos_ref[0], sin_ref[0],
        var_ref[pl.ds(m, 1), :], big_ref, same_ref,
        qkv_ref, prob_ref, inv_ref, mixed_ref, grads_ref, qkv_acc, out_acc, gain_acc, bias_acc,
    )
    grad_ref[0] = hidden_grad.astype(grad_ref.dtype)
    if layer == 0:
        sid_col = column(sid_ref[pl.ds(m, 1), :])
        grad_rows = jnp.sum(hidden_grad, axis=1, keepdims=True)
        cross_rows = jnp.sum(hidden_grad * hidden, axis=1, keepdims=True)
        hidden_rows = jnp.sum(hidden, axis=1, keepdims=True)
        series_ref[0] = jnp.zeros(series_ref.shape[1:], f32)
        for piece in range(series_ref.shape[-1] // LANES):
            hits = series_hits(sid_col, piece)
            part = slice(piece * LANES, (piece + 1) * LANES)
            series_ref[0, 0:1, part] = series_of(hits, grad_rows)
            series_ref[0, 1:2, part] = series_of(hits, cross_rows)
            series_ref[0, 2:3, part] = series_of(hits, hidden_rows)
    else:
        series_ref[0] = jnp.zeros(series_ref.shape[1:], f32)

    @pl.when(i == pl.num_programs(0) - 1)
    def _():
        tiles = []
        for first in range(0, 3 * width, width):
            tiles += column_tiles(qkv_acc, first, width)
        pack(sec_ref[0], pack_ref, tiles + column_tiles(out_acc))
        small_ref[...] = jnp.zeros_like(small_ref)
        small_ref[0:1, :] = gain_acc[...]
        bias_sums = jnp.sum(bias_acc[...], axis=1, keepdims=True)
        small_ref[8:16, :] = jnp.broadcast_to(bias_sums, (8, width))


def final_body(
    sec_ref, x_ref, sid_ref, stats_ref, series_ref, own_first, own_second, other_grad,
    own_out, other_out, out_ref, grads_ref,
):
    i = pl.program_id(0)
    sec = sec_ref[0]
    own = (i // 3) == sec
    grads_ref[0] = jnp.where(own, own_out[0], other_out[0])
    grad = jnp.where(
        own,
        jnp.where(sec == 0, own_first[0], own_second[0].astype(f32)),
        other_grad[0].astype(f32),
    )

    @pl.when(sec == 0)
    def _():
        x = x_ref[0].astype(f32)
        width = x.shape[1]
        entries, centre, scaling = centre_and_scale(stats_ref[0], width)
        sums = series_ref[0]
        cross = sums[1:2] * scaling
        spread_grad = -cross / (2.0 * scaling * scaling * scaling * entries)
        mean_grad = sums[0:1] / scaling + 2.0 * spread_grad * (sums[2:3] * scaling)
        tables = (centre, 1.0 / scaling, 2.0 * spread_grad, mean_grad / entries)
        sid_col = column(sid_ref[pl.ds(i, 1), :])
        looked = [0.0, 0.0, 0.0, 0.0]
        for piece in range(stats_ref.shape[-1] // LANES):
            hits = series_hits(sid_col, piece)
            part = slice(piece * LANES, (piece + 1) * LANES)
            for k in range(4):
                looked[k] = looked[k] + rows_of(hits, tables[k][:, part])
        out_ref[0] = grad * looked[1] + (x - looked[0]) * looked[2] - looked[3]

    @pl.when(sec != 0)
    def _():
        out_ref[0] = grad


def unpack_body(low_ref, high_ref, *out_refs):
    half = low_ref.shape[0]
    at = 0
    for out_ref in out_refs:
        rows, width = out_ref.shape
        for col in range(0, width, LANES):
            source = low_ref if at < half else high_ref
            start = at % half
            out_ref[:, col : col + LANES] = source[start : start + rows, :].astype(f32)
            at += rows


def swapped(x):
    return lax.ppermute(x, "section", [(0, 1), (1, 0)])


def exchange_steps(count):
    bits = []
    step = 1
    while step < count:
        bits.append(step)
        step *= 2
    first = list(bits)
    second = list(bits)
    for k in range(0, len(bits) - 1, 2):
        second[k], second[k + 1] = bits[k + 1], bits[k]
    return first, second


def partner(x, by_first, by_second, count):
    pairs = [(i, i ^ by_first) for i in range(count)]
    pairs += [(count + i, count + (i ^ by_second)) for i in range(count)]
    return lax.ppermute(x, ("section", "dp"), pairs)


def sum_over_dp(kept, sec, index, count):
    first, second = exchange_steps(count)
    current = kept
    for a, b in zip(first, second):
        step = jnp.where(sec == 0, a, b)
        bit = (index // step) % 2
        half = current.shape[0] // 2
        keep = lax.dynamic_slice_in_dim(current, bit * half, half, 0)
        send = lax.dynamic_slice_in_dim(current, (1 - bit) * half, half, 0)
        got = partner(send, a, b, count)
        current = (keep.astype(f32) + got.astype(f32)).astype(bf16)
    for a, b in zip(reversed(first), reversed(second)):
        step = jnp.where(sec == 0, a, b)
        bit = (index // step) % 2
        got = partner(current, a, b, count)
        low = jnp.where(bit == 0, current, got)
        high = jnp.where(bit == 0, got, current)
        current = jnp.concatenate([low, high], axis=0)
    return current


def sum_halves(packed, sec, index, count):
    kept = (packed[0].astype(f32) + swapped(packed[1]).astype(f32)).astype(bf16)
    return sum_over_dp(kept, sec, index, count)


HBM = pl.BlockSpec(memory_space=pl.ANY)
SCALARS = pl.BlockSpec(memory_space=pltpu.SMEM)


def whole_block(shape):
    return pl.BlockSpec(shape, lambda i, *_: (0,) * len(shape))


def by_step(shape):
    return pl.BlockSpec((1,) + shape, lambda i, *_: (i,) + (0,) * len(shape))


def by_batch(shape):
    return pl.BlockSpec((1,) + shape, lambda i, s: (3 * s[0] + i,) + (0,) * len(shape))


def call(body, grid, in_specs, out_specs, out_shapes, scratch, flops, name):
    return pl.pallas_call(
        body,
        grid_spec=pltpu.PrefetchScalarGridSpec(
            num_scalar_prefetch=1,
            grid=(grid,),
            in_specs=in_specs,
            out_specs=out_specs,
            scratch_shapes=scratch,
        ),
        out_shape=out_shapes,
        compiler_params=pltpu.CompilerParams(vmem_limit_bytes=58 * 2**20),
        cost_estimate=pl.CostEstimate(flops=flops, bytes_accessed=2**22, transcendentals=0),
        name=name,
    )


def per_device(
    inputs,
    series_id,
    item_offset,
    variate_offset,
    cotangent,
    attention_gain,
    query_weight,
    key_weight,
    value_weight,
    out_weight,
    variate_bias,
    feed_gain,
    gate_weight,
    up_weight,
    down_weight,
):
    sec = lax.axis_index("section")
    index = lax.axis_index("dp")
    count = lax.axis_size("dp")
    on_first = sec == 0
    sec_arr = sec.astype(jnp.int32).reshape(1)
    micro, rows, width = inputs.shape
    own_micro = micro // 2
    heads = variate_bias.shape[1]
    hidden = down_weight.shape[1]
    series_count = SER_DEV * count
    lanes_series = -(-series_count // LANES) * LANES
    stats_shape = (8, lanes_series)
    all_rows = whole_block((micro, rows))

    own_big = jnp.concatenate(
        [w[0] for w in (query_weight, key_weight, value_weight, out_weight, gate_weight, up_weight)],
        axis=1,
    )
    own_down = down_weight[0]
    own_small = jnp.concatenate(
        [
            attention_gain,
            feed_gain,
            jnp.pad(variate_bias.reshape(1, 2 * heads), ((0, 0), (0, width - 2 * heads))),
        ],
        axis=0,
    ).astype(f32)
    own_small = jnp.pad(own_small, ((0, 5), (0, 0)))

    stats = pl.pallas_call(
        stats_body,
        grid=(micro,),
        in_specs=[by_step((rows, width)), all_rows],
        out_specs=by_step(stats_shape),
        out_shape=jax.ShapeDtypeStruct((micro,) + stats_shape, f32),
        name="series_stats",
    )(inputs, series_id)
    for step in exchange_steps(count)[0]:
        stats = merge_stats(stats, partner(stats, step, step, count), width)

    other_small = swapped(own_small)
    other_big = swapped(own_big)
    other_down = swapped(own_down)
    small = (
        jnp.where(on_first, own_small, other_small),
        jnp.where(on_first, other_small, own_small),
    )
    bias = tuple(s[2, : 2 * heads] for s in small)
    weights = (own_big, other_big, own_down, other_down)

    own_variates = lax.dynamic_slice_in_dim(variate_offset, own_micro * sec, own_micro, 0)
    time = (jnp.arange(rows, dtype=jnp.int32) % BLOCK)[None, :] - own_variates
    lane = jnp.arange(LANES, dtype=jnp.int32)
    frequency = 10000.0 ** (-(lane % (HD // 2)).astype(f32) * (2.0 / HD))
    angle = time.astype(f32)[:, :, None] * frequency
    cosine = jnp.cos(angle)
    sine = jnp.sin(angle) * jnp.where(lane % HD < HD // 2, -1.0, 1.0)

    row_block = by_step((rows, width))
    head_block = by_step((heads, rows, rows))
    qkv_block = by_step((rows, 3 * width))
    lane_block = by_step((rows, LANES))
    weight_specs = [HBM] * 4
    gain_spec = whole_block((8, width))
    big_scratch = pltpu.VMEM(own_big.shape, bf16)
    down_scratch = pltpu.VMEM(own_down.shape, bf16)
    same_scratch = pltpu.VMEM((rows, rows), f32)
    sums_scratch = pltpu.VMEM((LANES, rows), f32)
    feed_accs = [
        pltpu.VMEM((width, hidden), f32),
        pltpu.VMEM((width, hidden), f32),
        pltpu.VMEM((hidden, width), f32),
        pltpu.VMEM((1, width), f32),
    ]
    sems = pltpu.SemaphoreType.DMA((2,))
    layer_flops = 2 * rows * (4 * width * width + 3 * width * hidden) * own_micro

    def shape(*dims, dtype=f32):
        return jax.ShapeDtypeStruct(dims, dtype)

    saved_shapes = [
        shape(own_micro, rows, 3 * width, dtype=bf16),
        shape(own_micro, heads, rows, rows, dtype=bf16),
        shape(own_micro, rows, LANES),
        shape(own_micro, rows, width, dtype=bf16),
    ]
    saved_blocks = [qkv_block, head_block, lane_block, row_block]
    row_shape = shape(own_micro, rows, width)
    low_shape = shape(own_micro, rows, width, dtype=bf16)
    feed_rows = 3 * width * hidden // LANES
    attention_rows = 4 * width * width // LANES
    feed_pack = (2, feed_rows // 2, LANES)
    attention_pack = (2, attention_rows // 2, LANES)

    result_one, standard, qkv_one, prob_one, inv_one, mixed_one, middle_one = call(
        first_layer_body, own_micro,
        [SCALARS, by_batch((rows, width)), all_rows, all_rows, all_rows, by_batch(stats_shape),
         lane_block, lane_block, gain_spec] + weight_specs,
        [row_block, row_block] + saved_blocks + [row_block],
        [low_shape, row_shape] + saved_shapes + [row_shape],
        [big_scratch, down_scratch, same_scratch, sums_scratch, sems],
        2 * layer_flops, "first_layer",
    )(sec_arr, bias[0], inputs, series_id, item_offset, variate_offset, stats, cosine, sine,
      small[0], *weights)

    result_two, qkv_two, prob_two, inv_two, mixed_two, middle_grad_two, feed_two, gain_two = call(
        second_layer_body, own_micro,
        [SCALARS, row_block, by_batch((rows, width)), all_rows, all_rows, lane_block, lane_block,
         gain_spec] + weight_specs,
        [row_block] + saved_blocks + [row_block, whole_block(feed_pack), whole_block((8, width))],
        [low_shape] + saved_shapes
        + [row_shape, shape(*feed_pack, dtype=bf16), shape(8, width)],
        [big_scratch, down_scratch, same_scratch, sums_scratch] + feed_accs + [sems],
        4 * layer_flops, "second_layer",
    )(sec_arr, bias[1], result_one, cotangent, item_offset, variate_offset, cosine, sine,
      small[1], *weights)

    def attention_back(layer, middle_grad, h, saved, dtype):
        return call(
            functools.partial(attention_backward_body, layer), own_micro,
            [row_block, row_block] + saved_blocks
            + [all_rows, all_rows, lane_block, lane_block, gain_spec, HBM, HBM],
            [row_block, by_step(stats_shape), whole_block(attention_pack), whole_block((16, width))],
            [shape(own_micro, rows, width, dtype=dtype), shape(own_micro, *stats_shape),
             shape(*attention_pack, dtype=bf16), shape(16, width)],
            [pltpu.VMEM((width, 4 * width), bf16), same_scratch,
             pltpu.VMEM((rows, 3 * width), bf16), pltpu.VMEM((width, 3 * width), f32),
             pltpu.VMEM((width, width), f32), pltpu.VMEM((1, width), f32),
             pltpu.VMEM((8, rows), f32), sems],
            2 * layer_flops, "attention_back_%d" % layer,
        )(sec_arr, middle_grad, h, *saved, series_id, variate_offset, cosine, sine, small[layer],
          own_big, other_big)

    grad_one, _, attention_two, small_two = attention_back(
        1, middle_grad_two, result_one, (qkv_two, prob_two, inv_two, mixed_two), bf16
    )

    middle_grad_one, feed_one, gain_one = call(
        feed_backward_body, own_micro,
        [row_block, row_block, gain_spec] + weight_specs,
        [row_block, whole_block(feed_pack), whole_block((8, width))],
        [row_shape, shape(*feed_pack, dtype=bf16), shape(8, width)],
        [big_scratch, down_scratch] + feed_accs + [sems],
        2 * layer_flops, "feed_back",
    )(sec_arr, middle_one, grad_one, small[0], *weights)

    standard_grad, series_sums, attention_one, small_one = attention_back(
        0, middle_grad_one, standard, (qkv_one, prob_one, inv_one, mixed_one), f32
    )

    feed_two_sum = sum_halves(feed_two, sec, index, count)
    attention_two_sum = sum_halves(attention_two, sec, index, count)
    feed_one_sum = sum_halves(feed_one, sec, index, count)
    attention_one_sum = sum_halves(attention_one, sec, index, count)

    zeros = jnp.zeros_like(series_sums)
    series_all = jnp.concatenate(
        [jnp.where(on_first, series_sums, zeros), jnp.where(on_first, zeros, series_sums)], axis=0
    )
    small_all = jnp.concatenate(
        [series_all.reshape(-1, LANES)]
        + [
            part.reshape(-1, LANES)
            for part in (small_one, gain_one, small_two, gain_two)
        ],
        axis=0,
    )
    for step in exchange_steps(count)[0]:
        small_all = small_all + partner(small_all, step, step, count)
    small_all = small_all + swapped(small_all)
    series_rows = micro * stats_shape[0] * lanes_series // LANES
    series_all = small_all[:series_rows].reshape((micro,) + stats_shape)
    rest = small_all[series_rows:].reshape(2, 24, width)
    mine = jnp.where(on_first, rest[0], rest[1])
    grad_attention_gain = mine[0:1]
    grad_feed_gain = mine[16:17]
    same_sum = mine[8 : 8 + heads, 0]
    grad_bias = jnp.stack([same_sum, -same_sum], axis=-1)[None]

    own_out = jnp.where(on_first, result_one, result_two)
    other_out = swapped(jnp.where(on_first, result_two, result_one))
    other_grad = swapped(jnp.where(on_first, grad_one, standard_grad.astype(bf16)))

    def own_step(i, s):
        return (jnp.clip(i - own_micro * s[0], 0, own_micro - 1), 0, 0)

    def other_step(i, s):
        return (jnp.clip(i - own_micro * (1 - s[0]), 0, own_micro - 1), 0, 0)

    own_spec = pl.BlockSpec((1, rows, width), own_step)
    other_spec = pl.BlockSpec((1, rows, width), other_step)
    input_grads, section_output = call(
        final_body, micro,
        [row_block, all_rows, by_step(stats_shape), by_step(stats_shape), own_spec, own_spec,
         other_spec, own_spec, other_spec],
        [row_block, row_block],
        [shape(micro, rows, width), shape(micro, rows, width, dtype=bf16)],
        [], 10**8, "final",
    )(sec_arr, inputs, series_id, stats, series_all, standard_grad, grad_one, other_grad,
      own_out, other_out)

    def whole(one, two):
        other = swapped(jnp.where(on_first, two, one))
        own = jnp.where(on_first, one, two)
        return jnp.where(on_first, own, other), jnp.where(on_first, other, own)

    def unpack(halves, *shapes):
        return pl.pallas_call(
            unpack_body,
            out_shape=[jax.ShapeDtypeStruct(s, f32) for s in shapes],
            compiler_params=pltpu.CompilerParams(vmem_limit_bytes=58 * 2**20),
            name="unpack",
        )(*halves)

    grad_gate, grad_up, grad_down = unpack(
        whole(feed_one_sum, feed_two_sum), (width, hidden), (width, hidden), (hidden, width)
    )
    grad_query, grad_key, grad_value, grad_out = unpack(
        whole(attention_one_sum, attention_two_sum), *([(width, width)] * 4)
    )
    return (
        section_output[None],
        input_grads[None],
        grad_attention_gain,
        grad_query[None],
        grad_key[None],
        grad_value[None],
        grad_out[None],
        grad_bias,
        grad_feed_gain,
        grad_gate[None],
        grad_up[None],
        grad_down[None],
    )


def solution(mesh):
    placed = (
        P(None, "dp", None),
        P(None, "dp"),
        P(None, "dp"),
        P(None, "dp"),
        P(None, "dp", None),
        P("section", None),
        P("section", None, None),
        P("section", None, None),
        P("section", None, None),
        P("section", None, None),
        P("section", None, None),
        P("section", None),
        P("section", None, None),
        P("section", None, None),
        P("section", None, None),
    )
    return jax.shard_map(
        per_device,
        mesh=mesh,
        in_specs=placed,
        out_specs=(
            P("section", None, "dp", None),
            P("section", None, "dp", None),
            P("section", None),
            P("section", None, None),
            P("section", None, None),
            P("section", None, None),
            P("section", None, None),
            P("section", None, None),
            P("section", None),
            P("section", None, None),
            P("section", None, None),
            P("section", None, None),
        ),
        check_vma=False,
    )
```

```python
import functools

import jax
import jax.numpy as jnp
import numpy as np
from jax import lax
from jax.experimental import pallas as pl
from jax.experimental.pallas import tpu as pltpu
from jax.sharding import PartitionSpec as P

HD = 64
BLOCK = 512
SER_DEV = 4
LANES = 128
CHUNK = 256

norm_epsilon = 1e-05
scale_epsilon = 1e-05
masked_score = -1e30

f32 = jnp.float32
bf16 = jnp.bfloat16

AS_IS = (((1,), (0,)), ((), ()))
RIGHT_T = (((1,), (1,)), ((), ()))
LEFT_T = (((0,), (0,)), ((), ()))


def dot(left, right, dims=AS_IS):
    return lax.dot_general(left, right, dims, preferred_element_type=f32)


def column(row):
    return jnp.broadcast_to(row.astype(f32), (LANES, row.shape[1])).T


def lane_index(rows):
    return lax.broadcasted_iota(jnp.int32, (rows, LANES), 1)


def swap_halves(x):
    low_half = (lane_index(x.shape[0]) % HD) < HD // 2
    return jnp.where(low_half, pltpu.roll(x, LANES - HD // 2, 1), pltpu.roll(x, HD // 2, 1))


def turn(x, cosine, sine):
    return x * cosine + swap_halves(x) * sine


def turn_back(x, cosine, sine):
    return x * cosine - swap_halves(x) * sine


def inverse_rms(x):
    return lax.rsqrt(jnp.mean(x * x, axis=1, keepdims=True) + norm_epsilon)


def series_hits(sid_col, piece):
    return sid_col == (lane_index(sid_col.shape[0]) + piece * LANES).astype(f32)


def rows_of(hits, per_series):
    return jnp.sum(jnp.where(hits, per_series, 0.0), axis=1, keepdims=True)


def series_of(hits, per_row):
    return jnp.sum(jnp.where(hits, per_row, 0.0), axis=0, keepdims=True)


def stats_body(sec_ref, x_ref, sid_ref, out_ref):
    m = pl.num_programs(0) * sec_ref[0] + pl.program_id(0)
    x = x_ref[0].astype(f32)
    width = x.shape[1]
    sid_col = column(sid_ref[pl.ds(m, 1), :])
    pieces = out_ref.shape[-1] // LANES
    totals = jnp.sum(x, axis=1, keepdims=True)
    centre = jnp.zeros_like(totals)
    out_ref[0] = jnp.zeros(out_ref.shape[1:], f32)
    for piece in range(pieces):
        hits = series_hits(sid_col, piece)
        count = series_of(hits, 1.0)
        total = series_of(hits, totals)
        centre = centre + rows_of(hits, total / (jnp.maximum(count, 1.0) * width))
        out_ref[0, 0:1, piece * LANES : (piece + 1) * LANES] = count
        out_ref[0, 1:2, piece * LANES : (piece + 1) * LANES] = total
    centred = x - centre
    squares = jnp.sum(centred * centred, axis=1, keepdims=True)
    for piece in range(pieces):
        hits = series_hits(sid_col, piece)
        out_ref[0, 2:3, piece * LANES : (piece + 1) * LANES] = series_of(hits, squares)


def merge_stats(here, there, width):
    count_a, total_a, spread_a = here[:, 0], here[:, 1], here[:, 2]
    count_b, total_b, spread_b = there[:, 0], there[:, 1], there[:, 2]
    count = count_a + count_b
    gap = total_a / (jnp.maximum(count_a, 1.0) * width) - total_b / (
        jnp.maximum(count_b, 1.0) * width
    )
    weight = count_a * count_b * width / jnp.maximum(count, 1.0)
    spread = spread_a + spread_b + gap * gap * weight
    rest = jnp.zeros_like(here[:, 3:])
    return jnp.concatenate(
        [jnp.stack([count, total_a + total_b, spread], axis=1), rest], axis=1
    )


def centre_and_scale(stats, width):
    entries = jnp.maximum(stats[0:1], 1.0) * width
    centre = stats[1:2] / entries
    scaling = jnp.sqrt(stats[2:3] / entries + scale_epsilon)
    return entries, centre, scaling


class Weights:
    def __init__(self, take_own, own_refs, other_refs, big_ref, down_ref, sems):
        self.first_step = pl.program_id(0) == 0
        self.big, self.down = big_ref, down_ref
        self.own_refs, self.sems = own_refs, sems
        self.targets = []
        at = 0
        for ref in own_refs[:6]:
            self.targets.append(big_ref.at[:, pl.ds(at, ref.shape[1])])
            at += ref.shape[1]
        if down_ref is not None:
            self.targets.append(down_ref)

        def start(refs):
            for k, (src, dst) in enumerate(zip(refs, self.targets)):
                pltpu.make_async_copy(src, dst, sems.at[k]).start()

        @pl.when(jnp.logical_and(self.first_step, take_own))
        def _():
            start(own_refs)

        @pl.when(jnp.logical_and(self.first_step, jnp.logical_not(take_own)))
        def _():
            start(other_refs)

    def wait(self, *numbers):
        @pl.when(self.first_step)
        def _():
            for k in numbers:
                pltpu.make_async_copy(self.own_refs[k], self.targets[k], self.sems.at[k]).wait()


def fill_same(var_row, same_ref):
    rows = same_ref.shape[0]
    var_col = column(var_row)
    row = var_row.astype(f32)
    for piece in range(rows // LANES):
        part = row[:, piece * LANES : (piece + 1) * LANES]
        same_ref[:, piece * LANES : (piece + 1) * LANES] = jnp.where(var_col == part, 1.0, 0.0)


def attention_forward(
    hidden, gains, cosine, sine, item_row, var_row, bias_ref, weights, same_ref, sums_ref,
    qkv_ref, prob_ref, inv_ref, mixed_ref,
):
    rows, width = hidden.shape
    pairs = width // LANES
    big_ref = weights.big
    normed = (hidden * inverse_rms(hidden) * gains).astype(bf16)
    weights.wait(0, 1, 2)
    qkv = dot(normed, big_ref[:, : 3 * width])
    for p in range(pairs):
        at = p * LANES
        q = turn(qkv[:, at : at + LANES], cosine, sine)
        k = turn(qkv[:, width + at : width + at + LANES], cosine, sine)
        qkv_ref[0, :, at : at + LANES] = (q * HD**-0.5).astype(bf16)
        qkv_ref[0, :, width + at : width + at + LANES] = k.astype(bf16)
        qkv_ref[0, :, 2 * width + at : 2 * width + at + LANES] = qkv[
            :, 2 * width + at : 2 * width + at + LANES
        ].astype(bf16)
    fill_same(var_row, same_ref)
    lane = lane_index(rows)
    second = jnp.where(column(item_row) > 0.0, 1.0, 0.0)
    item_q = jnp.where(lane == 0, second, jnp.where(lane == 1, 1.0 - second, 0.0)).astype(bf16)
    item_k = jnp.where(
        lane == 0, (1.0 - second) * masked_score, jnp.where(lane == 1, second * masked_score, 0.0)
    ).astype(bf16)
    extra = lax.broadcasted_iota(jnp.int32, (16, rows), 0)
    sums_ref[...] = jnp.ones_like(sums_ref)
    for p in range(pairs):
        at = p * LANES
        q_pair = qkv_ref[0, :, at : at + LANES]
        k_pair = jnp.concatenate([qkv_ref[0, :, width + at : width + at + LANES], item_k], axis=1)
        v_turned = qkv_ref[0, :, 2 * width + at : 2 * width + at + LANES].T
        first_rows = lax.broadcasted_iota(jnp.int32, (LANES, rows), 0) < HD
        attended = None
        for half in range(2):
            head = 2 * p + half
            mine = (lane // HD) == half
            q_aug = jnp.concatenate([jnp.where(mine, q_pair, 0.0).astype(bf16), item_q], axis=1)
            scores = dot(k_pair, q_aug, RIGHT_T)
            scores = scores + same_ref[...] * (bias_ref[2 * head] - bias_ref[2 * head + 1])
            peak = jnp.max(scores, axis=0, keepdims=True)
            prob = jnp.exp(scores - peak).astype(bf16)
            prob_ref[0, head] = prob
            own_rows = first_rows if half == 0 else jnp.logical_not(first_rows)
            v_aug = jnp.concatenate(
                [
                    jnp.where(own_rows, v_turned, 0.0).astype(bf16),
                    jnp.where(extra == half, 1.0, 0.0).astype(bf16),
                ],
                axis=0,
            )
            part = dot(v_aug, prob)
            attended = part if attended is None else attended + part
        inv_a = 1.0 / attended[LANES : LANES + 1]
        inv_b = 1.0 / attended[LANES + 1 : LANES + 2]
        sums_ref[2 * p : 2 * p + 1, :] = inv_a
        sums_ref[2 * p + 1 : 2 * p + 2, :] = inv_b
        mixed_t = attended[:LANES] * jnp.where(first_rows, inv_a, inv_b)
        mixed_ref[0, :, at : at + LANES] = mixed_t.T.astype(bf16)
    inv_ref[0] = sums_ref[...].T
    weights.wait(3)
    return hidden + dot(mixed_ref[0], big_ref[:, 3 * width : 4 * width])


def sigmoid(x):
    return 0.5 * jnp.tanh(0.5 * x) + 0.5


def feed_forward(middle, gains, weights):
    big_ref, down_ref = weights.big, weights.down
    weights.wait(4, 5, 6)
    width = middle.shape[1]
    hidden = down_ref.shape[0]
    feed = (middle * inverse_rms(middle) * gains).astype(bf16)
    total = middle
    for at in range(0, hidden, CHUNK):
        gate = dot(feed, big_ref[:, 4 * width + at : 4 * width + at + CHUNK])
        up = dot(feed, big_ref[:, 4 * width + hidden + at : 4 * width + hidden + at + CHUNK])
        active = (gate * sigmoid(gate) * up).astype(bf16)
        total = total + dot(active, down_ref[at : at + CHUNK, :])
    return total.astype(bf16)


def feed_both(
    middle, gains, grad_low, weights, gate_acc, up_acc, down_acc, gain_acc, with_result
):
    big_ref, down_ref = weights.big, weights.down
    weights.wait(4, 5, 6)
    width = middle.shape[1]
    hidden = down_ref.shape[0]
    inverse = inverse_rms(middle)
    feed = (middle * inverse * gains).astype(bf16)
    feed_t = feed.T
    total = middle
    feed_grad = jnp.zeros(middle.shape, f32)
    for at in range(0, hidden, CHUNK):
        gate_w = big_ref[:, 4 * width + at : 4 * width + at + CHUNK]
        up_w = big_ref[:, 4 * width + hidden + at : 4 * width + hidden + at + CHUNK]
        down_w = down_ref[at : at + CHUNK, :]
        gate = dot(feed, gate_w)
        up = dot(feed, up_w)
        act_grad = dot(grad_low, down_w, RIGHT_T)
        gated = sigmoid(gate)
        swish = gate * gated
        active = (swish * up).astype(bf16)
        gate_grad = (act_grad * up * (gated + swish * (1.0 - gated))).astype(bf16)
        up_grad = (act_grad * swish).astype(bf16)
        if with_result:
            total = total + dot(active, down_w)
        feed_grad = feed_grad + dot(gate_grad, gate_w, RIGHT_T) + dot(up_grad, up_w, RIGHT_T)
        gate_acc[:, at : at + CHUNK] += dot(feed_t, gate_grad)
        up_acc[:, at : at + CHUNK] += dot(feed_t, up_grad)
        down_acc[at : at + CHUNK, :] += dot(active, grad_low, LEFT_T)
    scaled = feed_grad * gains
    gain_acc[...] += jnp.sum(feed_grad * middle * inverse, axis=0, keepdims=True)
    middle_grad = (
        grad_low.astype(f32)
        + inverse * scaled
        - middle * (inverse * inverse * inverse) * jnp.mean(scaled * middle, axis=1, keepdims=True)
    )
    return total, middle_grad


def attention_backward(
    middle_grad, hidden, gains, cosine, sine, var_row, weights, same_ref,
    qkv_ref, prob_ref, inv_ref, mixed_ref, grads_ref, qkv_acc, out_acc, gain_acc, bias_acc,
):
    rows, width = hidden.shape
    big_ref = weights.big
    pairs = width // LANES
    inverse = inverse_rms(hidden)
    normed = (hidden * inverse * gains).astype(bf16)
    mix_grad = middle_grad.astype(bf16)
    out_acc[...] += dot(mixed_ref[0], mix_grad, LEFT_T)
    weights.wait(3)
    att_grad = dot(mix_grad, big_ref[:, 3 * width : 4 * width], RIGHT_T).astype(bf16)
    fill_same(var_row, same_ref)
    lane = lane_index(rows)
    ones_two = jnp.where(lane < 2, 1.0, 0.0).astype(bf16)
    first_rows = lax.broadcasted_iota(jnp.int32, (LANES, rows), 0) < HD
    for p in range(pairs):
        at = p * LANES
        q_pair = qkv_ref[0, :, at : at + LANES]
        k_turned = qkv_ref[0, :, width + at : width + at + LANES].T
        v_aug = jnp.concatenate(
            [qkv_ref[0, :, 2 * width + at : 2 * width + at + LANES], ones_two], axis=1
        )
        grad_pair = att_grad[:, at : at + LANES].astype(f32)
        product = grad_pair * mixed_ref[0, :, at : at + LANES].astype(f32)
        value_grad = key_grad = query_grad_t = None
        for half in range(2):
            head = 2 * p + half
            mine = (lane // HD) == half
            inv = inv_ref[0, :, head : head + 1]
            inner = jnp.sum(jnp.where(mine, product, 0.0), axis=1, keepdims=True) * inv
            grad_low = jnp.where(mine, grad_pair * inv, 0.0).astype(bf16)
            inner_high = inner.astype(bf16).astype(f32)
            tail = jnp.where(
                lane == 0, -inner_high, jnp.where(lane == 1, inner_high - inner, 0.0)
            ).astype(bf16)
            prob = prob_ref[0, head]
            prob_grad = dot(v_aug, jnp.concatenate([grad_low, tail], axis=1), RIGHT_T)
            score_grad = prob.astype(f32) * prob_grad
            bias_acc[head : head + 1, :] += jnp.sum(
                score_grad * same_ref[...], axis=0, keepdims=True
            )
            score_low = score_grad.astype(bf16)
            own_rows = first_rows if half == 0 else jnp.logical_not(first_rows)
            q_mine = jnp.where(mine, q_pair, 0.0).astype(bf16)
            k_mine = jnp.where(own_rows, k_turned, 0.0).astype(bf16)
            part_v = dot(prob, grad_low)
            part_k = dot(score_low, q_mine)
            part_q = dot(k_mine, score_low)
            value_grad = part_v if value_grad is None else value_grad + part_v
            key_grad = part_k if key_grad is None else key_grad + part_k
            query_grad_t = part_q if query_grad_t is None else query_grad_t + part_q
        query_grad = query_grad_t.T * HD**-0.5
        grads_ref[:, at : at + LANES] = turn_back(query_grad, cosine, sine).astype(bf16)
        grads_ref[:, width + at : width + at + LANES] = turn_back(key_grad, cosine, sine).astype(
            bf16
        )
        grads_ref[:, 2 * width + at : 2 * width + at + LANES] = value_grad.astype(bf16)
    qkv_acc[...] += dot(normed, grads_ref[...], LEFT_T)
    weights.wait(0, 1, 2)
    normed_grad = dot(grads_ref[...], big_ref[:, : 3 * width], RIGHT_T)
    scaled = normed_grad * gains
    gain_acc[...] += jnp.sum(normed_grad * hidden * inverse, axis=0, keepdims=True)
    return (
        middle_grad
        + inverse * scaled
        - hidden * (inverse * inverse * inverse) * jnp.mean(scaled * hidden, axis=1, keepdims=True)
    )


def pack(out_ref, at, tiles):
    for tile in tiles:
        out_ref[at : at + tile.shape[0], :] = tile.astype(bf16)
        at += tile.shape[0]


def column_tiles(acc_ref):
    return [acc_ref[:, at : at + LANES] for at in range(0, acc_ref.shape[1], LANES)]


def first_layer_body(
    sec_ref, bias_ref, x_ref, sid_ref, item_ref, var_ref, stats_ref, table_ref, gain_ref, *refs
):
    own_refs, other_refs, refs = refs[:7], refs[7:14], refs[14:]
    (
        result_ref, hidden_ref, cos_ref, sin_ref, qkv_ref, prob_ref, inv_ref, mixed_ref, middle_ref,
        big_ref, down_ref, same_ref, sums_ref, sems,
    ) = refs
    i = pl.program_id(0)
    m = pl.num_programs(0) * sec_ref[0] + i
    weights = Weights(sec_ref[0] == 0, own_refs, other_refs, big_ref, down_ref, sems)
    x = x_ref[0].astype(f32)
    rows, width = x.shape
    var_row = var_ref[pl.ds(m, 1), :]

    position = lax.broadcasted_iota(jnp.int32, (rows, LANES), 0)
    time = position.astype(f32) - column(var_row)
    cosine = sine = jnp.zeros((rows, LANES), f32)
    for at in range(0, rows, LANES):
        hot = jnp.where(time == (lane_index(rows) + at).astype(f32), 1.0, 0.0).astype(bf16)
        found = dot(hot, table_ref[at : at + LANES, :])
        cosine = cosine + found[:, :LANES] + found[:, LANES : 2 * LANES]
        sine = sine + found[:, 2 * LANES : 3 * LANES] + found[:, 3 * LANES :]
    cos_ref[0] = cosine
    sin_ref[0] = sine

    _, centre, scaling = centre_and_scale(stats_ref[0], width)
    sid_col = column(sid_ref[pl.ds(m, 1), :])
    centre_rows = scale_rows = 0.0
    for piece in range(stats_ref.shape[-1] // LANES):
        hits = series_hits(sid_col, piece)
        part = slice(piece * LANES, (piece + 1) * LANES)
        centre_rows = centre_rows + rows_of(hits, centre[:, part])
        scale_rows = scale_rows + rows_of(hits, scaling[:, part])
    hidden = (x - centre_rows) / scale_rows
    hidden_ref[0] = hidden
    middle = attention_forward(
        hidden, gain_ref[0:1, :], cosine, sine, item_ref[pl.ds(m, 1), :], var_row, bias_ref,
        weights, same_ref, sums_ref, qkv_ref, prob_ref, inv_ref, mixed_ref,
    )
    middle_ref[0] = middle
    result_ref[0] = feed_forward(middle, gain_ref[1:2, :], weights)


def clear_first(i, *accs):
    @pl.when(i == 0)
    def _():
        for acc in accs:
            acc[...] = jnp.zeros_like(acc)


def write_gain(small_ref, gain_acc):
    small_ref[...] = jnp.zeros_like(small_ref)
    for k in range(gain_acc.shape[1] // LANES):
        small_ref[k : k + 1, :] = gain_acc[:, k * LANES : (k + 1) * LANES]


def finish_feed(i, pack_ref, small_ref, gate_acc, up_acc, down_acc, gain_acc):
    @pl.when(i == pl.num_programs(0) - 1)
    def _():
        tiles = column_tiles(gate_acc) + column_tiles(up_acc) + column_tiles(down_acc)
        half = pack_ref.shape[1]
        at = 0
        for tile in tiles:
            pack(pack_ref.at[at // half], at % half, [tile])
            at += tile.shape[0]
        write_gain(small_ref, gain_acc)


def second_layer_body(
    sec_ref, bias_ref, h_ref, grad_ref, item_ref, var_ref, cos_ref, sin_ref, gain_ref, *refs
):
    own_refs, other_refs, refs = refs[:7], refs[7:14], refs[14:]
    (
        result_ref, qkv_ref, prob_ref, inv_ref, mixed_ref, middle_grad_ref, pack_ref, small_ref,
        big_ref, down_ref, same_ref, sums_ref, gate_acc, up_acc, down_acc, gain_acc, sems,
    ) = refs
    i = pl.program_id(0)
    m = pl.num_programs(0) * sec_ref[0] + i
    weights = Weights(sec_ref[0] == 1, own_refs, other_refs, big_ref, down_ref, sems)
    clear_first(i, gate_acc, up_acc, down_acc, gain_acc)
    middle = attention_forward(
        h_ref[0].astype(f32), gain_ref[0:1, :], cos_ref[0], sin_ref[0],
        item_ref[pl.ds(m, 1), :], var_ref[pl.ds(m, 1), :], bias_ref, weights, same_ref, sums_ref,
        qkv_ref, prob_ref, inv_ref, mixed_ref,
    )
    total, middle_grad = feed_both(
        middle, gain_ref[1:2, :], grad_ref[0], weights,
        gate_acc, up_acc, down_acc, gain_acc, True,
    )
    result_ref[0] = total.astype(bf16)
    middle_grad_ref[0] = middle_grad
    finish_feed(i, pack_ref, small_ref, gate_acc, up_acc, down_acc, gain_acc)


def feed_backward_body(sec_ref, middle_ref, grad_ref, gain_ref, *refs):
    own_refs, other_refs, refs = refs[:7], refs[7:14], refs[14:]
    (
        middle_grad_ref, pack_ref, small_ref,
        big_ref, down_ref, gate_acc, up_acc, down_acc, gain_acc, sems,
    ) = refs
    i = pl.program_id(0)
    weights = Weights(sec_ref[0] == 0, own_refs, other_refs, big_ref, down_ref, sems)
    weights.wait(0, 1, 2, 3)
    clear_first(i, gate_acc, up_acc, down_acc, gain_acc)
    _, middle_grad = feed_both(
        middle_ref[0], gain_ref[1:2, :], grad_ref[0], weights,
        gate_acc, up_acc, down_acc, gain_acc, False,
    )
    middle_grad_ref[0] = middle_grad
    finish_feed(i, pack_ref, small_ref, gate_acc, up_acc, down_acc, gain_acc)


def attention_backward_body(
    layer, sec_ref, middle_grad_ref, h_ref, qkv_ref, prob_ref, inv_ref, mixed_ref, sid_ref, var_ref,
    cos_ref, sin_ref, gain_ref, *refs
):
    own_refs, other_refs, refs = refs[:4], refs[4:8], refs[8:]
    grad_ref, refs = refs[0], refs[1:]
    if layer == 0:
        series_ref, refs = refs[0], refs[1:]
    (
        pack_ref, small_ref,
        big_ref, same_ref, grads_ref, qkv_acc, out_acc, gain_acc, bias_acc, sems,
    ) = refs
    i = pl.program_id(0)
    m = pl.num_programs(0) * sec_ref[0] + i
    weights = Weights(sec_ref[0] == layer, own_refs, other_refs, big_ref, None, sems)
    clear_first(i, qkv_acc, out_acc, gain_acc, bias_acc)
    hidden = h_ref[0].astype(f32)
    hidden_grad = attention_backward(
        middle_grad_ref[0], hidden, gain_ref[0:1, :], cos_ref[0], sin_ref[0],
        var_ref[pl.ds(m, 1), :], weights, same_ref,
        qkv_ref, prob_ref, inv_ref, mixed_ref, grads_ref, qkv_acc, out_acc, gain_acc, bias_acc,
    )
    grad_ref[0] = hidden_grad.astype(grad_ref.dtype)
    if layer == 0:
        sid_col = column(sid_ref[pl.ds(m, 1), :])
        grad_rows = jnp.sum(hidden_grad, axis=1, keepdims=True)
        cross_rows = jnp.sum(hidden_grad * hidden, axis=1, keepdims=True)
        hidden_rows = jnp.sum(hidden, axis=1, keepdims=True)
        series_ref[0] = jnp.zeros(series_ref.shape[1:], f32)
        for piece in range(series_ref.shape[-1] // LANES):
            hits = series_hits(sid_col, piece)
            part = slice(piece * LANES, (piece + 1) * LANES)
            series_ref[0, 0:1, part] = series_of(hits, grad_rows)
            series_ref[0, 1:2, part] = series_of(hits, cross_rows)
            series_ref[0, 2:3, part] = series_of(hits, hidden_rows)

    @pl.when(i == pl.num_programs(0) - 1)
    def _():
        pack(pack_ref, 0, column_tiles(qkv_acc) + column_tiles(out_acc))
        write_gain(small_ref, gain_acc)
        bias_sums = jnp.sum(bias_acc[...], axis=1, keepdims=True)
        small_ref[8:16, :] = jnp.broadcast_to(bias_sums, (8, LANES))


def final_body(
    sec_ref, x_ref, sid_ref, stats_ref, series_ref, own_first, own_second, other_grad,
    own_out, other_out, out_ref, grads_ref,
):
    i = pl.program_id(0)
    sec = sec_ref[0]
    own = (i // (pl.num_programs(0) // 2)) == sec
    grads_ref[0] = jnp.where(own, own_out[0], other_out[0])
    grad = jnp.where(
        own,
        jnp.where(sec == 0, own_first[0], own_second[0].astype(f32)),
        other_grad[0].astype(f32),
    )

    @pl.when(sec == 0)
    def _():
        x = x_ref[0].astype(f32)
        width = x.shape[1]
        entries, centre, scaling = centre_and_scale(stats_ref[0], width)
        sums = series_ref[0]
        cross = sums[1:2] * scaling
        spread_grad = -cross / (2.0 * scaling * scaling * scaling * entries)
        mean_grad = sums[0:1] / scaling + 2.0 * spread_grad * (sums[2:3] * scaling)
        tables = (centre, 1.0 / scaling, 2.0 * spread_grad, mean_grad / entries)
        sid_col = column(sid_ref[pl.ds(i, 1), :])
        looked = [0.0, 0.0, 0.0, 0.0]
        for piece in range(stats_ref.shape[-1] // LANES):
            hits = series_hits(sid_col, piece)
            part = slice(piece * LANES, (piece + 1) * LANES)
            for k in range(4):
                looked[k] = looked[k] + rows_of(hits, tables[k][:, part])
        out_ref[0] = grad * looked[1] + (x - looked[0]) * looked[2] - looked[3]

    @pl.when(sec != 0)
    def _():
        out_ref[0] = grad


def spread(part_refs, out_refs):
    size = part_refs[0].shape[0]
    at = 0
    for out_ref in out_refs:
        rows, width = out_ref.shape
        for col in range(0, width, LANES):
            source = part_refs[at // size]
            start = at % size
            out_ref[:, col : col + LANES] = source[start : start + rows, :].astype(f32)
            at += rows


def unpack_feed_body(first_ref, second_ref, *out_refs):
    spread((first_ref, second_ref), out_refs)


def unpack_attention_body(sec_ref, part_ref, small_ref, *out_refs):
    spread((part_ref,), out_refs[:4])
    attention_gain_ref, feed_gain_ref, bias_ref = out_refs[4:]
    base = 24 * sec_ref[0]
    for k in range(attention_gain_ref.shape[1] // LANES):
        cols = slice(k * LANES, (k + 1) * LANES)
        attention_gain_ref[:, cols] = small_ref[pl.ds(base + k, 1), :]
        feed_gain_ref[:, cols] = small_ref[pl.ds(base + 16 + k, 1), :]
    same = small_ref[pl.ds(base + 8, 8), 0:1][: bias_ref.shape[0]]
    bias_ref[:, 0:1] = same
    bias_ref[:, 1:2] = -same


def swapped(x):
    return lax.ppermute(x, "section", [(0, 1), (1, 0)])


def to_section(x, section):
    return lax.ppermute(x, "section", [(1 - section, section)])


def exchange_steps(count):
    bits = []
    step = 1
    while step < count:
        bits.append(step)
        step *= 2
    other = list(bits)
    for k in range(0, len(bits) - 1, 2):
        other[k], other[k + 1] = bits[k + 1], bits[k]
    return bits, other


def partner(x, by_first, by_second, count):
    pairs = [(i, i ^ by_first) for i in range(count)]
    pairs += [(count + i, count + (i ^ by_second)) for i in range(count)]
    return lax.ppermute(x, ("section", "dp"), pairs)


def halve(current, steps, sec, index, count):
    step = jnp.where(sec == 0, *steps)
    bit = (index // step) % 2
    half = current.shape[0] // 2
    keep = lax.dynamic_slice_in_dim(current, bit * half, half, 0)
    send = lax.dynamic_slice_in_dim(current, (1 - bit) * half, half, 0)
    got = partner(send, *steps, count)
    return (keep.astype(f32) + got.astype(f32)).astype(bf16)


def double(current, steps, sec, index, count):
    step = jnp.where(sec == 0, *steps)
    bit = (index // step) % 2
    got = partner(current, *steps, count)
    low = jnp.where(bit == 0, current, got)
    high = jnp.where(bit == 0, got, current)
    return jnp.concatenate([low, high], axis=0)


HBM = pl.BlockSpec(memory_space=pl.ANY)
SCALARS = pl.BlockSpec(memory_space=pltpu.SMEM)


def whole_block(shape):
    return pl.BlockSpec(shape, lambda i, *_: (0,) * len(shape))


def by_step(shape):
    return pl.BlockSpec((1,) + shape, lambda i, *_: (i,) + (0,) * len(shape))


def by_batch(shape, own):
    return pl.BlockSpec((1,) + shape, lambda i, s: (own * s[0] + i,) + (0,) * len(shape))


def call(body, grid, in_specs, out_specs, out_shapes, scratch, flops, name):
    return pl.pallas_call(
        body,
        grid_spec=pltpu.PrefetchScalarGridSpec(
            num_scalar_prefetch=1,
            grid=(grid,),
            in_specs=in_specs,
            out_specs=out_specs,
            scratch_shapes=scratch,
        ),
        out_shape=out_shapes,
        compiler_params=pltpu.CompilerParams(vmem_limit_bytes=56 * 2**20),
        cost_estimate=pl.CostEstimate(flops=flops, bytes_accessed=2**22, transcendentals=0),
        name=name,
    )


def shape(*dims, dtype=f32):
    return jax.ShapeDtypeStruct(dims, dtype)


class Sizes:
    def __init__(self, inputs, heads, hidden, count):
        self.micro, self.rows, self.width = inputs.shape
        self.own = self.micro // 2
        self.heads, self.hidden, self.count = heads, hidden, count
        rows, width, own = self.rows, self.width, self.own
        self.stats = (8, -(-SER_DEV * count // LANES) * LANES)
        self.all_rows = whole_block((self.micro, rows))
        self.row = by_step((rows, width))
        self.row_batch = by_batch((rows, width), own)
        self.lane = by_step((rows, LANES))
        self.gain = whole_block((8, width))
        self.saved = [
            by_step((rows, 3 * width)), by_step((heads, rows, rows)), self.lane, self.row
        ]
        self.row_shape = shape(own, rows, width)
        self.low_shape = shape(own, rows, width, dtype=bf16)
        self.lane_shape = shape(own, rows, LANES)
        self.saved_shapes = [
            shape(own, rows, 3 * width, dtype=bf16), shape(own, heads, rows, rows, dtype=bf16),
            self.lane_shape, self.low_shape,
        ]
        self.feed_pack = (2, 3 * width * hidden // LANES // 2, LANES)
        self.attention_pack = (4 * width * width // LANES, LANES)
        self.big = pltpu.VMEM((width, 4 * width + 2 * hidden), bf16)
        self.down = pltpu.VMEM((hidden, width), bf16)
        self.same = pltpu.VMEM((rows, rows), f32)
        self.sums = pltpu.VMEM((LANES, rows), f32)
        self.feed_accs = [
            pltpu.VMEM((width, hidden), f32), pltpu.VMEM((width, hidden), f32),
            pltpu.VMEM((hidden, width), f32), pltpu.VMEM((1, width), f32),
        ]
        self.flops = 2 * rows * (4 * width * width + 3 * width * hidden) * own


def rotary_table(rows):
    lane = np.arange(LANES)
    frequency = np.float32(10000.0) ** (
        -(lane % (HD // 2)).astype(np.float32) * np.float32(2.0 / HD)
    )
    angle = np.arange(rows, dtype=np.float32)[:, None] * frequency[None, :].astype(np.float32)
    cosine = np.cos(angle.astype(np.float64))
    sine = np.sin(angle.astype(np.float64)) * np.where(lane % HD < HD // 2, -1.0, 1.0)
    parts = []
    for values in (cosine, sine):
        high = values.astype(jnp.bfloat16)
        parts += [high, (values - high.astype(np.float64)).astype(jnp.bfloat16)]
    return np.concatenate(parts, axis=1)


def series_stats(z, sec, inputs, series_id):
    return call(
        stats_body, z.own, [z.row_batch, z.all_rows], by_step(z.stats), shape(z.own, *z.stats),
        [], 10**7, "series_stats",
    )(sec, inputs, series_id)


def first_layer(z, sec, bias, inputs, series_id, item, variate, stats, gains, own, other):
    table = rotary_table(z.rows)
    return call(
        first_layer_body, z.own,
        [SCALARS, z.row_batch, z.all_rows, z.all_rows, z.all_rows, by_step(z.stats),
         whole_block(table.shape), z.gain] + [HBM] * 14,
        [z.row, z.row, z.lane, z.lane] + z.saved + [z.row],
        [z.low_shape, z.row_shape, z.lane_shape, z.lane_shape] + z.saved_shapes + [z.row_shape],
        [z.big, z.down, z.same, z.sums, pltpu.SemaphoreType.DMA((7,))],
        2 * z.flops, "first_layer",
    )(sec, bias, inputs, series_id, item, variate, stats, jnp.asarray(table), gains, *own, *other)


def second_layer(z, sec, bias, h, cotangent, item, variate, cosine, sine, gains, own, other):
    return call(
        second_layer_body, z.own,
        [SCALARS, z.row, z.row_batch, z.all_rows, z.all_rows, z.lane, z.lane, z.gain] + [HBM] * 14,
        [z.row] + z.saved + [z.row, whole_block(z.feed_pack), whole_block((8, LANES))],
        [z.low_shape] + z.saved_shapes
        + [z.row_shape, shape(*z.feed_pack, dtype=bf16), shape(8, LANES)],
        [z.big, z.down, z.same, z.sums] + z.feed_accs + [pltpu.SemaphoreType.DMA((7,))],
        4 * z.flops, "second_layer",
    )(sec, bias, h, cotangent, item, variate, cosine, sine, gains, *own, *other)


def feed_back(z, sec, middle, grad, gains, own, other):
    return call(
        feed_backward_body, z.own,
        [z.row, z.row, z.gain] + [HBM] * 14,
        [z.row, whole_block(z.feed_pack), whole_block((8, LANES))],
        [z.row_shape, shape(*z.feed_pack, dtype=bf16), shape(8, LANES)],
        [z.big, z.down] + z.feed_accs + [pltpu.SemaphoreType.DMA((7,))],
        2 * z.flops, "feed_back",
    )(sec, middle, grad, gains, *own, *other)


def attention_back(z, layer, sec, middle_grad, h, saved, series_id, variate, cosine, sine, gains,
                   own, other):
    series = layer == 0
    width = z.width
    return call(
        functools.partial(attention_backward_body, layer), z.own,
        [z.row, z.row] + z.saved + [z.all_rows, z.all_rows, z.lane, z.lane, z.gain] + [HBM] * 8,
        [z.row] + [by_step(z.stats)] * series
        + [whole_block(z.attention_pack), whole_block((16, LANES))],
        [z.row_shape if series else z.low_shape] + [shape(z.own, *z.stats)] * series
        + [shape(*z.attention_pack, dtype=bf16), shape(16, LANES)],
        [pltpu.VMEM((width, 4 * width), bf16), z.same,
         pltpu.VMEM((z.rows, 3 * width), bf16), pltpu.VMEM((width, 3 * width), f32),
         pltpu.VMEM((width, width), f32), pltpu.VMEM((1, width), f32),
         pltpu.VMEM((8, z.rows), f32), pltpu.SemaphoreType.DMA((4,))],
        2 * z.flops, "attention_back_%d" % layer,
    )(sec, middle_grad, h, *saved, series_id, variate, cosine, sine, gains, *own[:4], *other[:4])


def final(z, sec, inputs, series_id, stats, series, own_first, own_second, other_grad,
          own_out, other_out):
    own_count = z.own

    def own_step(i, s):
        return (jnp.clip(i - own_count * s[0], 0, own_count - 1), 0, 0)

    def other_step(i, s):
        return (jnp.clip(i - own_count * (1 - s[0]), 0, own_count - 1), 0, 0)

    own_spec = pl.BlockSpec((1, z.rows, z.width), own_step)
    other_spec = pl.BlockSpec((1, z.rows, z.width), other_step)
    return call(
        final_body, z.micro,
        [z.row, z.all_rows, by_step(z.stats), by_step(z.stats), own_spec, own_spec,
         other_spec, own_spec, other_spec],
        [z.row, z.row],
        [shape(z.micro, z.rows, z.width), shape(z.micro, z.rows, z.width, dtype=bf16)],
        [], 10**8, "final",
    )(sec, inputs, series_id, stats, series, own_first, own_second, other_grad, own_out, other_out)


def per_device(
    inputs,
    series_id,
    item_offset,
    variate_offset,
    cotangent,
    attention_gain,
    query_weight,
    key_weight,
    value_weight,
    out_weight,
    variate_bias,
    feed_gain,
    gate_weight,
    up_weight,
    down_weight,
):
    section = lax.axis_index("section")
    index = lax.axis_index("dp")
    count = lax.axis_size("dp")
    on_first = section == 0
    sec = section.astype(jnp.int32).reshape(1)
    heads = variate_bias.shape[1]
    z = Sizes(inputs, heads, down_weight.shape[1], count)
    width = z.width

    stats = series_stats(z, sec, inputs, series_id)
    for step in exchange_steps(count)[0]:
        stats = merge_stats(stats, partner(stats, step, step, count), width)

    own_small = jnp.concatenate(
        [
            attention_gain,
            feed_gain,
            jnp.pad(variate_bias.reshape(1, 2 * heads), ((0, 0), (0, width - 2 * heads))),
        ],
        axis=0,
    ).astype(f32)
    own_small = jnp.pad(own_small, ((0, 5), (0, 0)))
    other_small = swapped(own_small)
    own = tuple(
        w[0]
        for w in (
            query_weight, key_weight, value_weight, out_weight, gate_weight, up_weight, down_weight
        )
    )
    other = tuple(swapped(w) for w in own)
    gains = (
        jnp.where(on_first, own_small, other_small),
        jnp.where(on_first, other_small, own_small),
    )
    bias = tuple(g[2, : 2 * heads] for g in gains)

    result_one, standard, cosine, sine, *saved_one, middle_one = first_layer(
        z, sec, bias[0], inputs, series_id, item_offset, variate_offset, stats, gains[0], own, other
    )
    result_two, *saved_two, middle_grad_two, feed_two, gain_two = second_layer(
        z, sec, bias[1], result_one, cotangent, item_offset, variate_offset, cosine, sine,
        gains[1], own, other,
    )
    grad_one, attention_two, small_two = attention_back(
        z, 1, sec, middle_grad_two, result_one, saved_two, series_id, variate_offset, cosine, sine,
        gains[1], own, other,
    )
    middle_grad_one, feed_one, gain_one = feed_back(
        z, sec, middle_one, grad_one, gains[0], own, other
    )
    standard_grad, series_sums, attention_one, small_one = attention_back(
        z, 0, sec, middle_grad_one, standard, saved_one, series_id, variate_offset, cosine, sine,
        gains[0], own, other,
    )

    series_rows = z.own * z.stats[0] * z.stats[1] // LANES
    small = jnp.concatenate(
        [series_sums.reshape(-1, LANES), small_one, gain_one, small_two, gain_two], axis=0
    )
    for step in exchange_steps(count)[0]:
        small = small + partner(small, step, step, count)
    other_sums = swapped(small)
    mine = small[:series_rows].reshape((z.own,) + z.stats)
    theirs = other_sums[:series_rows].reshape((z.own,) + z.stats)
    series_all = jnp.where(
        on_first, jnp.concatenate([mine, theirs]), jnp.concatenate([theirs, mine])
    )
    small = small[series_rows:] + other_sums[series_rows:]
    other_stats = swapped(stats)
    stats_all = jnp.where(
        on_first, jnp.concatenate([stats, other_stats]), jnp.concatenate([other_stats, stats])
    )

    own_out = jnp.where(on_first, result_one, result_two)
    other_out = swapped(jnp.where(on_first, result_two, result_one))
    other_grad = swapped(jnp.where(on_first, grad_one, standard_grad.astype(bf16)))
    input_grads, section_output = final(
        z, sec, inputs, series_id, stats_all, series_all, standard_grad, grad_one, other_grad,
        own_out, other_out,
    )

    parts = []
    for one, two in (
        (feed_one[0], feed_two[0]), (feed_one[1], feed_two[1]), (attention_one, attention_two)
    ):
        kept = jnp.where(
            on_first,
            one.astype(f32) + to_section(one, 0).astype(f32),
            two.astype(f32) + to_section(two, 1).astype(f32),
        )
        parts.append(kept.astype(bf16))
    bits, turned = exchange_steps(count)
    near, far = list(zip(bits, turned)), list(zip(turned, bits))
    orders = (near, far, near[2:] + near[:2])
    for k in range(len(bits)):
        parts = [halve(p, o[k], section, index, count) for p, o in zip(parts, orders)]
    for k in reversed(range(len(bits))):
        parts = [double(p, o[k], section, index, count) for p, o in zip(parts, orders)]

    params = pltpu.CompilerParams(vmem_limit_bytes=56 * 2**20)
    grad_gate, grad_up, grad_down = pl.pallas_call(
        unpack_feed_body,
        out_shape=[shape(width, z.hidden), shape(width, z.hidden), shape(z.hidden, width)],
        compiler_params=params,
        name="unpack_feed",
    )(*parts[:2])
    vmem = pl.BlockSpec(memory_space=pltpu.VMEM)
    grad_query, grad_key, grad_value, grad_out, grad_attention_gain, grad_feed_gain, grad_bias = (
        pl.pallas_call(
            unpack_attention_body,
            in_specs=[SCALARS, vmem, vmem],
            out_shape=[shape(width, width)] * 4 + [shape(1, width)] * 2 + [shape(heads, 2)],
            compiler_params=params,
            name="unpack_attention",
        )(sec, parts[2], small)
    )
    return (
        section_output[None],
        input_grads[None],
        grad_attention_gain,
        grad_query[None],
        grad_key[None],
        grad_value[None],
        grad_out[None],
        grad_bias[None],
        grad_feed_gain,
        grad_gate[None],
        grad_up[None],
        grad_down[None],
    )


def solution(mesh):
    placed = (
        P(None, "dp", None),
        P(None, "dp"),
        P(None, "dp"),
        P(None, "dp"),
        P(None, "dp", None),
        P("section", None),
        P("section", None, None),
        P("section", None, None),
        P("section", None, None),
        P("section", None, None),
        P("section", None, None),
        P("section", None),
        P("section", None, None),
        P("section", None, None),
        P("section", None, None),
    )
    return jax.shard_map(
        per_device,
        mesh=mesh,
        in_specs=placed,
        out_specs=(
            P("section", None, "dp", None),
            P("section", None, "dp", None),
            P("section", None),
            P("section", None, None),
            P("section", None, None),
            P("section", None, None),
            P("section", None, None),
            P("section", None, None),
            P("section", None),
            P("section", None, None),
            P("section", None, None),
            P("section", None, None),
        ),
        check_vma=False,
    )
```

```python
import jax
import jax.numpy as jnp
import numpy as np
from jax import lax
from jax.experimental import pallas as pl
from jax.experimental.pallas import tpu as pltpu
from jax.sharding import PartitionSpec as P

HD = 64
BLOCK = 512
SER_DEV = 4
LANES = 128
CHUNK = 256
TILE = 256

norm_epsilon = 1e-05
scale_epsilon = 1e-05
masked_score = -1e30

f32 = jnp.float32
bf16 = jnp.bfloat16

AS_IS = (((1,), (0,)), ((), ()))
RIGHT_T = (((1,), (1,)), ((), ()))
LEFT_T = (((0,), (0,)), ((), ()))


def dot(left, right, dims=AS_IS):
    return lax.dot_general(left, right, dims, preferred_element_type=f32)


def column(row):
    return jnp.broadcast_to(row.astype(f32), (LANES, row.shape[1])).T


def lane_index(rows):
    return lax.broadcasted_iota(jnp.int32, (rows, LANES), 1)


def regroup(x):
    group = lane_index(x.shape[0]) // (HD // 2)
    return jnp.where(
        group == 1,
        pltpu.roll(x, LANES - HD // 2, 1),
        jnp.where(group == 2, pltpu.roll(x, HD // 2, 1), x),
    )


def turn(x, cosine, sine):
    return x * cosine + pltpu.roll(x, LANES // 2, 1) * sine


def turn_back(x, cosine, sine):
    return x * cosine - pltpu.roll(x, LANES // 2, 1) * sine


def inverse_rms(x):
    return lax.rsqrt(jnp.mean(x * x, axis=1, keepdims=True) + norm_epsilon)


def series_hits(sid_col, piece):
    return sid_col == (lane_index(sid_col.shape[0]) + piece * LANES).astype(f32)


def rows_of(hits, per_series):
    return jnp.sum(jnp.where(hits, per_series, 0.0), axis=1, keepdims=True)


def series_of(hits, per_row):
    return jnp.sum(jnp.where(hits, per_row, 0.0), axis=0, keepdims=True)


def stats_body(sec_ref, x_ref, sid_ref, out_ref):
    m = pl.num_programs(0) * sec_ref[0] + pl.program_id(0)
    x = x_ref[0].astype(f32)
    width = x.shape[1]
    sid_col = column(sid_ref[pl.ds(m, 1), :])
    pieces = out_ref.shape[-1] // LANES
    totals = jnp.sum(x, axis=1, keepdims=True)
    centre = jnp.zeros_like(totals)
    out_ref[0] = jnp.zeros(out_ref.shape[1:], f32)
    for piece in range(pieces):
        hits = series_hits(sid_col, piece)
        count = series_of(hits, 1.0)
        total = series_of(hits, totals)
        centre = centre + rows_of(hits, total / (jnp.maximum(count, 1.0) * width))
        out_ref[0, 0:1, piece * LANES : (piece + 1) * LANES] = count
        out_ref[0, 1:2, piece * LANES : (piece + 1) * LANES] = total
    centred = x - centre
    squares = jnp.sum(centred * centred, axis=1, keepdims=True)
    for piece in range(pieces):
        hits = series_hits(sid_col, piece)
        out_ref[0, 2:3, piece * LANES : (piece + 1) * LANES] = series_of(hits, squares)


def merge_stats(here, there, width):
    count_a, total_a, spread_a = here[:, 0], here[:, 1], here[:, 2]
    count_b, total_b, spread_b = there[:, 0], there[:, 1], there[:, 2]
    count = count_a + count_b
    gap = total_a / (jnp.maximum(count_a, 1.0) * width) - total_b / (
        jnp.maximum(count_b, 1.0) * width
    )
    weight = count_a * count_b * width / jnp.maximum(count, 1.0)
    spread = spread_a + spread_b + gap * gap * weight
    rest = jnp.zeros_like(here[:, 3:])
    return jnp.concatenate(
        [jnp.stack([count, total_a + total_b, spread], axis=1), rest], axis=1
    )


def centre_and_scale(stats, width):
    entries = jnp.maximum(stats[0:1], 1.0) * width
    centre = stats[1:2] / entries
    scaling = jnp.sqrt(stats[2:3] / entries + scale_epsilon)
    return entries, centre, scaling


class Weights:
    def __init__(self, take_own, own_refs, other_refs, big_ref, down_ref, sems):
        self.first_step = pl.program_id(0) == 0
        self.big, self.down = big_ref, down_ref
        self.own_refs, self.sems = own_refs, sems
        self.targets = []
        at = 0
        for ref in own_refs[:6]:
            self.targets.append(big_ref.at[:, pl.ds(at, ref.shape[1])])
            at += ref.shape[1]
        self.targets.append(down_ref)

        def start(refs):
            for k, (src, dst) in enumerate(zip(refs, self.targets)):
                pltpu.make_async_copy(src, dst, sems.at[k]).start()

        @pl.when(jnp.logical_and(self.first_step, take_own))
        def _():
            start(own_refs)

        @pl.when(jnp.logical_and(self.first_step, jnp.logical_not(take_own)))
        def _():
            start(other_refs)

    def wait_here(self, *numbers):
        for k in numbers:
            pltpu.make_async_copy(self.own_refs[k], self.targets[k], self.sems.at[k]).wait()

    def wait(self, *numbers):
        @pl.when(self.first_step)
        def _():
            self.wait_here(*numbers)

    def wait_attention(self):
        width = self.big.shape[0]

        @pl.when(self.first_step)
        def _():
            self.wait_here(0, 1, 2, 3)
            for at in range(0, 2 * width, LANES):
                tile = self.big[:, at : at + LANES].astype(f32)
                self.big[:, at : at + LANES] = regroup(tile).astype(bf16)


def sigmoid(x):
    return 0.5 * jnp.tanh(0.5 * x) + 0.5


def in_head(half, lanes, grouped):
    if grouped:
        return (lanes % HD) // (HD // 2) == half
    return lanes // HD == half


def row_index(rows):
    return lax.broadcasted_iota(jnp.int32, (LANES, rows), 0)


class Block:
    def __init__(self, cosine, sine, item_col, var_col, var_row, same_ref):
        rows = cosine.shape[0]
        self.cosine, self.sine, self.same_ref = cosine, sine, same_ref
        row = var_row.astype(f32)
        for at in range(0, rows, LANES):
            same_ref[:, at : at + LANES] = jnp.where(var_col == row[:, at : at + LANES], 1.0, 0.0)
        lane = lane_index(rows)
        second = jnp.where(item_col > 0.0, 1.0, 0.0)
        self.item_q = jnp.where(
            lane == 0, second, jnp.where(lane == 1, 1.0 - second, 0.0)
        ).astype(bf16)
        self.item_k = jnp.where(
            lane == 0,
            (1.0 - second) * masked_score,
            jnp.where(lane == 1, second * masked_score, 0.0),
        ).astype(bf16)


def attention_forward(hidden, gains, block, bias_ref, bias_at, weights, saved):
    qkv_ref, prob_ref, inv_ref, mixed_ref = saved
    rows, width = hidden.shape
    pairs = width // LANES
    tiles = rows // TILE
    big_ref = weights.big
    normed = (hidden * inverse_rms(hidden) * gains).astype(bf16)
    weights.wait_attention()
    lane = lane_index(rows)
    first_rows = row_index(rows) < HD
    extra = lax.broadcasted_iota(jnp.int32, (16, rows), 0)

    def project(p):
        at = p * LANES
        q = turn(dot(normed, big_ref[:, at : at + LANES]), block.cosine, block.sine)
        k = turn(dot(normed, big_ref[:, width + at : width + at + LANES]), block.cosine, block.sine)
        v = dot(normed, big_ref[:, 2 * width + at : 2 * width + at + LANES])
        qkv_ref[:, at : at + LANES] = (q * HD**-0.5).astype(bf16)
        qkv_ref[:, width + at : width + at + LANES] = k.astype(bf16)
        qkv_ref[:, 2 * width + at : 2 * width + at + LANES] = v.astype(bf16)

    def operands(p):
        at = p * LANES
        q_pair = qkv_ref[:, at : at + LANES]
        k_aug = jnp.concatenate([qkv_ref[:, width + at : width + at + LANES], block.item_k], axis=1)
        v_turned = qkv_ref[:, 2 * width + at : 2 * width + at + LANES].T
        heads = []
        for half in range(2):
            q_aug = jnp.concatenate(
                [jnp.where(in_head(half, lane, True), q_pair, 0.0).astype(bf16), block.item_q],
                axis=1,
            )
            own_rows = first_rows if half == 0 else jnp.logical_not(first_rows)
            v_aug = jnp.concatenate(
                [
                    jnp.where(own_rows, v_turned, 0.0).astype(bf16),
                    jnp.where(extra == half, 1.0, 0.0).astype(bf16),
                ],
                axis=0,
            )
            heads.append((q_aug, v_aug))
        return k_aug, heads

    prepared = {}

    def scores_of(p, half, t):
        if p not in prepared:
            project(p)
            prepared[p] = operands(p)
        k_aug, heads = prepared[p]
        return dot(k_aug, heads[half][0][t * TILE : (t + 1) * TILE, :], RIGHT_T)

    order = [(p, half, t) for p in range(pairs) for half in range(2) for t in range(tiles)]
    attended = {}
    scores = scores_of(*order[0])
    for n, (p, half, t) in enumerate(order):
        following = scores_of(*order[n + 1]) if n + 1 < len(order) else None
        head = 2 * p + half
        cols = slice(t * TILE, (t + 1) * TILE)
        gap = bias_ref[bias_at + 2 * head] - bias_ref[bias_at + 2 * head + 1]
        biased = scores + block.same_ref[:, cols] * gap
        peak = jnp.max(biased, axis=0, keepdims=True)
        prob = jnp.exp(biased - peak).astype(bf16)
        prob_ref[head, :, cols] = prob
        part = dot(prepared[p][1][half][1], prob)
        attended[p, t] = part if half == 0 else attended[p, t] + part
        if half == 1:
            sums = attended.pop((p, t))
            own_rows = row_index(TILE) < HD
            inv = jnp.where(
                own_rows, 1.0 / sums[LANES : LANES + 1], 1.0 / sums[LANES + 1 : LANES + 2]
            )
            inv_ref[cols, p * LANES : (p + 1) * LANES] = inv.T
            mixed_ref[cols, p * LANES : (p + 1) * LANES] = (sums[:LANES] * inv).T
        scores = following
    return hidden + dot(mixed_ref[...].astype(bf16), big_ref[:, 3 * width : 4 * width])


def feed_forward(middle, gains, weights):
    big_ref, down_ref = weights.big, weights.down
    weights.wait(4, 5, 6)
    width = middle.shape[1]
    hidden = down_ref.shape[0]
    feed = (middle * inverse_rms(middle) * gains).astype(bf16)
    total = middle
    for at in range(0, hidden, CHUNK):
        gate = dot(feed, big_ref[:, 4 * width + at : 4 * width + at + CHUNK])
        up = dot(feed, big_ref[:, 4 * width + hidden + at : 4 * width + hidden + at + CHUNK])
        active = (gate * sigmoid(gate) * up).astype(bf16)
        total = total + dot(active, down_ref[at : at + CHUNK, :])
    return total.astype(bf16)


def feed_both(middle, gains, grad_low, weights, accs, with_result):
    gate_acc, up_acc, down_acc, gain_acc = accs
    big_ref, down_ref = weights.big, weights.down
    if with_result:
        weights.wait(4, 5, 6)
    width = middle.shape[1]
    hidden = down_ref.shape[0]
    inverse = inverse_rms(middle)
    feed = (middle * inverse * gains).astype(bf16)
    feed_t = feed.T
    total = middle
    feed_grad = jnp.zeros(middle.shape, f32)
    for at in range(0, hidden, CHUNK):
        gate_w = big_ref[:, 4 * width + at : 4 * width + at + CHUNK]
        up_w = big_ref[:, 4 * width + hidden + at : 4 * width + hidden + at + CHUNK]
        down_w = down_ref[at : at + CHUNK, :]
        gate = dot(feed, gate_w)
        up = dot(feed, up_w)
        act_grad = dot(grad_low, down_w, RIGHT_T)
        gated = sigmoid(gate)
        swish = gate * gated
        active = (swish * up).astype(bf16)
        gate_grad = (act_grad * up * (gated + swish * (1.0 - gated))).astype(bf16)
        up_grad = (act_grad * swish).astype(bf16)
        if with_result:
            total = total + dot(active, down_w)
        feed_grad = feed_grad + dot(gate_grad, gate_w, RIGHT_T) + dot(up_grad, up_w, RIGHT_T)
        gate_acc[:, at : at + CHUNK] += dot(feed_t, gate_grad)
        up_acc[:, at : at + CHUNK] += dot(feed_t, up_grad)
        down_acc[at : at + CHUNK, :] += dot(active, grad_low, LEFT_T)
    scaled = feed_grad * gains
    gain_acc[...] += jnp.sum(feed_grad * middle * inverse, axis=0, keepdims=True)
    middle_grad = (
        grad_low.astype(f32)
        + inverse * scaled
        - middle * (inverse * inverse * inverse) * jnp.mean(scaled * middle, axis=1, keepdims=True)
    )
    return total, middle_grad


def attention_backward(middle_grad, hidden, gains, block, weights, saved, grads_ref, accs):
    qkv_ref, prob_ref, inv_ref, mixed_ref = saved
    qkv_acc, out_acc, gain_acc, bias_acc = accs
    rows, width = hidden.shape
    pairs = width // LANES
    tiles = rows // TILE
    big_ref = weights.big
    mix_grad = middle_grad.astype(bf16)
    att_grad = dot(mix_grad, big_ref[:, 3 * width : 4 * width], RIGHT_T).astype(bf16)
    lane = lane_index(rows)
    ones_four = jnp.where(lane < 4, 1.0, 0.0).astype(bf16)
    source = lax.broadcasted_iota(jnp.int32, (2 * LANES, LANES), 0) % LANES // HD
    target = lax.broadcasted_iota(jnp.int32, (2 * LANES, LANES), 1)
    gather = jnp.where((target // 2 == source) & (target < 4), 1.0, 0.0).astype(bf16)

    def operands(p):
        at = p * LANES
        q_pair = qkv_ref[:, at : at + LANES]
        k_turned = qkv_ref[:, width + at : width + at + LANES].T
        v_aug = jnp.concatenate(
            [qkv_ref[:, 2 * width + at : 2 * width + at + LANES], ones_four], axis=1
        )
        grad_pair = (att_grad[:, at : at + LANES].astype(f32) * inv_ref[:, at : at + LANES]).astype(
            bf16
        )
        product = grad_pair.astype(f32) * mixed_ref[:, at : at + LANES]
        high = product.astype(bf16)
        low = (product - high.astype(f32)).astype(bf16)
        inner = dot(jnp.concatenate([high, low], axis=1), gather)
        inner_high = inner.astype(bf16).astype(f32)
        tail = jnp.where(lane % 2 == 0, -inner_high, inner_high - inner)
        heads = []
        for half in range(2):
            grad_low = jnp.where(in_head(half, lane, False), grad_pair, 0.0).astype(bf16)
            tail_low = jnp.where(lane // 2 == half, tail, 0.0).astype(bf16)
            q_mine = jnp.where(in_head(half, lane, True), q_pair, 0.0).astype(bf16)
            k_mine = jnp.where(in_head(half, row_index(rows), True), k_turned, 0.0).astype(bf16)
            heads.append(
                (jnp.concatenate([grad_low, tail_low], axis=1), grad_low, q_mine, k_mine)
            )
        return v_aug, heads

    prepared = {}

    def prob_grad_of(p, half, t):
        if p not in prepared:
            prepared[p] = operands(p)
        v_aug, heads = prepared[p]
        return dot(v_aug, heads[half][0][t * TILE : (t + 1) * TILE, :], RIGHT_T)

    order = [(p, half, t) for p in range(pairs) for half in range(2) for t in range(tiles)]
    value_grad = key_grad = None
    query_grad = {}
    prob_grad = prob_grad_of(*order[0])
    for n, (p, half, t) in enumerate(order):
        following = prob_grad_of(*order[n + 1]) if n + 1 < len(order) else None
        head = 2 * p + half
        cols = slice(t * TILE, (t + 1) * TILE)
        at = p * LANES
        _, grad_low, q_mine, k_mine = prepared[p][1][half]
        prob = prob_ref[head, :, cols]
        score_grad = prob.astype(f32) * prob_grad
        bias_acc[head : head + 1, cols] += jnp.sum(
            score_grad * block.same_ref[:, cols], axis=0, keepdims=True
        )
        score_low = score_grad.astype(bf16)
        part_v = dot(prob, grad_low[cols, :])
        part_k = dot(score_low, q_mine[cols, :])
        part_q = dot(k_mine, score_low)
        value_grad = part_v if value_grad is None else value_grad + part_v
        key_grad = part_k if key_grad is None else key_grad + part_k
        query_grad[t] = part_q if half == 0 else query_grad[t] + part_q
        if half == 1:
            back = query_grad[t].T * HD**-0.5
            grads_ref[cols, at : at + LANES] = turn_back(
                back, block.cosine[cols, :], block.sine[cols, :]
            ).astype(bf16)
        if half == 1 and t == tiles - 1:
            grads_ref[:, width + at : width + at + LANES] = turn_back(
                key_grad, block.cosine, block.sine
            ).astype(bf16)
            grads_ref[:, 2 * width + at : 2 * width + at + LANES] = value_grad.astype(bf16)
            value_grad = key_grad = None
        prob_grad = following
    out_acc[...] += dot(mixed_ref[...].astype(bf16), mix_grad, LEFT_T)
    inverse = inverse_rms(hidden)
    normed = (hidden * inverse * gains).astype(bf16)
    normed_grad = dot(grads_ref[...], big_ref[:, : 3 * width], RIGHT_T)
    qkv_acc[...] += dot(normed, grads_ref[...], LEFT_T)
    scaled = normed_grad * gains
    gain_acc[...] += jnp.sum(normed_grad * hidden * inverse, axis=0, keepdims=True)
    return (
        middle_grad
        + inverse * scaled
        - hidden * (inverse * inverse * inverse) * jnp.mean(scaled * hidden, axis=1, keepdims=True)
    )


def column_tiles(acc_ref):
    return [acc_ref[:, at : at + LANES] for at in range(0, acc_ref.shape[1], LANES)]


class Packer:
    def __init__(self, stage_ref, sems, kept_refs, sent_refs):
        self.stage_ref, self.sems = stage_ref, sems
        self.kept_refs, self.sent_refs = kept_refs, sent_refs
        self.sent = []

    def copy(self, out_ref, slot, count):
        source = self.stage_ref.at[slot, pl.ds(0, count)]
        return pltpu.make_async_copy(source, out_ref, self.sems.at[slot])

    def send(self, keep, part, start, tiles):
        slot = len(self.sent) % 2
        if len(self.sent) >= 2:
            self.wait(2)
        at = 0
        for tile in tiles:
            self.stage_ref[slot, at : at + tile.shape[0], :] = tile.astype(bf16)
            at += tile.shape[0]
        where = pl.ds(start, at)

        @pl.when(keep)
        def _():
            self.copy(self.kept_refs[part].at[where], slot, at).start()

        @pl.when(jnp.logical_not(keep))
        def _():
            self.copy(self.sent_refs[part].at[where], slot, at).start()

        self.sent.append((self.kept_refs[part].at[where], slot, at))

    def wait(self, back):
        self.copy(*self.sent[-back]).wait()

    def finish(self):
        self.wait(2)
        self.wait(1)


def layers_body(
    sec_ref, bias_ref, x_ref, grad_ref, sid_ref, item_ref, var_ref, stats_ref, table_ref,
    gain_one_ref, gain_two_ref, *refs
):
    own_refs, other_refs, refs = refs[:7], refs[7:14], refs[14:]
    result_one_ref, result_two_ref, grad_one_ref, grad_zero_ref, series_ref = refs[:5]
    small_refs, kept_refs, sent_refs, refs = refs[5:7], refs[7:10], refs[10:13], refs[13:]
    big_refs, down_refs, refs = refs[:2], refs[2:4], refs[4:]
    feed_accs, attention_accs, refs = (refs[:4], refs[4:8]), (refs[8:12], refs[12:16]), refs[16:]
    saved, refs = (refs[:4], refs[4:8]), refs[8:]
    same_ref, grads_ref, standard_ref, middle_ref, stage_ref, sems, stage_sems = refs

    i = pl.program_id(0)
    last = i == pl.num_programs(0) - 1
    m = pl.num_programs(0) * sec_ref[0] + i
    weights = [
        Weights(sec_ref[0] == k, own_refs, other_refs, big_refs[k], down_refs[k], sems.at[k])
        for k in range(2)
    ]
    packer = Packer(stage_ref, stage_sems, kept_refs, sent_refs)
    on_first = sec_ref[0] == 0

    @pl.when(i == 0)
    def _():
        for accs in feed_accs + attention_accs:
            for acc in accs:
                acc[...] = jnp.zeros_like(acc)

    x = x_ref[0].astype(f32)
    rows, width = x.shape
    var_row = var_ref[pl.ds(m, 1), :]
    var_col = column(var_row)
    sid_col = column(sid_ref[pl.ds(m, 1), :])
    pieces = stats_ref.shape[-1] // LANES

    time = lax.broadcasted_iota(jnp.int32, (rows, LANES), 0).astype(f32) - var_col
    cosine = sine = jnp.zeros((rows, LANES), f32)
    for at in range(0, rows, LANES):
        hot = jnp.where(time == (lane_index(rows) + at).astype(f32), 1.0, 0.0).astype(bf16)
        found = dot(hot, table_ref[at : at + LANES, :])
        cosine = cosine + found[:, :LANES] + found[:, LANES : 2 * LANES]
        sine = sine + found[:, 2 * LANES : 3 * LANES] + found[:, 3 * LANES :]
    block = Block(cosine, sine, column(item_ref[pl.ds(m, 1), :]), var_col, var_row, same_ref)

    _, centre, scaling = centre_and_scale(stats_ref[0], width)
    centre_rows = scale_rows = 0.0
    for piece in range(pieces):
        hits = series_hits(sid_col, piece)
        part = slice(piece * LANES, (piece + 1) * LANES)
        centre_rows = centre_rows + rows_of(hits, centre[:, part])
        scale_rows = scale_rows + rows_of(hits, scaling[:, part])
    standard_ref[...] = (x - centre_rows) / scale_rows

    attention_gains = (gain_one_ref[0:1, :], gain_two_ref[0:1, :])
    feed_gains = (gain_one_ref[1:2, :], gain_two_ref[1:2, :])

    middle_ref[...] = attention_forward(
        standard_ref[...], attention_gains[0], block, bias_ref, 0, weights[0], saved[0]
    )
    result_one_ref[0] = feed_forward(middle_ref[...], feed_gains[0], weights[0])
    middle = attention_forward(
        result_one_ref[0].astype(f32), attention_gains[1], block, bias_ref,
        bias_ref.shape[0] // 2, weights[1], saved[1],
    )

    total, middle_grad = feed_both(
        middle, feed_gains[1], grad_ref[0], weights[1], feed_accs[1], True
    )
    result_two_ref[0] = total.astype(bf16)
    hidden_grad = attention_backward(
        middle_grad, result_one_ref[0].astype(f32), attention_gains[1], block, weights[1],
        saved[1], grads_ref, attention_accs[1],
    )
    grad_one_ref[0] = hidden_grad.astype(bf16)

    gate_rows = width * feed_accs[0][0].shape[1] // LANES

    def send_feed(layer, keep):
        gate, up, down = (column_tiles(acc) for acc in feed_accs[layer][:3])
        packer.send(keep, 0, 0, gate)
        packer.send(keep, 0, gate_rows, up[:4])
        packer.send(keep, 1, 0, up[4:])
        packer.send(keep, 1, gate_rows // 2, down)

    def send_attention(layer, keep):
        tiles = column_tiles(attention_accs[layer][0])
        turned = [regroup(tile) for tile in tiles[:6]]
        packer.send(keep, 2, 0, turned)
        packer.send(keep, 2, 6 * width, tiles[6:] + column_tiles(attention_accs[layer][1]))

    @pl.when(last)
    def _():
        send_feed(1, jnp.logical_not(on_first))
        send_attention(1, jnp.logical_not(on_first))

    _, middle_grad = feed_both(
        middle_ref[...], feed_gains[0], grad_one_ref[0], weights[0], feed_accs[0], False
    )

    @pl.when(last)
    def _():
        send_feed(0, on_first)

    standard = standard_ref[...]
    hidden_grad = attention_backward(
        middle_grad, standard, attention_gains[0], block, weights[0], saved[0], grads_ref,
        attention_accs[0],
    )
    grad_zero_ref[0] = hidden_grad
    grad_rows = jnp.sum(hidden_grad, axis=1, keepdims=True)
    cross_rows = jnp.sum(hidden_grad * standard, axis=1, keepdims=True)
    standard_rows = jnp.sum(standard, axis=1, keepdims=True)
    series_ref[0] = jnp.zeros(series_ref.shape[1:], f32)
    for piece in range(pieces):
        hits = series_hits(sid_col, piece)
        part = slice(piece * LANES, (piece + 1) * LANES)
        series_ref[0, 0:1, part] = series_of(hits, grad_rows)
        series_ref[0, 1:2, part] = series_of(hits, cross_rows)
        series_ref[0, 2:3, part] = series_of(hits, standard_rows)

    @pl.when(last)
    def _():
        send_attention(0, on_first)
        for small_ref, feed_acc, attention_acc in zip(small_refs, feed_accs, attention_accs):
            small_ref[...] = jnp.zeros_like(small_ref)
            for k in range(width // LANES):
                cols = slice(k * LANES, (k + 1) * LANES)
                small_ref[k : k + 1, :] = attention_acc[2][:, cols]
                small_ref[16 + k : 17 + k, :] = feed_acc[3][:, cols]
            bias_sums = jnp.sum(attention_acc[3][...], axis=1, keepdims=True)
            small_ref[8:16, :] = jnp.broadcast_to(bias_sums, (8, LANES))
        packer.finish()


def final_body(
    sec_ref, x_ref, sid_ref, stats_ref, series_ref, own_first, own_second, other_grad,
    own_out, other_out, out_ref, grads_ref,
):
    i = pl.program_id(0)
    sec = sec_ref[0]
    own = (i // (pl.num_programs(0) // 2)) == sec
    grads_ref[0] = jnp.where(own, own_out[0], other_out[0])
    grad = jnp.where(
        own,
        jnp.where(sec == 0, own_first[0], own_second[0].astype(f32)),
        other_grad[0].astype(f32),
    )

    @pl.when(sec == 0)
    def _():
        x = x_ref[0].astype(f32)
        width = x.shape[1]
        entries, centre, scaling = centre_and_scale(stats_ref[0], width)
        sums = series_ref[0]
        cross = sums[1:2] * scaling
        spread_grad = -cross / (2.0 * scaling * scaling * scaling * entries)
        mean_grad = sums[0:1] / scaling + 2.0 * spread_grad * (sums[2:3] * scaling)
        tables = (centre, 1.0 / scaling, 2.0 * spread_grad, mean_grad / entries)
        sid_col = column(sid_ref[pl.ds(i, 1), :])
        looked = [0.0, 0.0, 0.0, 0.0]
        for piece in range(stats_ref.shape[-1] // LANES):
            hits = series_hits(sid_col, piece)
            part = slice(piece * LANES, (piece + 1) * LANES)
            for k in range(4):
                looked[k] = looked[k] + rows_of(hits, tables[k][:, part])
        out_ref[0] = grad * looked[1] + (x - looked[0]) * looked[2] - looked[3]

    @pl.when(sec != 0)
    def _():
        out_ref[0] = grad


class Halves:
    def __init__(self, own_ref, got_ref, bit):
        self.own_ref, self.got_ref, self.bit = own_ref, got_ref, bit
        self.half = own_ref.shape[0]
        self.at = 0

    def rows(self, start, count, low):
        own = self.own_ref[start : start + count, :]
        got = self.got_ref[start : start + count, :]
        return jnp.where((self.bit == 0) == low, own, got).astype(f32)

    def take(self, out_ref, col, count):
        done = 0
        while done < count:
            low = self.at < self.half
            room = min(count - done, (self.half if low else 2 * self.half) - self.at)
            out_ref[done : done + room, col : col + LANES] = self.rows(
                self.at - (0 if low else self.half), room, low
            )
            done += room
            self.at += room


def unpack_body(bit_ref, *refs):
    parts = [Halves(refs[2 * k], refs[2 * k + 1], bit_ref[k]) for k in range(3)]
    refs = refs[6:]
    count = len(refs) // 2
    outs, scratch, sems = refs[:count], refs[count : 2 * count], refs[2 * count]
    copies = []
    for out_ref, scratch_ref in zip(outs, scratch):
        for col in range(0, scratch_ref.shape[1], LANES):
            while parts[0].at == 2 * parts[0].half:
                parts.pop(0)
            parts[0].take(scratch_ref, col, scratch_ref.shape[0])
        copies.append(pltpu.make_async_copy(scratch_ref, out_ref, sems.at[len(copies)]))
        copies[-1].start()
    for copy in copies:
        copy.wait()


def unpack_small_body(sec_ref, small_ref, attention_gain_ref, feed_gain_ref, bias_ref):
    base = 24 * sec_ref[0]
    for k in range(attention_gain_ref.shape[1] // LANES):
        cols = slice(k * LANES, (k + 1) * LANES)
        attention_gain_ref[:, cols] = small_ref[pl.ds(base + k, 1), :]
        feed_gain_ref[:, cols] = small_ref[pl.ds(base + 16 + k, 1), :]
    same = small_ref[pl.ds(base + 8, 8), 0:1][: bias_ref.shape[0]]
    bias_ref[:, 0:1] = same
    bias_ref[:, 1:2] = -same


def swapped(x):
    return lax.ppermute(x, "section", [(0, 1), (1, 0)])


def to_section(x, section):
    return lax.ppermute(x, "section", [(1 - section, section)])


def exchange_steps(count):
    bits = []
    step = 1
    while step < count:
        bits.append(step)
        step *= 2
    other = list(bits)
    for k in range(0, len(bits) - 1, 2):
        other[k], other[k + 1] = bits[k + 1], bits[k]
    return bits, other


def partner(x, by_first, by_second, count):
    pairs = [(i, i ^ by_first) for i in range(count)]
    pairs += [(count + i, count + (i ^ by_second)) for i in range(count)]
    return lax.ppermute(x, ("section", "dp"), pairs)


def place(steps, section, index):
    step = jnp.where(section == 0, *steps)
    return (index // step) % 2


def halve(parts, orders, k, section, index, count, *more):
    keeps, sends = [], []
    for current, order in zip(parts, orders):
        bit = place(order[k], section, index)
        half = current.shape[0] // 2
        keeps.append(lax.dynamic_slice_in_dim(current, bit * half, half, 0))
        sends.append(lax.dynamic_slice_in_dim(current, (1 - bit) * half, half, 0))
    sends, keeps, more = lax.optimization_barrier((sends, keeps, more))
    got = [partner(send, *order[k], count) for send, order in zip(sends, orders)]
    parts = [(a.astype(f32) + b.astype(f32)).astype(bf16) for a, b in zip(keeps, got)]
    return (parts, *more)


def double(parts, orders, k, section, index, count):
    parts = lax.optimization_barrier(parts)
    result = []
    for current, order in zip(parts, orders):
        bit = place(order[k], section, index)
        got = partner(current, *order[k], count)
        low = jnp.where(bit == 0, current, got)
        high = jnp.where(bit == 0, got, current)
        result.append(jnp.concatenate([low, high], axis=0))
    return result


HBM = pl.BlockSpec(memory_space=pl.ANY)
SCALARS = pl.BlockSpec(memory_space=pltpu.SMEM)


def whole_block(shape):
    return pl.BlockSpec(shape, lambda i, *_: (0,) * len(shape))


def by_step(shape):
    return pl.BlockSpec((1,) + shape, lambda i, *_: (i,) + (0,) * len(shape))


def by_batch(shape, own):
    return pl.BlockSpec((1,) + shape, lambda i, s: (own * s[0] + i,) + (0,) * len(shape))


def call(body, grid, in_specs, out_specs, out_shapes, scratch, flops, name):
    return pl.pallas_call(
        body,
        grid_spec=pltpu.PrefetchScalarGridSpec(
            num_scalar_prefetch=1,
            grid=(grid,),
            in_specs=in_specs,
            out_specs=out_specs,
            scratch_shapes=scratch,
        ),
        out_shape=out_shapes,
        compiler_params=pltpu.CompilerParams(vmem_limit_bytes=62 * 2**20),
        cost_estimate=pl.CostEstimate(flops=flops, bytes_accessed=2**22, transcendentals=0),
        name=name,
    )


def shape(*dims, dtype=f32):
    return jax.ShapeDtypeStruct(dims, dtype)


class Sizes:
    def __init__(self, inputs, heads, hidden, count):
        self.micro, self.rows, self.width = inputs.shape
        self.own = self.micro // 2
        self.heads, self.hidden, self.count = heads, hidden, count
        rows, width, own = self.rows, self.width, self.own
        self.stats = (8, -(-SER_DEV * count // LANES) * LANES)
        self.all_rows = whole_block((self.micro, rows))
        self.row = by_step((rows, width))
        self.row_batch = by_batch((rows, width), own)
        self.gain = whole_block((8, width))
        self.row_shape = shape(own, rows, width)
        self.low_shape = shape(own, rows, width, dtype=bf16)
        self.flops = 2 * rows * (4 * width * width + 3 * width * hidden) * own


def rotary_table(rows):
    lane = np.arange(LANES)
    frequency = np.float32(10000.0) ** (
        -(lane % (HD // 2)).astype(np.float32) * np.float32(2.0 / HD)
    )
    angle = np.arange(rows, dtype=np.float32)[:, None] * frequency[None, :].astype(np.float32)
    cosine = np.cos(angle.astype(np.float64))
    sine = np.sin(angle.astype(np.float64)) * np.where(lane < HD, -1.0, 1.0)
    parts = []
    for values in (cosine, sine):
        high = values.astype(jnp.bfloat16)
        parts += [high, (values - high.astype(np.float64)).astype(jnp.bfloat16)]
    return np.concatenate(parts, axis=1)


def series_stats(z, sec, inputs, series_id):
    return call(
        stats_body, z.own, [z.row_batch, z.all_rows], by_step(z.stats), shape(z.own, *z.stats),
        [], 10**7, "series_stats",
    )(sec, inputs, series_id)


def layers(z, sec, bias, inputs, cotangent, series_id, item, variate, stats, gains, own, other):
    table = rotary_table(z.rows)
    rows, width, hidden = z.rows, z.width, z.hidden
    feed_accs = [
        pltpu.VMEM((width, hidden), f32), pltpu.VMEM((width, hidden), f32),
        pltpu.VMEM((hidden, width), f32), pltpu.VMEM((1, width), f32),
    ]
    attention_accs = [
        pltpu.VMEM((width, 3 * width), f32), pltpu.VMEM((width, width), f32),
        pltpu.VMEM((1, width), f32), pltpu.VMEM((8, rows), f32),
    ]
    saved = [
        pltpu.VMEM((rows, 3 * width), bf16), pltpu.VMEM((z.heads, rows, rows), bf16),
        pltpu.VMEM((rows, width), f32), pltpu.VMEM((rows, width), f32),
    ]
    part = shape(4 * width * width // LANES, LANES, dtype=bf16)
    assert 3 * width * hidden // LANES == 2 * part.shape[0]
    return call(
        layers_body, z.own,
        [SCALARS, z.row_batch, z.row_batch, z.all_rows, z.all_rows, z.all_rows, by_step(z.stats),
         whole_block(table.shape), z.gain, z.gain] + [HBM] * 14,
        [z.row] * 4 + [by_step(z.stats)] + [whole_block((24, LANES))] * 2 + [HBM] * 6,
        [z.low_shape] * 3 + [z.row_shape, shape(z.own, *z.stats)] + [shape(24, LANES)] * 2
        + [part] * 6,
        [pltpu.VMEM((width, 4 * width + 2 * hidden), bf16)] * 2
        + [pltpu.VMEM((hidden, width), bf16)] * 2
        + feed_accs * 2 + attention_accs * 2 + saved * 2
        + [pltpu.VMEM((rows, rows), f32), pltpu.VMEM((rows, 3 * width), bf16),
           pltpu.VMEM((rows, width), f32), pltpu.VMEM((rows, width), f32),
           pltpu.VMEM((2, 8 * width, LANES), bf16),
           pltpu.SemaphoreType.DMA((2, 7)), pltpu.SemaphoreType.DMA((2,))],
        12 * z.flops, "layers",
    )(sec, bias, inputs, cotangent, series_id, item, variate, stats, jnp.asarray(table),
      *gains, *own, *other)


def final(z, sec, inputs, series_id, stats, series, own_first, own_second, other_grad,
          own_out, other_out):
    own_count = z.own

    def own_step(i, s):
        return (jnp.clip(i - own_count * s[0], 0, own_count - 1), 0, 0)

    def other_step(i, s):
        return (jnp.clip(i - own_count * (1 - s[0]), 0, own_count - 1), 0, 0)

    own_spec = pl.BlockSpec((1, z.rows, z.width), own_step)
    other_spec = pl.BlockSpec((1, z.rows, z.width), other_step)
    return call(
        final_body, z.micro,
        [z.row, z.all_rows, by_step(z.stats), by_step(z.stats), own_spec, own_spec,
         other_spec, own_spec, other_spec],
        [z.row, z.row],
        [shape(z.micro, z.rows, z.width), shape(z.micro, z.rows, z.width, dtype=bf16)],
        [], 10**10, "final",
    )(sec, inputs, series_id, stats, series, own_first, own_second, other_grad, own_out, other_out)


def per_device(
    inputs,
    series_id,
    item_offset,
    variate_offset,
    cotangent,
    attention_gain,
    query_weight,
    key_weight,
    value_weight,
    out_weight,
    variate_bias,
    feed_gain,
    gate_weight,
    up_weight,
    down_weight,
):
    section = lax.axis_index("section")
    index = lax.axis_index("dp")
    count = lax.axis_size("dp")
    on_first = section == 0
    sec = section.astype(jnp.int32).reshape(1)
    heads = variate_bias.shape[1]
    z = Sizes(inputs, heads, down_weight.shape[1], count)
    width = z.width

    stats = series_stats(z, sec, inputs, series_id)
    for step in exchange_steps(count)[0]:
        stats = merge_stats(stats, partner(stats, step, step, count), width)

    own_small = jnp.concatenate(
        [
            attention_gain,
            feed_gain,
            jnp.pad(variate_bias.reshape(1, 2 * heads), ((0, 0), (0, width - 2 * heads))),
        ],
        axis=0,
    ).astype(f32)
    own_small = jnp.pad(own_small, ((0, 5), (0, 0)))
    other_small = swapped(own_small)
    own = tuple(
        w[0]
        for w in (
            query_weight, key_weight, value_weight, out_weight, gate_weight, up_weight, down_weight
        )
    )
    other = tuple(swapped(w) for w in own)
    gains = (
        jnp.where(on_first, own_small, other_small),
        jnp.where(on_first, other_small, own_small),
    )
    bias = jnp.concatenate([g[2, : 2 * heads] for g in gains])

    result_one, result_two, grad_one, standard_grad, series_sums, small_one, small_two, *packs = (
        layers(
            z, sec, bias, inputs, cotangent, series_id, item_offset, variate_offset, stats, gains,
            own, other,
        )
    )

    parts = [
        (k.astype(f32) + swapped(t).astype(f32)).astype(bf16)
        for k, t in zip(packs[:3], packs[3:])
    ]
    bits, turned = exchange_steps(count)
    near, far = list(zip(bits, turned)), list(zip(turned, bits))
    orders = (near, far, near[2:] + near[:2])
    rounds = len(bits)

    series_rows = z.own * z.stats[0] * z.stats[1] // LANES
    small = jnp.concatenate(
        [series_sums.reshape(-1, LANES), small_one, small_two], axis=0
    )
    for k in range(rounds):
        parts, small = halve(parts, orders, k, section, index, count, small)
        small = small + partner(small, bits[rounds - 1 - k], bits[rounds - 1 - k], count)
    other_sums = swapped(small)
    mine = small[:series_rows].reshape((z.own,) + z.stats)
    theirs = other_sums[:series_rows].reshape((z.own,) + z.stats)
    series_all = jnp.where(
        on_first, jnp.concatenate([mine, theirs]), jnp.concatenate([theirs, mine])
    )
    small = small[series_rows:] + other_sums[series_rows:]
    other_stats = swapped(stats)
    stats_all = jnp.where(
        on_first, jnp.concatenate([stats, other_stats]), jnp.concatenate([other_stats, stats])
    )

    own_out = jnp.where(on_first, result_one, result_two)
    other_out = swapped(jnp.where(on_first, result_two, result_one))
    other_grad = swapped(jnp.where(on_first, grad_one, standard_grad.astype(bf16)))

    for k in reversed(range(1, rounds)):
        parts = double(parts, orders, k, section, index, count)
    sec_late, parts = lax.optimization_barrier((sec, parts))
    input_grads, section_output = final(
        z, sec_late, inputs, series_id, stats_all, series_all, standard_grad, grad_one, other_grad,
        own_out, other_out,
    )
    others = [partner(p, *o[0], count) for p, o in zip(parts, orders)]
    last_bits = jnp.stack([place(o[0], section, index) for o in orders]).astype(jnp.int32)

    vmem = pl.BlockSpec(memory_space=pltpu.VMEM)

    large = [shape(width, z.hidden)] * 2 + [shape(z.hidden, width)] + [shape(width, width)] * 4
    grad_gate, grad_up, grad_down, grad_query, grad_key, grad_value, grad_out = pl.pallas_call(
        unpack_body,
        in_specs=[SCALARS] + [vmem] * 6,
        out_specs=[HBM] * 7,
        out_shape=large,
        scratch_shapes=[pltpu.VMEM(s.shape, f32) for s in large] + [pltpu.SemaphoreType.DMA((7,))],
        compiler_params=pltpu.CompilerParams(vmem_limit_bytes=62 * 2**20),
        name="unpack",
    )(last_bits, *(array for pair in zip(parts, others) for array in pair))
    grad_attention_gain, grad_feed_gain, grad_bias = pl.pallas_call(
        unpack_small_body,
        in_specs=[SCALARS, vmem],
        out_shape=[shape(1, width)] * 2 + [shape(heads, 2)],
        name="unpack_small",
    )(sec, small)
    return (
        section_output[None],
        input_grads[None],
        grad_attention_gain,
        grad_query[None],
        grad_key[None],
        grad_value[None],
        grad_out[None],
        grad_bias[None],
        grad_feed_gain,
        grad_gate[None],
        grad_up[None],
        grad_down[None],
    )


def solution(mesh):
    placed = (
        P(None, "dp", None),
        P(None, "dp"),
        P(None, "dp"),
        P(None, "dp"),
        P(None, "dp", None),
        P("section", None),
        P("section", None, None),
        P("section", None, None),
        P("section", None, None),
        P("section", None, None),
        P("section", None, None),
        P("section", None),
        P("section", None, None),
        P("section", None, None),
        P("section", None, None),
    )
    return jax.shard_map(
        per_device,
        mesh=mesh,
        in_specs=placed,
        out_specs=(
            P("section", None, "dp", None),
            P("section", None, "dp", None),
            P("section", None),
            P("section", None, None),
            P("section", None, None),
            P("section", None, None),
            P("section", None, None),
            P("section", None, None),
            P("section", None),
            P("section", None, None),
            P("section", None, None),
            P("section", None, None),
        ),
        check_vma=False,
    )
```

```python
import jax
import jax.numpy as jnp
import numpy as np
from jax import lax
from jax.experimental import pallas as pl
from jax.experimental.pallas import tpu as pltpu
from jax.sharding import PartitionSpec as P

HD = 64
BLOCK = 512
SER_DEV = 4
LANES = 128
CHUNK = 256
TILE = 256

norm_epsilon = 1e-05
scale_epsilon = 1e-05
masked_score = -1e30

f32 = jnp.float32
bf16 = jnp.bfloat16

AS_IS = (((1,), (0,)), ((), ()))
RIGHT_T = (((1,), (1,)), ((), ()))
LEFT_T = (((0,), (0,)), ((), ()))


def dot(left, right, dims=AS_IS):
    return lax.dot_general(left, right, dims, preferred_element_type=f32)


def column(row):
    return jnp.broadcast_to(row.astype(f32), (LANES, row.shape[1])).T


def lane_index(rows):
    return lax.broadcasted_iota(jnp.int32, (rows, LANES), 1)


def regroup(x):
    group = lane_index(x.shape[0]) // (HD // 2)
    return jnp.where(
        group == 1,
        pltpu.roll(x, LANES - HD // 2, 1),
        jnp.where(group == 2, pltpu.roll(x, HD // 2, 1), x),
    )


def turn(x, cosine, sine):
    return x * cosine + pltpu.roll(x, LANES // 2, 1) * sine


def turn_back(x, cosine, sine):
    return x * cosine - pltpu.roll(x, LANES // 2, 1) * sine


def inverse_rms(x):
    return lax.rsqrt(jnp.mean(x * x, axis=1, keepdims=True) + norm_epsilon)


def series_hits(sid_col, piece):
    return sid_col == (lane_index(sid_col.shape[0]) + piece * LANES).astype(f32)


def rows_of(hits, per_series):
    return jnp.sum(jnp.where(hits, per_series, 0.0), axis=1, keepdims=True)


def series_of(hits, per_row):
    return jnp.sum(jnp.where(hits, per_row, 0.0), axis=0, keepdims=True)


def stats_body(sec_ref, x_ref, sid_ref, out_ref):
    m = pl.num_programs(0) * sec_ref[0] + pl.program_id(0)
    x = x_ref[0].astype(f32)
    width = x.shape[1]
    sid_col = column(sid_ref[pl.ds(m, 1), :])
    pieces = out_ref.shape[-1] // LANES
    totals = jnp.sum(x, axis=1, keepdims=True)
    centre = jnp.zeros_like(totals)
    out_ref[0] = jnp.zeros(out_ref.shape[1:], f32)
    for piece in range(pieces):
        hits = series_hits(sid_col, piece)
        count = series_of(hits, 1.0)
        total = series_of(hits, totals)
        centre = centre + rows_of(hits, total / (jnp.maximum(count, 1.0) * width))
        out_ref[0, 0:1, piece * LANES : (piece + 1) * LANES] = count
        out_ref[0, 1:2, piece * LANES : (piece + 1) * LANES] = total
    centred = x - centre
    squares = jnp.sum(centred * centred, axis=1, keepdims=True)
    for piece in range(pieces):
        hits = series_hits(sid_col, piece)
        out_ref[0, 2:3, piece * LANES : (piece + 1) * LANES] = series_of(hits, squares)


def merge_stats(here, there, width):
    count_a, total_a, spread_a = here[:, 0], here[:, 1], here[:, 2]
    count_b, total_b, spread_b = there[:, 0], there[:, 1], there[:, 2]
    count = count_a + count_b
    gap = total_a / (jnp.maximum(count_a, 1.0) * width) - total_b / (
        jnp.maximum(count_b, 1.0) * width
    )
    weight = count_a * count_b * width / jnp.maximum(count, 1.0)
    spread = spread_a + spread_b + gap * gap * weight
    rest = jnp.zeros_like(here[:, 3:])
    return jnp.concatenate(
        [jnp.stack([count, total_a + total_b, spread], axis=1), rest], axis=1
    )


def centre_and_scale(stats, width):
    entries = jnp.maximum(stats[0:1], 1.0) * width
    centre = stats[1:2] / entries
    scaling = jnp.sqrt(stats[2:3] / entries + scale_epsilon)
    return entries, centre, scaling


class Weights:
    def __init__(self, section, own_refs, other_refs, big_ref, down_ref, sems):
        self.first_step = pl.program_id(0) == 0
        self.big_ref, self.down_ref = big_ref, down_ref
        self.own_refs, self.sems = own_refs, sems

        @pl.when(self.first_step)
        def _():
            for layer_of, refs in ((section, own_refs), (1 - section, other_refs)):
                for k, ref in enumerate(refs):
                    pltpu.make_async_copy(ref, self.target(layer_of, k), sems.at[layer_of, k]).start()

    def target(self, layer, k):
        if k == 6:
            return self.down_ref.at[layer]
        at = sum(ref.shape[1] for ref in self.own_refs[:k])
        return self.big_ref.at[layer, :, pl.ds(at, self.own_refs[k].shape[1])]

    def wait_here(self, layer, numbers):
        for k in numbers:
            pltpu.make_async_copy(
                self.own_refs[k], self.target(layer, k), self.sems.at[layer, k]
            ).wait()

    def wait_attention(self, layer):
        width = self.big_ref.shape[1]

        @pl.when(self.first_step)
        def _():
            self.wait_here(layer, (0, 1, 2, 3))
            for at in range(0, 2 * width, LANES):
                tile = self.big_ref[layer, :, at : at + LANES].astype(f32)
                self.big_ref[layer, :, at : at + LANES] = regroup(tile).astype(bf16)

    def wait_feed(self, layer):
        @pl.when(self.first_step)
        def _():
            self.wait_here(layer, (4, 5, 6))


def sigmoid(x):
    return 0.5 * jnp.tanh(0.5 * x) + 0.5


def in_head(half, lanes, grouped):
    if grouped:
        return (lanes % HD) // (HD // 2) == half
    return lanes // HD == half


def row_index(rows):
    return lax.broadcasted_iota(jnp.int32, (LANES, rows), 0)


class Block:
    def __init__(self, cosine, sine, item_col, var_col, var_row, same_ref):
        rows = cosine.shape[0]
        self.cosine, self.sine, self.same_ref = cosine, sine, same_ref
        row = var_row.astype(f32)
        for at in range(0, rows, LANES):
            same_ref[:, at : at + LANES] = jnp.where(var_col == row[:, at : at + LANES], 1.0, 0.0)
        lane = lane_index(rows)
        second = jnp.where(item_col > 0.0, 1.0, 0.0)
        self.item_q = jnp.where(
            lane == 0, second, jnp.where(lane == 1, 1.0 - second, 0.0)
        ).astype(bf16)
        self.item_k = jnp.where(
            lane == 0,
            (1.0 - second) * masked_score,
            jnp.where(lane == 1, second * masked_score, 0.0),
        ).astype(bf16)


def attention_forward(layer, hidden, gains, block, bias_ref, weights, saved):
    qkv_ref, prob_ref, inv_ref, mixed_ref = (ref.at[layer] for ref in saved)
    bias_at = layer * (bias_ref.shape[0] // 2)
    rows, width = hidden.shape
    pairs = width // LANES
    tiles = rows // TILE
    big_ref = weights.big_ref.at[layer]
    normed = (hidden * inverse_rms(hidden) * gains).astype(bf16)
    weights.wait_attention(layer)
    lane = lane_index(rows)
    first_rows = row_index(rows) < HD
    extra = lax.broadcasted_iota(jnp.int32, (16, rows), 0)

    projected = dot(normed, big_ref[:, : 3 * width])

    def project(p):
        at = p * LANES
        q = turn(projected[:, at : at + LANES], block.cosine, block.sine)
        k = turn(projected[:, width + at : width + at + LANES], block.cosine, block.sine)
        v = projected[:, 2 * width + at : 2 * width + at + LANES]
        qkv_ref[:, at : at + LANES] = (q * HD**-0.5).astype(bf16)
        qkv_ref[:, width + at : width + at + LANES] = k.astype(bf16)
        qkv_ref[:, 2 * width + at : 2 * width + at + LANES] = v.astype(bf16)

    def operands(p):
        at = p * LANES
        q_pair = qkv_ref[:, at : at + LANES]
        k_aug = jnp.concatenate([qkv_ref[:, width + at : width + at + LANES], block.item_k], axis=1)
        v_turned = qkv_ref[:, 2 * width + at : 2 * width + at + LANES].T
        heads = []
        for half in range(2):
            q_aug = jnp.concatenate(
                [jnp.where(in_head(half, lane, True), q_pair, 0.0).astype(bf16), block.item_q],
                axis=1,
            )
            own_rows = first_rows if half == 0 else jnp.logical_not(first_rows)
            v_aug = jnp.concatenate(
                [
                    jnp.where(own_rows, v_turned, 0.0).astype(bf16),
                    jnp.where(extra == half, 1.0, 0.0).astype(bf16),
                ],
                axis=0,
            )
            heads.append((q_aug, v_aug))
        return k_aug, heads

    prepared = {}

    def scores_of(p, half, t):
        if p not in prepared:
            project(p)
            prepared[p] = operands(p)
        k_aug, heads = prepared[p]
        return dot(k_aug, heads[half][0][t * TILE : (t + 1) * TILE, :], RIGHT_T)

    order = [(p, half, t) for p in range(pairs) for half in range(2) for t in range(tiles)]
    attended = {}
    scores = scores_of(*order[0])
    for n, (p, half, t) in enumerate(order):
        following = scores_of(*order[n + 1]) if n + 1 < len(order) else None
        head = 2 * p + half
        cols = slice(t * TILE, (t + 1) * TILE)
        gap = bias_ref[bias_at + 2 * head] - bias_ref[bias_at + 2 * head + 1]
        biased = scores + block.same_ref[:, cols] * gap
        peak = jnp.max(biased, axis=0, keepdims=True)
        prob = jnp.exp(biased - peak).astype(bf16)
        prob_ref[head, :, cols] = prob
        part = dot(prepared[p][1][half][1], prob)
        attended[p, t] = part if half == 0 else attended[p, t] + part
        if half == 1:
            sums = attended.pop((p, t))
            own_rows = row_index(TILE) < HD
            inv = jnp.where(
                own_rows, 1.0 / sums[LANES : LANES + 1], 1.0 / sums[LANES + 1 : LANES + 2]
            )
            inv_ref[cols, p * LANES : (p + 1) * LANES] = inv.T
            mixed_ref[cols, p * LANES : (p + 1) * LANES] = (sums[:LANES] * inv).T
        scores = following
    return hidden + dot(mixed_ref[...].astype(bf16), big_ref[:, 3 * width : 4 * width])


def feed_forward(layer, middle, gains, weights):
    big_ref, down_ref = weights.big_ref.at[layer], weights.down_ref.at[layer]
    weights.wait_feed(layer)
    width = middle.shape[1]
    hidden = down_ref.shape[0]
    feed = (middle * inverse_rms(middle) * gains).astype(bf16)
    total = middle
    for at in range(0, hidden, CHUNK):
        gate = dot(feed, big_ref[:, 4 * width + at : 4 * width + at + CHUNK])
        up = dot(feed, big_ref[:, 4 * width + hidden + at : 4 * width + hidden + at + CHUNK])
        active = (gate * sigmoid(gate) * up).astype(bf16)
        total = total + dot(active, down_ref[at : at + CHUNK, :])
    return total.astype(bf16)


def feed_backward(layer, middle, gains, grad_low, weights, accs):
    gate_acc, up_acc, down_acc, gain_acc = (acc.at[layer] for acc in accs)
    big_ref, down_ref = weights.big_ref.at[layer], weights.down_ref.at[layer]
    width = middle.shape[1]
    hidden = down_ref.shape[0]
    inverse = inverse_rms(middle)
    feed = (middle * inverse * gains).astype(bf16)
    feed_t = feed.T
    feed_grad = jnp.zeros(middle.shape, f32)
    for at in range(0, hidden, CHUNK):
        gate_w = big_ref[:, 4 * width + at : 4 * width + at + CHUNK]
        up_w = big_ref[:, 4 * width + hidden + at : 4 * width + hidden + at + CHUNK]
        down_w = down_ref[at : at + CHUNK, :]
        gate = dot(feed, gate_w)
        up = dot(feed, up_w)
        act_grad = dot(grad_low, down_w, RIGHT_T)
        gated = sigmoid(gate)
        swish = gate * gated
        active = (swish * up).astype(bf16)
        gate_grad = (act_grad * up * (gated + swish * (1.0 - gated))).astype(bf16)
        up_grad = (act_grad * swish).astype(bf16)
        feed_grad = feed_grad + dot(gate_grad, gate_w, RIGHT_T) + dot(up_grad, up_w, RIGHT_T)
        gate_acc[:, at : at + CHUNK] += dot(feed_t, gate_grad)
        up_acc[:, at : at + CHUNK] += dot(feed_t, up_grad)
        down_acc[at : at + CHUNK, :] += dot(active, grad_low, LEFT_T)
    scaled = feed_grad * gains
    gain_acc[...] += jnp.sum(feed_grad * middle * inverse, axis=0, keepdims=True)
    return (
        grad_low.astype(f32)
        + inverse * scaled
        - middle * (inverse * inverse * inverse) * jnp.mean(scaled * middle, axis=1, keepdims=True)
    )


def attention_backward(layer, middle_grad, hidden, gains, block, weights, saved, grads_ref, accs):
    qkv_ref, prob_ref, inv_ref, mixed_ref = (ref.at[layer] for ref in saved)
    qkv_acc, out_acc, gain_acc, bias_acc = (acc.at[layer] for acc in accs)
    rows, width = hidden.shape
    pairs = width // LANES
    tiles = rows // TILE
    big_ref = weights.big_ref.at[layer]
    mix_grad = middle_grad.astype(bf16)
    att_grad = dot(mix_grad, big_ref[:, 3 * width : 4 * width], RIGHT_T).astype(bf16)
    lane = lane_index(rows)
    ones_four = jnp.where(lane < 4, 1.0, 0.0).astype(bf16)
    source = lax.broadcasted_iota(jnp.int32, (2 * LANES, LANES), 0) % LANES // HD
    target = lax.broadcasted_iota(jnp.int32, (2 * LANES, LANES), 1)
    gather = jnp.where((target // 2 == source) & (target < 4), 1.0, 0.0).astype(bf16)

    def operands(p):
        at = p * LANES
        q_pair = qkv_ref[:, at : at + LANES]
        k_turned = qkv_ref[:, width + at : width + at + LANES].T
        v_aug = jnp.concatenate(
            [qkv_ref[:, 2 * width + at : 2 * width + at + LANES], ones_four], axis=1
        )
        grad_pair = (att_grad[:, at : at + LANES].astype(f32) * inv_ref[:, at : at + LANES]).astype(
            bf16
        )
        product = grad_pair.astype(f32) * mixed_ref[:, at : at + LANES]
        high = product.astype(bf16)
        low = (product - high.astype(f32)).astype(bf16)
        inner = dot(jnp.concatenate([high, low], axis=1), gather)
        inner_high = inner.astype(bf16).astype(f32)
        tail = jnp.where(lane % 2 == 0, -inner_high, inner_high - inner)
        heads = []
        for half in range(2):
            grad_low = jnp.where(in_head(half, lane, False), grad_pair, 0.0).astype(bf16)
            tail_low = jnp.where(lane // 2 == half, tail, 0.0).astype(bf16)
            q_mine = jnp.where(in_head(half, lane, True), q_pair, 0.0).astype(bf16)
            k_mine = jnp.where(in_head(half, row_index(rows), True), k_turned, 0.0).astype(bf16)
            heads.append(
                (jnp.concatenate([grad_low, tail_low], axis=1), grad_low, q_mine, k_mine)
            )
        return v_aug, heads

    prepared = {}

    def prob_grad_of(p, half, t):
        if p not in prepared:
            prepared[p] = operands(p)
        v_aug, heads = prepared[p]
        return dot(v_aug, heads[half][0][t * TILE : (t + 1) * TILE, :], RIGHT_T)

    order = [(p, half, t) for p in range(pairs) for half in range(2) for t in range(tiles)]
    value_grad = key_grad = None
    query_grad = {}
    prob_grad = prob_grad_of(*order[0])
    for n, (p, half, t) in enumerate(order):
        following = prob_grad_of(*order[n + 1]) if n + 1 < len(order) else None
        head = 2 * p + half
        cols = slice(t * TILE, (t + 1) * TILE)
        at = p * LANES
        _, grad_low, q_mine, k_mine = prepared[p][1][half]
        prob = prob_ref[head, :, cols]
        score_grad = prob.astype(f32) * prob_grad
        bias_acc[head : head + 1, cols] += jnp.sum(
            score_grad * block.same_ref[:, cols], axis=0, keepdims=True
        )
        score_low = score_grad.astype(bf16)
        part_v = dot(prob, grad_low[cols, :])
        part_k = dot(score_low, q_mine[cols, :])
        part_q = dot(k_mine, score_low)
        value_grad = part_v if value_grad is None else value_grad + part_v
        key_grad = part_k if key_grad is None else key_grad + part_k
        query_grad[t] = part_q if half == 0 else query_grad[t] + part_q
        if half == 1:
            back = query_grad[t].T * HD**-0.5
            grads_ref[cols, at : at + LANES] = turn_back(
                back, block.cosine[cols, :], block.sine[cols, :]
            ).astype(bf16)
        if half == 1 and t == tiles - 1:
            grads_ref[:, width + at : width + at + LANES] = turn_back(
                key_grad, block.cosine, block.sine
            ).astype(bf16)
            grads_ref[:, 2 * width + at : 2 * width + at + LANES] = value_grad.astype(bf16)
            value_grad = key_grad = None
        prob_grad = following
    out_acc[...] += dot(mixed_ref[...].astype(bf16), mix_grad, LEFT_T)
    inverse = inverse_rms(hidden)
    normed = (hidden * inverse * gains).astype(bf16)
    normed_grad = dot(grads_ref[...], big_ref[:, : 3 * width], RIGHT_T)
    qkv_acc[...] += dot(normed, grads_ref[...], LEFT_T)
    scaled = normed_grad * gains
    gain_acc[...] += jnp.sum(normed_grad * hidden * inverse, axis=0, keepdims=True)
    return (
        middle_grad
        + inverse * scaled
        - hidden * (inverse * inverse * inverse) * jnp.mean(scaled * hidden, axis=1, keepdims=True)
    )


def column_tiles(acc_ref):
    return [acc_ref[:, at : at + LANES] for at in range(0, acc_ref.shape[1], LANES)]


class Packer:
    def __init__(self, stage_ref, sems, kept_refs, sent_refs):
        self.stage_ref, self.sems = stage_ref, sems
        self.kept_refs, self.sent_refs = kept_refs, sent_refs
        self.sent = []

    def copy(self, out_ref, slot, count):
        source = self.stage_ref.at[slot, pl.ds(0, count)]
        return pltpu.make_async_copy(source, out_ref, self.sems.at[slot])

    def send(self, keep, part, start, tiles):
        slot = len(self.sent) % 2
        if len(self.sent) >= 2:
            self.wait(2)
        at = 0
        for tile in tiles:
            self.stage_ref[slot, at : at + tile.shape[0], :] = tile.astype(bf16)
            at += tile.shape[0]
        where = pl.ds(start, at)

        @pl.when(keep)
        def _():
            self.copy(self.kept_refs[part].at[where], slot, at).start()

        @pl.when(jnp.logical_not(keep))
        def _():
            self.copy(self.sent_refs[part].at[where], slot, at).start()

        self.sent.append((self.kept_refs[part].at[where], slot, at))

    def wait(self, back):
        self.copy(*self.sent[-back]).wait()

    def finish(self):
        self.wait(2)
        self.wait(1)


def layers_body(
    sec_ref, bias_ref, x_ref, cotangent_ref, sid_ref, item_ref, var_ref, stats_ref, table_ref,
    gain_ref, *refs
):
    own_refs, other_refs, refs = refs[:7], refs[7:14], refs[14:]
    results_ref, grad_one_ref, grad_zero_ref, series_ref, small_ref = refs[:5]
    kept_refs, sent_refs, refs = refs[5:7], refs[7:9], refs[9:]
    big_ref, down_ref, refs = refs[0], refs[1], refs[2:]
    feed_accs, attention_accs, saved, refs = refs[:4], refs[4:8], refs[8:12], refs[12:]
    same_ref, grads_ref, hidden_ref, middle_ref, grad_ref, stage_ref, sems, stage_sems = refs

    i = pl.program_id(0)
    last = i == pl.num_programs(0) - 1
    m = pl.num_programs(0) * sec_ref[0] + i
    weights = Weights(sec_ref[0], own_refs, other_refs, big_ref, down_ref, sems)

    @pl.when(i == 0)
    def _():
        for acc in feed_accs + attention_accs:
            acc[...] = jnp.zeros_like(acc)

    x = x_ref[0].astype(f32)
    rows, width = x.shape
    var_row = var_ref[pl.ds(m, 1), :]
    var_col = column(var_row)
    sid_col = column(sid_ref[pl.ds(m, 1), :])
    pieces = stats_ref.shape[-1] // LANES

    time = lax.broadcasted_iota(jnp.int32, (rows, LANES), 0).astype(f32) - var_col
    cosine = sine = jnp.zeros((rows, LANES), f32)
    for at in range(0, rows, LANES):
        hot = jnp.where(time == (lane_index(rows) + at).astype(f32), 1.0, 0.0).astype(bf16)
        found = dot(hot, table_ref[at : at + LANES, :])
        cosine = cosine + found[:, :LANES] + found[:, LANES : 2 * LANES]
        sine = sine + found[:, 2 * LANES : 3 * LANES] + found[:, 3 * LANES :]
    block = Block(cosine, sine, column(item_ref[pl.ds(m, 1), :]), var_col, var_row, same_ref)

    _, centre, scaling = centre_and_scale(stats_ref[0], width)
    centre_rows = scale_rows = 0.0
    for piece in range(pieces):
        hits = series_hits(sid_col, piece)
        part = slice(piece * LANES, (piece + 1) * LANES)
        centre_rows = centre_rows + rows_of(hits, centre[:, part])
        scale_rows = scale_rows + rows_of(hits, scaling[:, part])
    hidden_ref[0] = (x - centre_rows) / scale_rows
    grad_ref[...] = cotangent_ref[0]

    def forward(layer, _):
        middle = attention_forward(
            layer, hidden_ref[layer], gain_ref[layer, 0:1, :], block, bias_ref, weights, saved
        )
        middle_ref[layer] = middle
        result = feed_forward(layer, middle, gain_ref[layer, 1:2, :], weights)
        results_ref[layer, 0] = result

        @pl.when(layer == 0)
        def _():
            hidden_ref[1] = result.astype(f32)

    def send(layer):
        packer = Packer(stage_ref, stage_sems, kept_refs, sent_refs)
        keep = sec_ref[0] == layer
        gate, up, down = (column_tiles(acc.at[layer]) for acc in feed_accs[:3])
        queries = column_tiles(attention_accs[0].at[layer])
        turned = [regroup(tile) for tile in queries[:6]]
        start = 0
        for tiles in (gate, up, down):
            packer.send(keep, 0, start, tiles)
            start += sum(tile.shape[0] for tile in tiles)
        packer.send(keep, 1, 0, turned)
        packer.send(keep, 1, width * 6, queries[6:] + column_tiles(attention_accs[1].at[layer]))
        packer.finish()

    def backward(step, _):
        layer = 1 - step
        middle_grad = feed_backward(
            layer, middle_ref[layer], gain_ref[layer, 1:2, :], grad_ref[...], weights, feed_accs
        )
        hidden_grad = attention_backward(
            layer, middle_grad, hidden_ref[layer], gain_ref[layer, 0:1, :], block, weights,
            saved, grads_ref, attention_accs,
        )
        grad_ref[...] = hidden_grad.astype(bf16)
        grad_zero_ref[0] = hidden_grad

        @pl.when(layer == 1)
        def _():
            grad_one_ref[0] = hidden_grad.astype(bf16)

        @pl.when(last)
        def _():
            send(layer)

    lax.fori_loop(0, 2, forward, None)
    lax.fori_loop(0, 2, backward, None)

    standard, hidden_grad = hidden_ref[0], grad_zero_ref[0]
    grad_rows = jnp.sum(hidden_grad, axis=1, keepdims=True)
    cross_rows = jnp.sum(hidden_grad * standard, axis=1, keepdims=True)
    standard_rows = jnp.sum(standard, axis=1, keepdims=True)
    series_ref[0] = jnp.zeros(series_ref.shape[1:], f32)
    for piece in range(pieces):
        hits = series_hits(sid_col, piece)
        part = slice(piece * LANES, (piece + 1) * LANES)
        series_ref[0, 0:1, part] = series_of(hits, grad_rows)
        series_ref[0, 1:2, part] = series_of(hits, cross_rows)
        series_ref[0, 2:3, part] = series_of(hits, standard_rows)

    @pl.when(last)
    def _():
        small_ref[...] = jnp.zeros_like(small_ref)
        for layer in range(2):
            base = 24 * layer
            for k in range(width // LANES):
                cols = slice(k * LANES, (k + 1) * LANES)
                small_ref[base + k : base + k + 1, :] = attention_accs[2][layer, :, cols]
                small_ref[base + 16 + k : base + 17 + k, :] = feed_accs[3][layer, :, cols]
            bias_sums = jnp.sum(attention_accs[3][layer], axis=1, keepdims=True)
            small_ref[base + 8 : base + 16, :] = jnp.broadcast_to(bias_sums, (8, LANES))


def final_body(
    sec_ref, x_ref, sid_ref, stats_ref, series_ref, own_first, own_second, other_grad,
    own_out, other_out, out_ref, grads_ref,
):
    i = pl.program_id(0)
    sec = sec_ref[0]
    own = (i // (pl.num_programs(0) // 2)) == sec
    grads_ref[0] = jnp.where(own, own_out[0], other_out[0])
    grad = jnp.where(
        own,
        jnp.where(sec == 0, own_first[0], own_second[0].astype(f32)),
        other_grad[0].astype(f32),
    )

    @pl.when(sec == 0)
    def _():
        x = x_ref[0].astype(f32)
        width = x.shape[1]
        entries, centre, scaling = centre_and_scale(stats_ref[0], width)
        sums = series_ref[0]
        cross = sums[1:2] * scaling
        spread_grad = -cross / (2.0 * scaling * scaling * scaling * entries)
        mean_grad = sums[0:1] / scaling + 2.0 * spread_grad * (sums[2:3] * scaling)
        tables = (centre, 1.0 / scaling, 2.0 * spread_grad, mean_grad / entries)
        sid_col = column(sid_ref[pl.ds(i, 1), :])
        looked = [0.0, 0.0, 0.0, 0.0]
        for piece in range(stats_ref.shape[-1] // LANES):
            hits = series_hits(sid_col, piece)
            part = slice(piece * LANES, (piece + 1) * LANES)
            for k in range(4):
                looked[k] = looked[k] + rows_of(hits, tables[k][:, part])
        out_ref[0] = grad * looked[1] + (x - looked[0]) * looked[2] - looked[3]

    @pl.when(sec != 0)
    def _():
        out_ref[0] = grad


class Halves:
    def __init__(self, own_ref, got_ref, bit):
        self.own_ref, self.got_ref, self.bit = own_ref, got_ref, bit
        self.half = own_ref.shape[0]
        self.at = 0

    def rows(self, start, count, low):
        own = self.own_ref[start : start + count, :]
        got = self.got_ref[start : start + count, :]
        return jnp.where((self.bit == 0) == low, own, got).astype(f32)

    def take(self, out_ref, col, count):
        done = 0
        while done < count:
            low = self.at < self.half
            room = min(count - done, (self.half if low else 2 * self.half) - self.at)
            out_ref[done : done + room, col : col + LANES] = self.rows(
                self.at - (0 if low else self.half), room, low
            )
            done += room
            self.at += room


def unpack_body(bit_ref, *refs):
    parts = [Halves(refs[2 * k], refs[2 * k + 1], bit_ref[k]) for k in range(2)]
    refs = refs[4:]
    count = len(refs) // 2
    outs, scratch, sems = refs[:count], refs[count : 2 * count], refs[2 * count]
    copies = []
    for out_ref, scratch_ref in zip(outs, scratch):
        for col in range(0, scratch_ref.shape[1], LANES):
            while parts[0].at == 2 * parts[0].half:
                parts.pop(0)
            parts[0].take(scratch_ref, col, scratch_ref.shape[0])
        copies.append(pltpu.make_async_copy(scratch_ref, out_ref, sems.at[len(copies)]))
        copies[-1].start()
    for copy in copies:
        copy.wait()


def unpack_small_body(sec_ref, small_ref, attention_gain_ref, feed_gain_ref, bias_ref):
    base = 24 * sec_ref[0]
    for k in range(attention_gain_ref.shape[1] // LANES):
        cols = slice(k * LANES, (k + 1) * LANES)
        attention_gain_ref[:, cols] = small_ref[pl.ds(base + k, 1), :]
        feed_gain_ref[:, cols] = small_ref[pl.ds(base + 16 + k, 1), :]
    same = small_ref[pl.ds(base + 8, 8), :].T[0:1, : bias_ref.shape[1]]
    bias_ref[0:1, :] = same
    bias_ref[1:2, :] = -same


def swapped(x):
    return lax.ppermute(x, "section", [(0, 1), (1, 0)])


def to_section(x, section):
    return lax.ppermute(x, "section", [(1 - section, section)])


def exchange_steps(count):
    bits = []
    step = 1
    while step < count:
        bits.append(step)
        step *= 2
    other = list(bits)
    for k in range(0, len(bits) - 1, 2):
        other[k], other[k + 1] = bits[k + 1], bits[k]
    return bits, other


def partner(x, by_first, by_second, count):
    pairs = [(i, i ^ by_first) for i in range(count)]
    pairs += [(count + i, count + (i ^ by_second)) for i in range(count)]
    return lax.ppermute(x, ("section", "dp"), pairs)


def place(steps, section, index):
    step = jnp.where(section == 0, *steps)
    return (index // step) % 2


def halve(parts, orders, k, section, index, count, *more):
    keeps, sends = [], []
    for current, order in zip(parts, orders):
        bit = place(order[k], section, index)
        half = current.shape[0] // 2
        keeps.append(lax.dynamic_slice_in_dim(current, bit * half, half, 0))
        sends.append(lax.dynamic_slice_in_dim(current, (1 - bit) * half, half, 0))
    sends, keeps, more = lax.optimization_barrier((sends, keeps, more))
    got = [partner(send, *order[k], count) for send, order in zip(sends, orders)]
    parts = [(a.astype(f32) + b.astype(f32)).astype(bf16) for a, b in zip(keeps, got)]
    return (parts, *more)


def double(parts, orders, k, section, index, count):
    parts = lax.optimization_barrier(parts)
    result = []
    for current, order in zip(parts, orders):
        bit = place(order[k], section, index)
        got = partner(current, *order[k], count)
        low = jnp.where(bit == 0, current, got)
        high = jnp.where(bit == 0, got, current)
        result.append(jnp.concatenate([low, high], axis=0))
    return result


HBM = pl.BlockSpec(memory_space=pl.ANY)
SCALARS = pl.BlockSpec(memory_space=pltpu.SMEM)


def whole_block(shape):
    return pl.BlockSpec(shape, lambda i, *_: (0,) * len(shape))


def by_step(shape):
    return pl.BlockSpec((1,) + shape, lambda i, *_: (i,) + (0,) * len(shape))


def by_batch(shape, own):
    return pl.BlockSpec((1,) + shape, lambda i, s: (own * s[0] + i,) + (0,) * len(shape))


def call(body, grid, in_specs, out_specs, out_shapes, scratch, flops, name):
    return pl.pallas_call(
        body,
        grid_spec=pltpu.PrefetchScalarGridSpec(
            num_scalar_prefetch=1,
            grid=(grid,),
            in_specs=in_specs,
            out_specs=out_specs,
            scratch_shapes=scratch,
        ),
        out_shape=out_shapes,
        compiler_params=pltpu.CompilerParams(vmem_limit_bytes=57 * 2**20),
        cost_estimate=pl.CostEstimate(flops=flops, bytes_accessed=2**22, transcendentals=0),
        name=name,
    )


def shape(*dims, dtype=f32):
    return jax.ShapeDtypeStruct(dims, dtype)


class Sizes:
    def __init__(self, inputs, heads, hidden, count):
        self.micro, self.rows, self.width = inputs.shape
        self.own = self.micro // 2
        self.heads, self.hidden, self.count = heads, hidden, count
        rows, width, own = self.rows, self.width, self.own
        self.stats = (8, -(-SER_DEV * count // LANES) * LANES)
        self.all_rows = whole_block((self.micro, rows))
        self.row = by_step((rows, width))
        self.row_batch = by_batch((rows, width), own)
        self.gain = whole_block((8, width))
        self.row_shape = shape(own, rows, width)
        self.low_shape = shape(own, rows, width, dtype=bf16)
        self.flops = 2 * rows * (4 * width * width + 3 * width * hidden) * own


def rotary_table(rows):
    lane = np.arange(LANES)
    frequency = np.float32(10000.0) ** (
        -(lane % (HD // 2)).astype(np.float32) * np.float32(2.0 / HD)
    )
    angle = np.arange(rows, dtype=np.float32)[:, None] * frequency[None, :].astype(np.float32)
    cosine = np.cos(angle.astype(np.float64))
    sine = np.sin(angle.astype(np.float64)) * np.where(lane < HD, -1.0, 1.0)
    parts = []
    for values in (cosine, sine):
        high = values.astype(jnp.bfloat16)
        parts += [high, (values - high.astype(np.float64)).astype(jnp.bfloat16)]
    return np.concatenate(parts, axis=1)


def series_stats(z, sec, inputs, series_id):
    return call(
        stats_body, z.own, [z.row_batch, z.all_rows], by_step(z.stats), shape(z.own, *z.stats),
        [], 10**7, "series_stats",
    )(sec, inputs, series_id)


def layers(z, sec, bias, inputs, cotangent, series_id, item, variate, stats, gains, own, other):
    table = rotary_table(z.rows)
    rows, width, hidden = z.rows, z.width, z.hidden
    parts = [
        shape(3 * width * hidden // LANES, LANES, dtype=bf16),
        shape(4 * width * width // LANES, LANES, dtype=bf16),
    ]

    def both(*dims, dtype=f32):
        return pltpu.VMEM((2,) + dims, dtype)

    return call(
        layers_body, z.own,
        [SCALARS, z.row_batch, z.row_batch, z.all_rows, z.all_rows, z.all_rows, by_step(z.stats),
         whole_block(table.shape), whole_block((2, 8, width))] + [HBM] * 14,
        [pl.BlockSpec((2, 1, rows, width), lambda i, *_: (0, i, 0, 0)), z.row, z.row,
         by_step(z.stats), whole_block((48, LANES))] + [HBM] * 4,
        [shape(2, z.own, rows, width, dtype=bf16), z.low_shape, z.row_shape,
         shape(z.own, *z.stats), shape(48, LANES)] + parts * 2,
        [both(width, 4 * width + 2 * hidden, dtype=bf16), both(hidden, width, dtype=bf16),
         both(width, hidden), both(width, hidden), both(hidden, width), both(1, width),
         both(width, 3 * width), both(width, width), both(1, width), both(8, rows),
         both(rows, 3 * width, dtype=bf16), both(z.heads, rows, rows, dtype=bf16),
         both(rows, width), both(rows, width),
         pltpu.VMEM((rows, rows), f32), pltpu.VMEM((rows, 3 * width), bf16),
         both(rows, width), both(rows, width), pltpu.VMEM((rows, width), bf16),
         both(8 * width, LANES, dtype=bf16),
         pltpu.SemaphoreType.DMA((2, 7)), pltpu.SemaphoreType.DMA((2,))],
        12 * z.flops, "layers",
    )(sec, bias, inputs, cotangent, series_id, item, variate, stats, jnp.asarray(table),
      gains, *own, *other)


def final(z, sec, inputs, series_id, stats, series, own_first, own_second, other_grad,
          own_out, other_out):
    own_count = z.own

    def own_step(i, s):
        return (jnp.clip(i - own_count * s[0], 0, own_count - 1), 0, 0)

    def other_step(i, s):
        return (jnp.clip(i - own_count * (1 - s[0]), 0, own_count - 1), 0, 0)

    own_spec = pl.BlockSpec((1, z.rows, z.width), own_step)
    other_spec = pl.BlockSpec((1, z.rows, z.width), other_step)
    return call(
        final_body, z.micro,
        [z.row, z.all_rows, by_step(z.stats), by_step(z.stats), own_spec, own_spec,
         other_spec, own_spec, other_spec],
        [z.row, z.row],
        [shape(z.micro, z.rows, z.width), shape(z.micro, z.rows, z.width, dtype=bf16)],
        [], 10**10, "final",
    )(sec, inputs, series_id, stats, series, own_first, own_second, other_grad, own_out, other_out)


def per_device(
    inputs,
    series_id,
    item_offset,
    variate_offset,
    cotangent,
    attention_gain,
    query_weight,
    key_weight,
    value_weight,
    out_weight,
    variate_bias,
    feed_gain,
    gate_weight,
    up_weight,
    down_weight,
):
    section = lax.axis_index("section")
    index = lax.axis_index("dp")
    count = lax.axis_size("dp")
    on_first = section == 0
    sec = section.astype(jnp.int32).reshape(1)
    heads = variate_bias.shape[1]
    z = Sizes(inputs, heads, down_weight.shape[1], count)
    width = z.width

    stats = series_stats(z, sec, inputs, series_id)
    for step in exchange_steps(count)[0]:
        stats = merge_stats(stats, partner(stats, step, step, count), width)

    own_small = jnp.concatenate(
        [
            attention_gain,
            feed_gain,
            jnp.pad(variate_bias.reshape(1, 2 * heads), ((0, 0), (0, width - 2 * heads))),
        ],
        axis=0,
    ).astype(f32)
    own_small = jnp.pad(own_small, ((0, 5), (0, 0)))
    other_small = swapped(own_small)
    own = tuple(
        w[0]
        for w in (
            query_weight, key_weight, value_weight, out_weight, gate_weight, up_weight, down_weight
        )
    )
    other = tuple(swapped(w) for w in own)
    gains = (
        jnp.where(on_first, own_small, other_small),
        jnp.where(on_first, other_small, own_small),
    )
    gains = jnp.stack(gains)
    bias = gains[:, 2, : 2 * heads].reshape(-1)

    results, grad_one, standard_grad, series_sums, small_sums, *packs = layers(
        z, sec, bias, inputs, cotangent, series_id, item_offset, variate_offset, stats, gains,
        own, other,
    )
    result_one, result_two = results[0], results[1]

    parts = [
        (k.astype(f32) + swapped(t).astype(f32)).astype(bf16)
        for k, t in zip(packs[:2], packs[2:])
    ]
    bits, turned = exchange_steps(count)
    near = list(zip(bits, turned))
    orders = (near, near[2:] + near[:2])
    rounds = len(bits)

    series_rows = z.own * z.stats[0] * z.stats[1] // LANES
    small = jnp.concatenate(
        [series_sums.reshape(-1, LANES), small_sums], axis=0
    )
    for k in range(rounds):
        parts, small = halve(parts, orders, k, section, index, count, small)
        small = small + partner(small, bits[rounds - 1 - k], bits[rounds - 1 - k], count)
    other_sums = swapped(small)
    mine = small[:series_rows].reshape((z.own,) + z.stats)
    theirs = other_sums[:series_rows].reshape((z.own,) + z.stats)
    series_all = jnp.where(
        on_first, jnp.concatenate([mine, theirs]), jnp.concatenate([theirs, mine])
    )
    small = small[series_rows:] + other_sums[series_rows:]
    other_stats = swapped(stats)
    stats_all = jnp.where(
        on_first, jnp.concatenate([stats, other_stats]), jnp.concatenate([other_stats, stats])
    )

    own_out = jnp.where(on_first, result_one, result_two)
    other_out = swapped(jnp.where(on_first, result_two, result_one))
    other_grad = swapped(jnp.where(on_first, grad_one, standard_grad.astype(bf16)))

    for k in reversed(range(1, rounds)):
        parts = double(parts, orders, k, section, index, count)
    sec_late, parts = lax.optimization_barrier((sec, parts))
    input_grads, section_output = final(
        z, sec_late, inputs, series_id, stats_all, series_all, standard_grad, grad_one, other_grad,
        own_out, other_out,
    )
    others = [partner(p, *o[0], count) for p, o in zip(parts, orders)]
    parts, input_grads, section_output = lax.optimization_barrier(
        (parts, input_grads, section_output)
    )
    last_bits = jnp.stack([place(o[0], section, index) for o in orders]).astype(jnp.int32)

    vmem = pl.BlockSpec(memory_space=pltpu.VMEM)

    large = [shape(width, z.hidden)] * 2 + [shape(z.hidden, width)] + [shape(width, width)] * 4
    grad_gate, grad_up, grad_down, grad_query, grad_key, grad_value, grad_out = pl.pallas_call(
        unpack_body,
        in_specs=[SCALARS] + [vmem] * 4,
        out_specs=[HBM] * 7,
        out_shape=large,
        scratch_shapes=[pltpu.VMEM(s.shape, f32) for s in large] + [pltpu.SemaphoreType.DMA((7,))],
        compiler_params=pltpu.CompilerParams(vmem_limit_bytes=57 * 2**20),
        name="unpack",
    )(last_bits, *(array for pair in zip(parts, others) for array in pair))
    grad_attention_gain, grad_feed_gain, grad_bias = pl.pallas_call(
        unpack_small_body,
        in_specs=[SCALARS, vmem],
        out_shape=[shape(1, width)] * 2 + [shape(2, heads)],
        name="unpack_small",
    )(sec, small)
    return (
        section_output[None],
        input_grads[None],
        grad_attention_gain,
        grad_query[None],
        grad_key[None],
        grad_value[None],
        grad_out[None],
        grad_bias.T[None],
        grad_feed_gain,
        grad_gate[None],
        grad_up[None],
        grad_down[None],
    )


def solution(mesh):
    placed = (
        P(None, "dp", None),
        P(None, "dp"),
        P(None, "dp"),
        P(None, "dp"),
        P(None, "dp", None),
        P("section", None),
        P("section", None, None),
        P("section", None, None),
        P("section", None, None),
        P("section", None, None),
        P("section", None, None),
        P("section", None),
        P("section", None, None),
        P("section", None, None),
        P("section", None, None),
    )
    return jax.shard_map(
        per_device,
        mesh=mesh,
        in_specs=placed,
        out_specs=(
            P("section", None, "dp", None),
            P("section", None, "dp", None),
            P("section", None),
            P("section", None, None),
            P("section", None, None),
            P("section", None, None),
            P("section", None, None),
            P("section", None, None),
            P("section", None),
            P("section", None, None),
            P("section", None, None),
            P("section", None, None),
        ),
        check_vma=False,
    )
```

```python
import jax
import jax.numpy as jnp
import numpy as np
from jax import lax
from jax.experimental import pallas as pl
from jax.experimental.pallas import tpu as pltpu
from jax.sharding import PartitionSpec as P

HD = 64
BLOCK = 512
SER_DEV = 4
LANES = 128
CHUNK = 512
TILE = 256

norm_epsilon = 1e-05
scale_epsilon = 1e-05
masked_score = -1e30

f32 = jnp.float32
bf16 = jnp.bfloat16

AS_IS = (((1,), (0,)), ((), ()))
RIGHT_T = (((1,), (1,)), ((), ()))
LEFT_T = (((0,), (0,)), ((), ()))


def dot(left, right, dims=AS_IS):
    return lax.dot_general(left, right, dims, preferred_element_type=f32)


def column(row):
    return jnp.broadcast_to(row.astype(f32), (LANES, row.shape[1])).T


def lane_index(rows):
    return lax.broadcasted_iota(jnp.int32, (rows, LANES), 1)


def regroup(x):
    group = lane_index(x.shape[0]) // (HD // 2)
    return jnp.where(
        group == 1,
        pltpu.roll(x, LANES - HD // 2, 1),
        jnp.where(group == 2, pltpu.roll(x, HD // 2, 1), x),
    )


def turn(x, cosine, sine):
    return x * cosine + pltpu.roll(x, LANES // 2, 1) * sine


def turn_back(x, cosine, sine):
    return x * cosine - pltpu.roll(x, LANES // 2, 1) * sine


def inverse_rms(x):
    return lax.rsqrt(jnp.mean(x * x, axis=1, keepdims=True) + norm_epsilon)


def series_hits(sid_col, piece):
    return sid_col == (lane_index(sid_col.shape[0]) + piece * LANES).astype(f32)


def rows_of(hits, per_series):
    return jnp.sum(jnp.where(hits, per_series, 0.0), axis=1, keepdims=True)


def series_of(hits, per_row):
    return jnp.sum(jnp.where(hits, per_row, 0.0), axis=0, keepdims=True)


def stats_body(sec_ref, x_ref, sid_ref, out_ref):
    own, _, width = x_ref.shape
    pieces = out_ref.shape[-1] // LANES
    out_ref[...] = jnp.zeros_like(out_ref)
    for i in range(own):
        x = x_ref[i].astype(f32)
        sid_col = column(sid_ref[pl.ds(own * sec_ref[0] + i, 1), :])
        totals = jnp.sum(x, axis=1, keepdims=True)
        centre = jnp.zeros_like(totals)
        for piece in range(pieces):
            hits = series_hits(sid_col, piece)
            count = series_of(hits, 1.0)
            total = series_of(hits, totals)
            centre = centre + rows_of(hits, total / (jnp.maximum(count, 1.0) * width))
            out_ref[i, 0:1, piece * LANES : (piece + 1) * LANES] = count
            out_ref[i, 1:2, piece * LANES : (piece + 1) * LANES] = total
        centred = x - centre
        squares = jnp.sum(centred * centred, axis=1, keepdims=True)
        for piece in range(pieces):
            hits = series_hits(sid_col, piece)
            out_ref[i, 2:3, piece * LANES : (piece + 1) * LANES] = series_of(hits, squares)


def merge_stats(here, there, width):
    count_a, total_a, spread_a = here[:, 0:1], here[:, 1:2], here[:, 2:3]
    count_b, total_b, spread_b = there[:, 0:1], there[:, 1:2], there[:, 2:3]
    count = count_a + count_b
    gap = total_a / (jnp.maximum(count_a, 1.0) * width) - total_b / (
        jnp.maximum(count_b, 1.0) * width
    )
    weight = count_a * count_b * width / jnp.maximum(count, 1.0)
    row = lax.broadcasted_iota(jnp.int32, here.shape, 1)
    return jnp.where(
        row == 0,
        count,
        jnp.where(row == 1, total_a + total_b, spread_a + spread_b + gap * gap * weight),
    )


def centre_and_scale(stats, width):
    entries = jnp.maximum(stats[0:1], 1.0) * width
    centre = stats[1:2] / entries
    scaling = jnp.sqrt(stats[2:3] / entries + scale_epsilon)
    return entries, centre, scaling


class Weights:
    def __init__(self, section, own_refs, other_refs, big_ref, down_ref, sems):
        self.first_step = pl.program_id(0) == 0
        self.big_ref, self.down_ref = big_ref, down_ref
        self.own_refs, self.sems = own_refs, sems

        @pl.when(self.first_step)
        def _():
            for layer_of, refs in ((section, own_refs), (1 - section, other_refs)):
                for k, ref in enumerate(refs):
                    pltpu.make_async_copy(ref, self.target(layer_of, k), sems.at[layer_of, k]).start()

    def target(self, layer, k):
        if k == 6:
            return self.down_ref.at[layer]
        at = sum(ref.shape[1] for ref in self.own_refs[:k])
        return self.big_ref.at[layer, :, pl.ds(at, self.own_refs[k].shape[1])]

    def wait_here(self, layer, numbers):
        for k in numbers:
            pltpu.make_async_copy(
                self.own_refs[k], self.target(layer, k), self.sems.at[layer, k]
            ).wait()

    def wait_attention(self, layer):
        width = self.big_ref.shape[1]

        @pl.when(self.first_step)
        def _():
            self.wait_here(layer, (0, 1, 2, 3))
            for at in range(0, 2 * width, LANES):
                tile = self.big_ref[layer, :, at : at + LANES].astype(f32)
                self.big_ref[layer, :, at : at + LANES] = regroup(tile).astype(bf16)

    def wait_feed(self, layer):
        @pl.when(self.first_step)
        def _():
            self.wait_here(layer, (4, 5, 6))


def sigmoid(x):
    return 0.5 * jnp.tanh(0.5 * x) + 0.5


def in_head(half, lanes, grouped):
    if grouped:
        return (lanes % HD) // (HD // 2) == half
    return lanes // HD == half


def row_index(rows):
    return lax.broadcasted_iota(jnp.int32, (LANES, rows), 0)


class Block:
    def __init__(self, cosine, sine, item_col, var_col, var_row, same_ref):
        rows = cosine.shape[0]
        self.cosine, self.sine, self.same_ref = cosine, sine, same_ref
        row = var_row.astype(f32)
        for at in range(0, rows, LANES):
            same_ref[:, at : at + LANES] = jnp.where(var_col == row[:, at : at + LANES], 1.0, 0.0)
        lane = lane_index(rows)
        second = jnp.where(item_col > 0.0, 1.0, 0.0)
        self.item_q = jnp.where(
            lane == 0, second, jnp.where(lane == 1, 1.0 - second, 0.0)
        ).astype(bf16)
        self.item_k = jnp.where(
            lane == 0,
            (1.0 - second) * masked_score,
            jnp.where(lane == 1, second * masked_score, 0.0),
        ).astype(bf16)


def attention_forward(layer, hidden, gains, block, bias, weights, saved):
    qkv_ref, prob_ref, inv_ref, mixed_ref = (ref.at[layer] for ref in saved)
    rows, width = hidden.shape
    pairs = width // LANES
    tiles = rows // TILE
    big_ref = weights.big_ref.at[layer]
    normed = (hidden * inverse_rms(hidden) * gains).astype(bf16)
    weights.wait_attention(layer)
    lane = lane_index(rows)
    first_rows = row_index(rows) < HD
    extra = lax.broadcasted_iota(jnp.int32, (16, rows), 0)

    projected = dot(normed, big_ref[:, : 3 * width])

    def project(p):
        at = p * LANES
        q = turn(projected[:, at : at + LANES], block.cosine, block.sine)
        k = turn(projected[:, width + at : width + at + LANES], block.cosine, block.sine)
        v = projected[:, 2 * width + at : 2 * width + at + LANES]
        qkv_ref[:, at : at + LANES] = (q * HD**-0.5).astype(bf16)
        qkv_ref[:, width + at : width + at + LANES] = k.astype(bf16)
        qkv_ref[:, 2 * width + at : 2 * width + at + LANES] = v.astype(bf16)

    def operands(p):
        at = p * LANES
        q_pair = qkv_ref[:, at : at + LANES]
        k_aug = jnp.concatenate([qkv_ref[:, width + at : width + at + LANES], block.item_k], axis=1)
        v_turned = qkv_ref[:, 2 * width + at : 2 * width + at + LANES].T
        heads = []
        for half in range(2):
            q_aug = jnp.concatenate(
                [jnp.where(in_head(half, lane, True), q_pair, 0.0).astype(bf16), block.item_q],
                axis=1,
            )
            own_rows = first_rows if half == 0 else jnp.logical_not(first_rows)
            v_aug = jnp.concatenate(
                [
                    jnp.where(own_rows, v_turned, 0.0).astype(bf16),
                    jnp.where(extra == half, 1.0, 0.0).astype(bf16),
                ],
                axis=0,
            )
            heads.append((q_aug, v_aug))
        return k_aug, heads

    prepared = {}

    def scores_of(p, half, t):
        if p not in prepared:
            project(p)
            prepared[p] = operands(p)
        k_aug, heads = prepared[p]
        return dot(k_aug, heads[half][0][t * TILE : (t + 1) * TILE, :], RIGHT_T)

    order = [(p, half, t) for p in range(pairs) for half in range(2) for t in range(tiles)]
    attended = {}
    scores = scores_of(*order[0])
    for n, (p, half, t) in enumerate(order):
        following = scores_of(*order[n + 1]) if n + 1 < len(order) else None
        head = 2 * p + half
        cols = slice(t * TILE, (t + 1) * TILE)
        gap = bias[0:1, 2 * head : 2 * head + 1] - bias[0:1, 2 * head + 1 : 2 * head + 2]
        biased = scores + block.same_ref[:, cols] * gap
        peak = jnp.max(biased, axis=0, keepdims=True)
        prob = jnp.exp(biased - peak).astype(bf16)
        prob_ref[head, :, cols] = prob
        part = dot(prepared[p][1][half][1], prob)
        attended[p, t] = part if half == 0 else attended[p, t] + part
        if half == 1:
            sums = attended.pop((p, t))
            own_rows = row_index(TILE) < HD
            inv = jnp.where(
                own_rows, 1.0 / sums[LANES : LANES + 1], 1.0 / sums[LANES + 1 : LANES + 2]
            )
            inv_ref[cols, p * LANES : (p + 1) * LANES] = inv.T
            mixed_ref[cols, p * LANES : (p + 1) * LANES] = (sums[:LANES] * inv).T
        scores = following
    return hidden + dot(mixed_ref[...].astype(bf16), big_ref[:, 3 * width : 4 * width])


def feed_forward(layer, middle, gains, weights):
    big_ref, down_ref = weights.big_ref.at[layer], weights.down_ref.at[layer]
    width = middle.shape[1]
    hidden = down_ref.shape[0]
    feed = (middle * inverse_rms(middle) * gains).astype(bf16)
    total = middle
    for at in range(0, hidden, CHUNK):
        gate = dot(feed, big_ref[:, 4 * width + at : 4 * width + at + CHUNK])
        up = dot(feed, big_ref[:, 4 * width + hidden + at : 4 * width + hidden + at + CHUNK])
        active = (gate * sigmoid(gate) * up).astype(bf16)
        total = total + dot(active, down_ref[at : at + CHUNK, :])
    return total.astype(bf16)


def feed_backward(layer, middle, gains, grad_low, weights, accs, active_ref):
    gate_acc, up_acc, down_acc, gain_acc = (acc.at[layer] for acc in accs)
    big_ref, down_ref = weights.big_ref.at[layer], weights.down_ref.at[layer]
    width = middle.shape[1]
    hidden = down_ref.shape[0]
    inverse = inverse_rms(middle)
    feed = (middle * inverse * gains).astype(bf16)
    feed_t = feed.T
    feed_grad = jnp.zeros(middle.shape, f32)
    for at in range(0, hidden, CHUNK):
        gate_w = big_ref[:, 4 * width + at : 4 * width + at + CHUNK]
        up_w = big_ref[:, 4 * width + hidden + at : 4 * width + hidden + at + CHUNK]
        down_w = down_ref[at : at + CHUNK, :]
        gate = dot(feed, gate_w)
        up = dot(feed, up_w)
        act_grad = dot(grad_low, down_w, RIGHT_T)
        gated = sigmoid(gate)
        swish = gate * gated
        active = (swish * up).astype(bf16)
        active_ref[:, at : at + CHUNK] = active
        gate_grad = (act_grad * up * (gated + swish * (1.0 - gated))).astype(bf16)
        up_grad = (act_grad * swish).astype(bf16)
        feed_grad = feed_grad + dot(gate_grad, gate_w, RIGHT_T) + dot(up_grad, up_w, RIGHT_T)
        gate_acc[:, at : at + CHUNK] += dot(feed_t, gate_grad)
        up_acc[:, at : at + CHUNK] += dot(feed_t, up_grad)
        down_acc[at : at + CHUNK, :] += dot(active, grad_low, LEFT_T)
    scaled = feed_grad * gains
    gain_acc[...] += jnp.sum(feed_grad * middle * inverse, axis=0, keepdims=True)
    return (
        grad_low.astype(f32)
        + inverse * scaled
        - middle * (inverse * inverse * inverse) * jnp.mean(scaled * middle, axis=1, keepdims=True)
    )


def attention_backward(layer, middle_grad, hidden, gains, block, weights, saved, grads_ref, accs):
    qkv_ref, prob_ref, inv_ref, mixed_ref = (ref.at[layer] for ref in saved)
    qkv_acc, out_acc, gain_acc, bias_acc = (acc.at[layer] for acc in accs)
    rows, width = hidden.shape
    pairs = width // LANES
    tiles = rows // TILE
    big_ref = weights.big_ref.at[layer]
    mix_grad = middle_grad.astype(bf16)
    att_grad = dot(mix_grad, big_ref[:, 3 * width : 4 * width], RIGHT_T).astype(bf16)
    lane = lane_index(rows)
    ones_four = jnp.where(lane < 4, 1.0, 0.0).astype(bf16)
    source = lax.broadcasted_iota(jnp.int32, (2 * LANES, LANES), 0) % LANES // HD
    target = lax.broadcasted_iota(jnp.int32, (2 * LANES, LANES), 1)
    gather = jnp.where((target // 2 == source) & (target < 4), 1.0, 0.0).astype(bf16)

    def operands(p):
        at = p * LANES
        q_pair = qkv_ref[:, at : at + LANES]
        k_turned = qkv_ref[:, width + at : width + at + LANES].T
        v_aug = jnp.concatenate(
            [qkv_ref[:, 2 * width + at : 2 * width + at + LANES], ones_four], axis=1
        )
        grad_pair = (att_grad[:, at : at + LANES].astype(f32) * inv_ref[:, at : at + LANES]).astype(
            bf16
        )
        product = grad_pair.astype(f32) * mixed_ref[:, at : at + LANES]
        high = product.astype(bf16)
        low = (product - high.astype(f32)).astype(bf16)
        inner = dot(jnp.concatenate([high, low], axis=1), gather)
        inner_high = inner.astype(bf16).astype(f32)
        tail = jnp.where(lane % 2 == 0, -inner_high, inner_high - inner)
        heads = []
        for half in range(2):
            grad_low = jnp.where(in_head(half, lane, False), grad_pair, 0.0).astype(bf16)
            tail_low = jnp.where(lane // 2 == half, tail, 0.0).astype(bf16)
            q_mine = jnp.where(in_head(half, lane, True), q_pair, 0.0).astype(bf16)
            low = half * (HD // 2)
            k_mine = jnp.concatenate(
                [k_turned[low : low + HD // 2], k_turned[HD + low : HD + low + HD // 2]], axis=0
            )
            heads.append(
                (jnp.concatenate([grad_low, tail_low], axis=1), grad_low, q_mine, k_mine)
            )
        return v_aug, heads

    prepared = {}

    def prob_grad_of(p, half, t):
        if p not in prepared:
            prepared[p] = operands(p)
        v_aug, heads = prepared[p]
        return dot(v_aug, heads[half][0][t * TILE : (t + 1) * TILE, :], RIGHT_T)

    order = [(p, half, t) for p in range(pairs) for half in range(2) for t in range(tiles)]
    value_grad = key_grad = None
    query_grad = {}
    prob_grad = prob_grad_of(*order[0])
    for n, (p, half, t) in enumerate(order):
        following = prob_grad_of(*order[n + 1]) if n + 1 < len(order) else None
        head = 2 * p + half
        cols = slice(t * TILE, (t + 1) * TILE)
        at = p * LANES
        _, grad_low, q_mine, k_mine = prepared[p][1][half]
        prob = prob_ref[head, :, cols]
        score_grad = prob.astype(f32) * prob_grad
        bias_acc[head : head + 1, cols] += jnp.sum(
            score_grad * block.same_ref[:, cols], axis=0, keepdims=True
        )
        score_low = score_grad.astype(bf16)
        part_v = dot(prob, grad_low[cols, :])
        part_k = dot(score_low, q_mine[cols, :])
        part_q = dot(k_mine, score_low)
        value_grad = part_v if value_grad is None else value_grad + part_v
        key_grad = part_k if key_grad is None else key_grad + part_k
        query_grad[t, half] = part_q
        if half == 1:
            one, two = query_grad.pop((t, 0)), query_grad.pop((t, 1))
            mid = HD // 2
            back = jnp.concatenate([one[:mid], two[:mid], one[mid:], two[mid:]], axis=0).T * HD**-0.5
            grads_ref[cols, at : at + LANES] = turn_back(
                back, block.cosine[cols, :], block.sine[cols, :]
            ).astype(bf16)
        if half == 1 and t == tiles - 1:
            grads_ref[:, width + at : width + at + LANES] = turn_back(
                key_grad, block.cosine, block.sine
            ).astype(bf16)
            grads_ref[:, 2 * width + at : 2 * width + at + LANES] = value_grad.astype(bf16)
            value_grad = key_grad = None
        prob_grad = following
    out_acc[...] += dot(mixed_ref[...].astype(bf16), mix_grad, LEFT_T)
    inverse = inverse_rms(hidden)
    normed = (hidden * inverse * gains).astype(bf16)
    normed_grad = dot(grads_ref[...], big_ref[:, : 3 * width], RIGHT_T)
    qkv_acc[...] += dot(normed, grads_ref[...], LEFT_T)
    scaled = normed_grad * gains
    gain_acc[...] += jnp.sum(normed_grad * hidden * inverse, axis=0, keepdims=True)
    return (
        middle_grad
        + inverse * scaled
        - hidden * (inverse * inverse * inverse) * jnp.mean(scaled * hidden, axis=1, keepdims=True)
    )


def column_tiles(acc_ref):
    return [acc_ref[:, at : at + LANES] for at in range(0, acc_ref.shape[1], LANES)]


class Packer:
    def __init__(self, stage_ref, sems, kept_refs, sent_refs):
        self.stage_ref, self.sems = stage_ref, sems
        self.kept_refs, self.sent_refs = kept_refs, sent_refs
        self.sent = []

    def copy(self, out_ref, slot, count):
        source = self.stage_ref.at[slot, pl.ds(0, count)]
        return pltpu.make_async_copy(source, out_ref, self.sems.at[slot])

    def send(self, keep, part, start, tiles):
        slot = len(self.sent) % 2
        if len(self.sent) >= 2:
            self.wait(2)
        at = 0
        for tile in tiles:
            self.stage_ref[slot, at : at + tile.shape[0], :] = tile.astype(bf16)
            at += tile.shape[0]
        where = pl.ds(start, at)

        @pl.when(keep)
        def _():
            self.copy(self.kept_refs[part].at[where], slot, at).start()

        @pl.when(jnp.logical_not(keep))
        def _():
            self.copy(self.sent_refs[part].at[where], slot, at).start()

        self.sent.append((self.kept_refs[part].at[where], slot, at))

    def wait(self, back):
        self.copy(*self.sent[-back]).wait()

    def finish(self):
        self.wait(2)
        self.wait(1)


def layers_body(
    sec_ref, x_ref, cotangent_ref, sid_ref, item_ref, var_ref, stats_ref, table_ref,
    own_small_ref, other_small_ref, *refs
):
    own_refs, other_refs, refs = refs[:7], refs[7:14], refs[14:]
    results_ref, grad_one_ref, grad_zero_ref, series_ref, small_ref = refs[:5]
    kept_refs, sent_refs, refs = refs[5:7], refs[7:9], refs[9:]
    big_ref, down_ref, refs = refs[0], refs[1], refs[2:]
    feed_accs, attention_accs, saved, refs = refs[:4], refs[4:8], refs[8:12], refs[12:]
    same_ref, grads_ref, hidden_ref, middle_ref, grad_ref, active_ref, stage_ref, *refs = refs
    sems, stage_sems = refs

    i = pl.program_id(0)
    last = i == pl.num_programs(0) - 1
    m = pl.num_programs(0) * sec_ref[0] + i
    weights = Weights(sec_ref[0], own_refs, other_refs, big_ref, down_ref, sems)

    @pl.when(i == 0)
    def _():
        for acc in feed_accs + attention_accs:
            acc[...] = jnp.zeros_like(acc)

    x = x_ref[0].astype(f32)
    rows, width = x.shape
    var_row = var_ref[pl.ds(m, 1), :]
    var_col = column(var_row)
    sid_col = column(sid_ref[pl.ds(m, 1), :])
    pieces = stats_ref.shape[-1] // LANES

    time = lax.broadcasted_iota(jnp.int32, (rows, LANES), 0).astype(f32) - var_col
    cosine = sine = jnp.zeros((rows, LANES), f32)
    for at in range(0, rows, LANES):
        hot = jnp.where(time == (lane_index(rows) + at).astype(f32), 1.0, 0.0).astype(bf16)
        found = dot(hot, table_ref[at : at + LANES, :])
        cosine = cosine + found[:, :LANES] + found[:, LANES : 2 * LANES]
        sine = sine + found[:, 2 * LANES : 3 * LANES] + found[:, 3 * LANES :]
    block = Block(cosine, sine, column(item_ref[pl.ds(m, 1), :]), var_col, var_row, same_ref)

    _, centre, scaling = centre_and_scale(stats_ref[0], width)
    centre_rows = scale_rows = 0.0
    for piece in range(pieces):
        hits = series_hits(sid_col, piece)
        part = slice(piece * LANES, (piece + 1) * LANES)
        centre_rows = centre_rows + rows_of(hits, centre[:, part])
        scale_rows = scale_rows + rows_of(hits, scaling[:, part])
    hidden_ref[0] = (x - centre_rows) / scale_rows
    grad_ref[...] = cotangent_ref[0]

    def small_row(layer, k):
        return jnp.where(
            sec_ref[0] == layer, own_small_ref[k : k + 1, :], other_small_ref[k : k + 1, :]
        )

    def forward(layer, _):
        middle = attention_forward(
            layer, hidden_ref[layer], small_row(layer, 0), block, small_row(layer, 2), weights,
            saved,
        )
        middle_ref[layer] = middle
        weights.wait_feed(layer)

        @pl.when(layer == 0)
        def _():
            result = feed_forward(layer, middle_ref[0], small_row(layer, 1), weights)
            results_ref[0, 0] = result
            hidden_ref[1] = result.astype(f32)

    def send(layer):
        packer = Packer(stage_ref, stage_sems, kept_refs, sent_refs)
        keep = sec_ref[0] == layer
        gate, up, down = (column_tiles(acc.at[layer]) for acc in feed_accs[:3])
        queries = column_tiles(attention_accs[0].at[layer])
        turned = [regroup(tile) for tile in queries[:6]]
        start = 0
        for tiles in (gate, up, down):
            packer.send(keep, 0, start, tiles)
            start += sum(tile.shape[0] for tile in tiles)
        packer.send(keep, 1, 0, turned)
        packer.send(keep, 1, width * 6, queries[6:] + column_tiles(attention_accs[1].at[layer]))
        packer.finish()

    def backward(step, _):
        layer = 1 - step
        middle_grad = feed_backward(
            layer, middle_ref[layer], small_row(layer, 1), grad_ref[...], weights, feed_accs,
            active_ref,
        )

        @pl.when(layer == 1)
        def _():
            total = middle_ref[1] + dot(active_ref[...], weights.down_ref[1])
            results_ref[1, 0] = total.astype(bf16)

        hidden_grad = attention_backward(
            layer, middle_grad, hidden_ref[layer], small_row(layer, 0), block, weights,
            saved, grads_ref, attention_accs,
        )
        grad_ref[...] = hidden_grad.astype(bf16)
        grad_zero_ref[0] = hidden_grad

        @pl.when(layer == 1)
        def _():
            grad_one_ref[0] = hidden_grad.astype(bf16)

        @pl.when(last)
        def _():
            send(layer)

    lax.fori_loop(0, 2, forward, None)
    lax.fori_loop(0, 2, backward, None)

    standard, hidden_grad = hidden_ref[0], grad_zero_ref[0]
    grad_rows = jnp.sum(hidden_grad, axis=1, keepdims=True)
    cross_rows = jnp.sum(hidden_grad * standard, axis=1, keepdims=True)
    standard_rows = jnp.sum(standard, axis=1, keepdims=True)
    series_ref[0] = jnp.zeros(series_ref.shape[1:], f32)
    for piece in range(pieces):
        hits = series_hits(sid_col, piece)
        part = slice(piece * LANES, (piece + 1) * LANES)
        series_ref[0, 0:1, part] = series_of(hits, grad_rows)
        series_ref[0, 1:2, part] = series_of(hits, cross_rows)
        series_ref[0, 2:3, part] = series_of(hits, standard_rows)

    @pl.when(last)
    def _():
        small_ref[...] = jnp.zeros_like(small_ref)
        for layer in range(2):
            base = 24 * layer
            for k in range(width // LANES):
                cols = slice(k * LANES, (k + 1) * LANES)
                small_ref[base + k : base + k + 1, :] = attention_accs[2][layer, :, cols]
                small_ref[base + 16 + k : base + 17 + k, :] = feed_accs[3][layer, :, cols]
            bias_sums = jnp.sum(attention_accs[3][layer], axis=1, keepdims=True)
            small_ref[base + 8 : base + 16, :] = jnp.broadcast_to(bias_sums, (8, LANES))


def final_body(
    sec_ref, x_ref, sid_ref, stats_ref, series_ref, own_first, own_second, other_grad,
    own_out, other_out, out_ref, grads_ref,
):
    i = pl.program_id(0)
    sec = sec_ref[0]
    own = (i // (pl.num_programs(0) // 2)) == sec
    grads_ref[0] = jnp.where(own, own_out[0], other_out[0])
    grad = jnp.where(
        own,
        jnp.where(sec == 0, own_first[0], own_second[0].astype(f32)),
        other_grad[0].astype(f32),
    )

    @pl.when(sec == 0)
    def _():
        x = x_ref[0].astype(f32)
        width = x.shape[1]
        entries, centre, scaling = centre_and_scale(stats_ref[0], width)
        sums = series_ref[0]
        cross = sums[1:2] * scaling
        spread_grad = -cross / (2.0 * scaling * scaling * scaling * entries)
        mean_grad = sums[0:1] / scaling + 2.0 * spread_grad * (sums[2:3] * scaling)
        tables = (centre, 1.0 / scaling, 2.0 * spread_grad, mean_grad / entries)
        sid_col = column(sid_ref[pl.ds(i, 1), :])
        looked = [0.0, 0.0, 0.0, 0.0]
        for piece in range(stats_ref.shape[-1] // LANES):
            hits = series_hits(sid_col, piece)
            part = slice(piece * LANES, (piece + 1) * LANES)
            for k in range(4):
                looked[k] = looked[k] + rows_of(hits, tables[k][:, part])
        out_ref[0] = grad * looked[1] + (x - looked[0]) * looked[2] - looked[3]

    @pl.when(sec != 0)
    def _():
        out_ref[0] = grad


class Halves:
    def __init__(self, own_ref, got_ref, bit):
        self.own_ref, self.got_ref, self.bit = own_ref, got_ref, bit
        self.half = own_ref.shape[0]
        self.at = 0

    def rows(self, start, count, low):
        own = self.own_ref[start : start + count, :]
        got = self.got_ref[start : start + count, :]
        return jnp.where((self.bit == 0) == low, own, got).astype(f32)

    def take(self, out_ref, col, count):
        done = 0
        while done < count:
            low = self.at < self.half
            room = min(count - done, (self.half if low else 2 * self.half) - self.at)
            out_ref[done : done + room, col : col + LANES] = self.rows(
                self.at - (0 if low else self.half), room, low
            )
            done += room
            self.at += room


def unpack_body(bit_ref, *refs):
    parts = [Halves(refs[2 * k], refs[2 * k + 1], bit_ref[k]) for k in range(2)]
    refs = refs[4:]
    count = len(refs) // 2
    outs, scratch, sems = refs[:count], refs[count : 2 * count], refs[2 * count]
    copies = []
    for out_ref, scratch_ref in zip(outs, scratch):
        for col in range(0, scratch_ref.shape[1], LANES):
            while parts[0].at == 2 * parts[0].half:
                parts.pop(0)
            parts[0].take(scratch_ref, col, scratch_ref.shape[0])
        copies.append(pltpu.make_async_copy(scratch_ref, out_ref, sems.at[len(copies)]))
        copies[-1].start()
    for copy in copies:
        copy.wait()


def unpack_small_body(sec_ref, small_ref, attention_gain_ref, feed_gain_ref, bias_ref):
    base = 24 * sec_ref[0]
    for k in range(attention_gain_ref.shape[1] // LANES):
        cols = slice(k * LANES, (k + 1) * LANES)
        attention_gain_ref[:, cols] = small_ref[pl.ds(base + k, 1), :]
        feed_gain_ref[:, cols] = small_ref[pl.ds(base + 16 + k, 1), :]
    same = small_ref[pl.ds(base + 8, 8), :].T[0:1, : bias_ref.shape[1]]
    bias_ref[0:1, :] = same
    bias_ref[1:2, :] = -same


def swapped(x):
    return lax.ppermute(x, "section", [(0, 1), (1, 0)])


def to_section(x, section):
    return lax.ppermute(x, "section", [(1 - section, section)])


def exchange_steps(count):
    bits = []
    step = 1
    while step < count:
        bits.append(step)
        step *= 2
    other = list(bits)
    for k in range(0, len(bits) - 1, 2):
        other[k], other[k + 1] = bits[k + 1], bits[k]
    return bits, other


def partner(x, by_first, by_second, count):
    pairs = [(i, i ^ by_first) for i in range(count)]
    pairs += [(count + i, count + (i ^ by_second)) for i in range(count)]
    return lax.ppermute(x, ("section", "dp"), pairs)


def place(steps, section, index):
    step = jnp.where(section == 0, *steps)
    return (index // step) % 2


def halve(parts, orders, k, section, index, count, *more):
    keeps, sends = [], []
    for current, order in zip(parts, orders):
        bit = place(order[k], section, index)
        half = current.shape[0] // 2
        keeps.append(lax.dynamic_slice_in_dim(current, bit * half, half, 0))
        sends.append(lax.dynamic_slice_in_dim(current, (1 - bit) * half, half, 0))
    sends, keeps, more = lax.optimization_barrier((sends, keeps, more))
    got = [partner(send, *order[k], count) for send, order in zip(sends, orders)]
    parts = [(a.astype(f32) + b.astype(f32)).astype(bf16) for a, b in zip(keeps, got)]
    return (parts, *more)


def add_whole(parts, orders, k, count, *more):
    parts, more = lax.optimization_barrier((parts, more))
    got = [partner(part, *order[k], count) for part, order in zip(parts, orders)]
    parts = [(a.astype(f32) + b.astype(f32)).astype(bf16) for a, b in zip(parts, got)]
    return (parts, *more)


def double(parts, orders, k, section, index, count):
    parts = lax.optimization_barrier(parts)
    result = []
    for current, order in zip(parts, orders):
        bit = place(order[k], section, index)
        got = partner(current, *order[k], count)
        low = jnp.where(bit == 0, current, got)
        high = jnp.where(bit == 0, got, current)
        result.append(jnp.concatenate([low, high], axis=0))
    return result


HBM = pl.BlockSpec(memory_space=pl.ANY)
SCALARS = pl.BlockSpec(memory_space=pltpu.SMEM)


def whole_block(shape):
    return pl.BlockSpec(shape, lambda i, *_: (0,) * len(shape))


def by_step(shape):
    return pl.BlockSpec((1,) + shape, lambda i, *_: (i,) + (0,) * len(shape))


def by_batch(shape, own):
    return pl.BlockSpec((1,) + shape, lambda i, s: (own * s[0] + i,) + (0,) * len(shape))


def call(body, grid, in_specs, out_specs, out_shapes, scratch, flops, name):
    return pl.pallas_call(
        body,
        grid_spec=pltpu.PrefetchScalarGridSpec(
            num_scalar_prefetch=1,
            grid=(grid,),
            in_specs=in_specs,
            out_specs=out_specs,
            scratch_shapes=scratch,
        ),
        out_shape=out_shapes,
        compiler_params=pltpu.CompilerParams(vmem_limit_bytes=57 * 2**20),
        cost_estimate=pl.CostEstimate(flops=flops, bytes_accessed=2**22, transcendentals=0),
        name=name,
    )


def shape(*dims, dtype=f32):
    return jax.ShapeDtypeStruct(dims, dtype)


class Sizes:
    def __init__(self, inputs, heads, hidden, count):
        self.micro, self.rows, self.width = inputs.shape
        self.own = self.micro // 2
        self.heads, self.hidden, self.count = heads, hidden, count
        rows, width, own = self.rows, self.width, self.own
        self.stats = (8, -(-SER_DEV * count // LANES) * LANES)
        self.all_rows = whole_block((self.micro, rows))
        self.row = by_step((rows, width))
        self.row_batch = by_batch((rows, width), own)
        self.gain = whole_block((8, width))
        self.row_shape = shape(own, rows, width)
        self.low_shape = shape(own, rows, width, dtype=bf16)
        self.flops = 2 * rows * (4 * width * width + 3 * width * hidden) * own


def rotary_table(rows):
    lane = np.arange(LANES)
    frequency = np.float32(10000.0) ** (
        -(lane % (HD // 2)).astype(np.float32) * np.float32(2.0 / HD)
    )
    angle = np.arange(rows, dtype=np.float32)[:, None] * frequency[None, :].astype(np.float32)
    cosine = np.cos(angle.astype(np.float64))
    sine = np.sin(angle.astype(np.float64)) * np.where(lane < HD, -1.0, 1.0)
    parts = []
    for values in (cosine, sine):
        high = values.astype(jnp.bfloat16)
        parts += [high, (values - high.astype(np.float64)).astype(jnp.bfloat16)]
    return np.concatenate(parts, axis=1)


def series_stats(z, sec, inputs, series_id):
    return call(
        stats_body, 1,
        [pl.BlockSpec((z.own, z.rows, z.width), lambda i, s: (s[0], 0, 0)), z.all_rows],
        whole_block((z.own,) + z.stats), shape(z.own, *z.stats),
        [], 10**7, "series_stats",
    )(sec, inputs, series_id)


def layers(z, sec, inputs, cotangent, series_id, item, variate, stats, small, own, other):
    table = rotary_table(z.rows)
    rows, width, hidden = z.rows, z.width, z.hidden
    parts = [
        shape(3 * width * hidden // LANES, LANES, dtype=bf16),
        shape(4 * width * width // LANES, LANES, dtype=bf16),
    ]

    def both(*dims, dtype=f32):
        return pltpu.VMEM((2,) + dims, dtype)

    return call(
        layers_body, z.own,
        [z.row_batch, z.row_batch, z.all_rows, z.all_rows, z.all_rows, by_step(z.stats),
         whole_block(table.shape), whole_block((8, width)), whole_block((8, width))] + [HBM] * 14,
        [pl.BlockSpec((2, 1, rows, width), lambda i, *_: (0, i, 0, 0)), z.row, z.row,
         by_step(z.stats), whole_block((48, LANES))] + [HBM] * 4,
        [shape(2, z.own, rows, width, dtype=bf16), z.low_shape, z.row_shape,
         shape(z.own, *z.stats), shape(48, LANES)] + parts * 2,
        [both(width, 4 * width + 2 * hidden, dtype=bf16), both(hidden, width, dtype=bf16),
         both(width, hidden), both(width, hidden), both(hidden, width), both(1, width),
         both(width, 3 * width), both(width, width), both(1, width), both(8, rows),
         both(rows, 3 * width, dtype=bf16), both(z.heads, rows, rows, dtype=bf16),
         both(rows, width), both(rows, width),
         pltpu.VMEM((rows, rows), f32), pltpu.VMEM((rows, 3 * width), bf16),
         both(rows, width), both(rows, width), pltpu.VMEM((rows, width), bf16),
         pltpu.VMEM((rows, hidden), bf16),
         both(8 * width, LANES, dtype=bf16),
         pltpu.SemaphoreType.DMA((2, 7)), pltpu.SemaphoreType.DMA((2,))],
        12 * z.flops, "layers",
    )(sec, inputs, cotangent, series_id, item, variate, stats, jnp.asarray(table),
      *small, *own, *other)


def final(z, sec, inputs, series_id, stats, series, own_first, own_second, other_grad,
          own_out, other_out):
    own_count = z.own

    def own_step(i, s):
        return (jnp.clip(i - own_count * s[0], 0, own_count - 1), 0, 0)

    def other_step(i, s):
        return (jnp.clip(i - own_count * (1 - s[0]), 0, own_count - 1), 0, 0)

    own_spec = pl.BlockSpec((1, z.rows, z.width), own_step)
    other_spec = pl.BlockSpec((1, z.rows, z.width), other_step)
    return call(
        final_body, z.micro,
        [z.row, z.all_rows, by_step(z.stats), by_step(z.stats), own_spec, own_spec,
         other_spec, own_spec, other_spec],
        [z.row, z.row],
        [shape(z.micro, z.rows, z.width), shape(z.micro, z.rows, z.width, dtype=bf16)],
        [], 10**10, "final",
    )(sec, inputs, series_id, stats, series, own_first, own_second, other_grad, own_out, other_out)


def per_device(
    inputs,
    series_id,
    item_offset,
    variate_offset,
    cotangent,
    attention_gain,
    query_weight,
    key_weight,
    value_weight,
    out_weight,
    variate_bias,
    feed_gain,
    gate_weight,
    up_weight,
    down_weight,
):
    section = lax.axis_index("section")
    index = lax.axis_index("dp")
    count = lax.axis_size("dp")
    on_first = section == 0
    sec = section.astype(jnp.int32).reshape(1)
    heads = variate_bias.shape[1]
    z = Sizes(inputs, heads, down_weight.shape[1], count)
    width = z.width

    own_small = jnp.concatenate(
        [
            attention_gain,
            feed_gain,
            jnp.pad(variate_bias.reshape(1, 2 * heads), ((0, 0), (0, width - 2 * heads))),
        ],
        axis=0,
    ).astype(f32)
    own_small = jnp.pad(own_small, ((0, 5), (0, 0)))
    other_small = swapped(own_small)
    own = tuple(
        w[0]
        for w in (
            query_weight, key_weight, value_weight, out_weight, gate_weight, up_weight, down_weight
        )
    )
    other = tuple(swapped(w) for w in own)
    stats = series_stats(z, sec, inputs, series_id)
    steps = exchange_steps(count)[0]
    for k, step in enumerate(steps):
        if k == len(steps) - 1:
            stats, other, other_small = lax.optimization_barrier((stats, other, other_small))
        stats = merge_stats(stats, partner(stats, step, step, count), width)

    results, grad_one, standard_grad, series_sums, small_sums, *packs = layers(
        z, sec, inputs, cotangent, series_id, item_offset, variate_offset, stats,
        (own_small, other_small), own, other,
    )

    parts = [
        (k.astype(f32) + swapped(t).astype(f32)).astype(bf16)
        for k, t in zip(packs[:2], packs[2:])
    ]
    bits, turned = exchange_steps(count)
    near = list(zip(bits, turned))
    orders = (near, near[2:] + near[:2])
    rounds = len(bits)

    series_rows = z.own * z.stats[0] * z.stats[1] // LANES
    small = jnp.concatenate(
        [series_sums.reshape(-1, LANES), small_sums], axis=0
    )
    parts = halve(parts, orders, 0, section, index, count)[0]
    for k in range(1, rounds):
        if k < rounds - 1:
            parts, small = halve(parts, orders, k, section, index, count, small)
        else:
            parts, small = add_whole(parts, orders, k, count, small)
        small = small + partner(small, bits[rounds - k], bits[rounds - k], count)
    for k in reversed(range(1, rounds - 1)):
        if k == rounds - 2:
            parts, small = lax.optimization_barrier((parts, small))
            small = small + partner(small, bits[0], bits[0], count)
        if k == 1:
            parts, small, results, grad_one, standard_grad, stats = lax.optimization_barrier(
                (parts, small, results, grad_one, standard_grad, stats)
            )
            result_one, result_two = results[0], results[1]
            own_out = jnp.where(on_first, result_one, result_two)
            other_out = swapped(jnp.where(on_first, result_two, result_one))
            other_grad = swapped(jnp.where(on_first, grad_one, standard_grad.astype(bf16)))
            other_sums = swapped(small)
            other_stats = swapped(stats)
        parts = double(parts, orders, k, section, index, count)
    mine = small[:series_rows].reshape((z.own,) + z.stats)
    theirs = other_sums[:series_rows].reshape((z.own,) + z.stats)
    series_all = jnp.where(
        on_first, jnp.concatenate([mine, theirs]), jnp.concatenate([theirs, mine])
    )
    small = small[series_rows:] + other_sums[series_rows:]
    stats_all = jnp.where(
        on_first, jnp.concatenate([stats, other_stats]), jnp.concatenate([other_stats, stats])
    )
    sec_late, parts = lax.optimization_barrier((sec, parts))
    input_grads, section_output = final(
        z, sec_late, inputs, series_id, stats_all, series_all, standard_grad, grad_one, other_grad,
        own_out, other_out,
    )
    others = [partner(p, *o[0], count) for p, o in zip(parts, orders)]
    last_bits = jnp.stack([place(o[0], section, index) for o in orders]).astype(jnp.int32)

    vmem = pl.BlockSpec(memory_space=pltpu.VMEM)

    large = [shape(width, z.hidden)] * 2 + [shape(z.hidden, width)] + [shape(width, width)] * 4
    grad_gate, grad_up, grad_down, grad_query, grad_key, grad_value, grad_out = pl.pallas_call(
        unpack_body,
        in_specs=[SCALARS] + [vmem] * 4,
        out_specs=[HBM] * 7,
        out_shape=large,
        scratch_shapes=[pltpu.VMEM(s.shape, f32) for s in large] + [pltpu.SemaphoreType.DMA((7,))],
        compiler_params=pltpu.CompilerParams(vmem_limit_bytes=57 * 2**20),
        name="unpack",
    )(last_bits, *(array for pair in zip(parts, others) for array in pair))
    grad_attention_gain, grad_feed_gain, grad_bias = pl.pallas_call(
        unpack_small_body,
        in_specs=[SCALARS, vmem],
        out_shape=[shape(1, width)] * 2 + [shape(2, heads)],
        name="unpack_small",
    )(sec, small)
    return (
        section_output[None],
        input_grads[None],
        grad_attention_gain,
        grad_query[None],
        grad_key[None],
        grad_value[None],
        grad_out[None],
        grad_bias.T[None],
        grad_feed_gain,
        grad_gate[None],
        grad_up[None],
        grad_down[None],
    )


def solution(mesh):
    placed = (
        P(None, "dp", None),
        P(None, "dp"),
        P(None, "dp"),
        P(None, "dp"),
        P(None, "dp", None),
        P("section", None),
        P("section", None, None),
        P("section", None, None),
        P("section", None, None),
        P("section", None, None),
        P("section", None, None),
        P("section", None),
        P("section", None, None),
        P("section", None, None),
        P("section", None, None),
    )
    return jax.shard_map(
        per_device,
        mesh=mesh,
        in_specs=placed,
        out_specs=(
            P("section", None, "dp", None),
            P("section", None, "dp", None),
            P("section", None),
            P("section", None, None),
            P("section", None, None),
            P("section", None, None),
            P("section", None, None),
            P("section", None, None),
            P("section", None),
            P("section", None, None),
            P("section", None, None),
            P("section", None, None),
        ),
        check_vma=False,
    )
```

```python
import functools

import jax
import jax.numpy as jnp
import numpy as np
from jax import lax
from jax.experimental import pallas as pl
from jax.experimental.pallas import tpu as pltpu
from jax.sharding import PartitionSpec as P

HD = 64
BLOCK = 512
SER_DEV = 4
LANES = 128
CHUNK = 512
TILE = 256

norm_epsilon = 1e-05
scale_epsilon = 1e-05
masked_score = -1e30

f32 = jnp.float32
bf16 = jnp.bfloat16

AS_IS = (((1,), (0,)), ((), ()))
RIGHT_T = (((1,), (1,)), ((), ()))
LEFT_T = (((0,), (0,)), ((), ()))


def dot(left, right, dims=AS_IS):
    return lax.dot_general(left, right, dims, preferred_element_type=f32)


def column(row):
    return jnp.broadcast_to(row.astype(f32), (LANES, row.shape[1])).T


def lane_index(rows):
    return lax.broadcasted_iota(jnp.int32, (rows, LANES), 1)


def regroup(x):
    group = lane_index(x.shape[0]) // (HD // 2)
    return jnp.where(
        group == 1,
        pltpu.roll(x, LANES - HD // 2, 1),
        jnp.where(group == 2, pltpu.roll(x, HD // 2, 1), x),
    )


def turn(x, cosine, sine):
    return x * cosine + pltpu.roll(x, LANES // 2, 1) * sine


def turn_back(x, cosine, sine):
    return x * cosine - pltpu.roll(x, LANES // 2, 1) * sine


def inverse_rms(x):
    return lax.rsqrt(jnp.mean(x * x, axis=1, keepdims=True) + norm_epsilon)


def series_hits(sid_col, piece):
    return sid_col == (lane_index(sid_col.shape[0]) + piece * LANES).astype(f32)


def rows_of(hits, per_series):
    return jnp.sum(jnp.where(hits, per_series, 0.0), axis=1, keepdims=True)


def series_of(hits, per_row):
    return jnp.sum(jnp.where(hits, per_row, 0.0), axis=0, keepdims=True)


def stats_body(sec_ref, x_ref, sid_ref, out_ref):
    own, _, width = x_ref.shape
    pieces = out_ref.shape[-1] // LANES
    out_ref[...] = jnp.zeros_like(out_ref)
    for i in range(own):
        x = x_ref[i].astype(f32)
        sid_col = column(sid_ref[pl.ds(own * sec_ref[0] + i, 1), :])
        totals = jnp.sum(x, axis=1, keepdims=True)
        centre = jnp.zeros_like(totals)
        for piece in range(pieces):
            hits = series_hits(sid_col, piece)
            count = series_of(hits, 1.0)
            total = series_of(hits, totals)
            centre = centre + rows_of(hits, total / (jnp.maximum(count, 1.0) * width))
            out_ref[i, 0:1, piece * LANES : (piece + 1) * LANES] = count
            out_ref[i, 1:2, piece * LANES : (piece + 1) * LANES] = total
        centred = x - centre
        squares = jnp.sum(centred * centred, axis=1, keepdims=True)
        for piece in range(pieces):
            hits = series_hits(sid_col, piece)
            out_ref[i, 2:3, piece * LANES : (piece + 1) * LANES] = series_of(hits, squares)


def merge_stats(here, there, width):
    count_a, total_a, spread_a = here[:, 0:1], here[:, 1:2], here[:, 2:3]
    count_b, total_b, spread_b = there[:, 0:1], there[:, 1:2], there[:, 2:3]
    count = count_a + count_b
    gap = total_a / (jnp.maximum(count_a, 1.0) * width) - total_b / (
        jnp.maximum(count_b, 1.0) * width
    )
    weight = count_a * count_b * width / jnp.maximum(count, 1.0)
    row = lax.broadcasted_iota(jnp.int32, here.shape, 1)
    return jnp.where(
        row == 0,
        count,
        jnp.where(row == 1, total_a + total_b, spread_a + spread_b + gap * gap * weight),
    )


def centre_and_scale(stats, width):
    entries = jnp.maximum(stats[0:1], 1.0) * width
    centre = stats[1:2] / entries
    scaling = jnp.sqrt(stats[2:3] / entries + scale_epsilon)
    return entries, centre, scaling


class Weights:
    def __init__(self, section, own_refs, other_refs, big_ref, down_ref, sems):
        self.first_step = pl.program_id(0) == 0
        self.big_ref, self.down_ref = big_ref, down_ref
        self.own_refs, self.sems = own_refs, sems

        @pl.when(self.first_step)
        def _():
            for layer_of, refs in ((section, own_refs), (1 - section, other_refs)):
                for k, ref in enumerate(refs):
                    pltpu.make_async_copy(ref, self.target(layer_of, k), sems.at[layer_of, k]).start()

    def target(self, layer, k):
        if k == 6:
            return self.down_ref.at[layer]
        at = sum(ref.shape[1] for ref in self.own_refs[:k])
        return self.big_ref.at[layer, :, pl.ds(at, self.own_refs[k].shape[1])]

    def wait_here(self, layer, numbers):
        for k in numbers:
            pltpu.make_async_copy(
                self.own_refs[k], self.target(layer, k), self.sems.at[layer, k]
            ).wait()

    def wait_attention(self, layer):
        width = self.big_ref.shape[1]

        @pl.when(self.first_step)
        def _():
            self.wait_here(layer, (0, 1, 2, 3))
            for at in range(0, 2 * width, LANES):
                tile = self.big_ref[layer, :, at : at + LANES].astype(f32)
                self.big_ref[layer, :, at : at + LANES] = regroup(tile).astype(bf16)

    def wait_feed(self, layer):
        @pl.when(self.first_step)
        def _():
            self.wait_here(layer, (4, 5, 6))


def sigmoid(x):
    return 0.5 * jnp.tanh(0.5 * x) + 0.5


def in_head(half, lanes, grouped):
    if grouped:
        return (lanes % HD) // (HD // 2) == half
    return lanes // HD == half


def row_index(rows):
    return lax.broadcasted_iota(jnp.int32, (LANES, rows), 0)


class Block:
    def __init__(self, cosine, sine, item_col, var_col, var_row, same_ref):
        rows = cosine.shape[0]
        self.cosine, self.sine, self.same_ref = cosine, sine, same_ref
        row = var_row.astype(f32)
        for at in range(0, rows, LANES):
            same_ref[:, at : at + LANES] = jnp.where(var_col == row[:, at : at + LANES], 1.0, 0.0)
        lane = lane_index(rows)
        second = jnp.where(item_col > 0.0, 1.0, 0.0)
        self.item_q = jnp.where(
            lane == 0, second, jnp.where(lane == 1, 1.0 - second, 0.0)
        ).astype(bf16)
        self.item_k = jnp.where(
            lane == 0,
            (1.0 - second) * masked_score,
            jnp.where(lane == 1, second * masked_score, 0.0),
        ).astype(bf16)


def attention_forward(layer, hidden, gains, block, bias, weights, saved):
    qkv_ref, prob_ref, inv_ref, mixed_ref = (ref.at[layer] for ref in saved)
    rows, width = hidden.shape
    pairs = width // LANES
    tiles = rows // TILE
    big_ref = weights.big_ref.at[layer]
    normed = (hidden * inverse_rms(hidden) * gains).astype(bf16)
    weights.wait_attention(layer)
    lane = lane_index(rows)
    first_rows = row_index(rows) < HD
    extra = lax.broadcasted_iota(jnp.int32, (16, rows), 0)

    projected = dot(normed, big_ref[:, : 3 * width])

    def project(p):
        at = p * LANES
        q = turn(projected[:, at : at + LANES], block.cosine, block.sine)
        k = turn(projected[:, width + at : width + at + LANES], block.cosine, block.sine)
        v = projected[:, 2 * width + at : 2 * width + at + LANES]
        qkv_ref[:, at : at + LANES] = (q * HD**-0.5).astype(bf16)
        qkv_ref[:, width + at : width + at + LANES] = k.astype(bf16)
        qkv_ref[:, 2 * width + at : 2 * width + at + LANES] = v.astype(bf16)

    def operands(p):
        at = p * LANES
        q_pair = qkv_ref[:, at : at + LANES]
        k_aug = jnp.concatenate([qkv_ref[:, width + at : width + at + LANES], block.item_k], axis=1)
        v_turned = qkv_ref[:, 2 * width + at : 2 * width + at + LANES].T
        heads = []
        for half in range(2):
            q_aug = jnp.concatenate(
                [jnp.where(in_head(half, lane, True), q_pair, 0.0).astype(bf16), block.item_q],
                axis=1,
            )
            own_rows = first_rows if half == 0 else jnp.logical_not(first_rows)
            v_aug = jnp.concatenate(
                [
                    jnp.where(own_rows, v_turned, 0.0).astype(bf16),
                    jnp.where(extra == half, 1.0, 0.0).astype(bf16),
                ],
                axis=0,
            )
            heads.append((q_aug, v_aug))
        return k_aug, heads

    prepared = {}

    def scores_of(p, half, t):
        if p not in prepared:
            project(p)
            prepared[p] = operands(p)
        k_aug, heads = prepared[p]
        return dot(k_aug, heads[half][0][t * TILE : (t + 1) * TILE, :], RIGHT_T)

    order = [(p, half, t) for p in range(pairs) for half in range(2) for t in range(tiles)]
    attended = {}
    scores = scores_of(*order[0])
    for n, (p, half, t) in enumerate(order):
        following = scores_of(*order[n + 1]) if n + 1 < len(order) else None
        head = 2 * p + half
        cols = slice(t * TILE, (t + 1) * TILE)
        gap = bias[0:1, 2 * head : 2 * head + 1] - bias[0:1, 2 * head + 1 : 2 * head + 2]
        biased = scores + block.same_ref[:, cols] * gap
        peak = jnp.max(biased, axis=0, keepdims=True)
        prob = jnp.exp(biased - peak).astype(bf16)
        prob_ref[head, :, cols] = prob
        part = dot(prepared[p][1][half][1], prob)
        attended[p, t] = part if half == 0 else attended[p, t] + part
        if half == 1:
            sums = attended.pop((p, t))
            own_rows = row_index(TILE) < HD
            inv = jnp.where(
                own_rows, 1.0 / sums[LANES : LANES + 1], 1.0 / sums[LANES + 1 : LANES + 2]
            )
            inv_ref[cols, p * LANES : (p + 1) * LANES] = inv.T
            mixed_ref[cols, p * LANES : (p + 1) * LANES] = (sums[:LANES] * inv).T
        scores = following
    return hidden + dot(mixed_ref[...].astype(bf16), big_ref[:, 3 * width : 4 * width])


def feed_forward(layer, middle, gains, weights):
    big_ref, down_ref = weights.big_ref.at[layer], weights.down_ref.at[layer]
    width = middle.shape[1]
    hidden = down_ref.shape[0]
    feed = (middle * inverse_rms(middle) * gains).astype(bf16)
    total = middle
    for at in range(0, hidden, CHUNK):
        gate = dot(feed, big_ref[:, 4 * width + at : 4 * width + at + CHUNK])
        up = dot(feed, big_ref[:, 4 * width + hidden + at : 4 * width + hidden + at + CHUNK])
        active = (gate * sigmoid(gate) * up).astype(bf16)
        total = total + dot(active, down_ref[at : at + CHUNK, :])
    return total.astype(bf16)


def feed_backward(layer, middle, gains, grad_low, weights, accs, active_ref):
    gate_acc, up_acc, down_acc, gain_acc = (acc.at[layer] for acc in accs)
    big_ref, down_ref = weights.big_ref.at[layer], weights.down_ref.at[layer]
    width = middle.shape[1]
    hidden = down_ref.shape[0]
    inverse = inverse_rms(middle)
    feed = (middle * inverse * gains).astype(bf16)
    feed_t = feed.T
    feed_grad = jnp.zeros(middle.shape, f32)
    for at in range(0, hidden, CHUNK):
        gate_w = big_ref[:, 4 * width + at : 4 * width + at + CHUNK]
        up_w = big_ref[:, 4 * width + hidden + at : 4 * width + hidden + at + CHUNK]
        down_w = down_ref[at : at + CHUNK, :]
        gate = dot(feed, gate_w)
        up = dot(feed, up_w)
        act_grad = dot(grad_low, down_w, RIGHT_T)
        gated = sigmoid(gate)
        swish = gate * gated
        active = (swish * up).astype(bf16)
        active_ref[:, at : at + CHUNK] = active
        gate_grad = (act_grad * up * (gated + swish * (1.0 - gated))).astype(bf16)
        up_grad = (act_grad * swish).astype(bf16)
        feed_grad = feed_grad + dot(gate_grad, gate_w, RIGHT_T) + dot(up_grad, up_w, RIGHT_T)
        gate_acc[:, at : at + CHUNK] += dot(feed_t, gate_grad)
        up_acc[:, at : at + CHUNK] += dot(feed_t, up_grad)
        down_acc[at : at + CHUNK, :] += dot(active, grad_low, LEFT_T)
    scaled = feed_grad * gains
    gain_acc[...] += jnp.sum(feed_grad * middle * inverse, axis=0, keepdims=True)
    return (
        grad_low.astype(f32)
        + inverse * scaled
        - middle * (inverse * inverse * inverse) * jnp.mean(scaled * middle, axis=1, keepdims=True)
    )


def attention_backward(layer, middle_grad, hidden, gains, block, weights, saved, grads_ref, accs):
    qkv_ref, prob_ref, inv_ref, mixed_ref = (ref.at[layer] for ref in saved)
    qkv_acc, out_acc, gain_acc, bias_acc = (acc.at[layer] for acc in accs)
    rows, width = hidden.shape
    pairs = width // LANES
    tiles = rows // TILE
    big_ref = weights.big_ref.at[layer]
    mix_grad = middle_grad.astype(bf16)
    att_grad = dot(mix_grad, big_ref[:, 3 * width : 4 * width], RIGHT_T).astype(bf16)
    lane = lane_index(rows)
    ones_four = jnp.where(lane < 4, 1.0, 0.0).astype(bf16)
    source = lax.broadcasted_iota(jnp.int32, (2 * LANES, LANES), 0) % LANES // HD
    target = lax.broadcasted_iota(jnp.int32, (2 * LANES, LANES), 1)
    gather = jnp.where((target // 2 == source) & (target < 4), 1.0, 0.0).astype(bf16)

    def operands(p):
        at = p * LANES
        q_pair = qkv_ref[:, at : at + LANES]
        k_turned = qkv_ref[:, width + at : width + at + LANES].T
        v_aug = jnp.concatenate(
            [qkv_ref[:, 2 * width + at : 2 * width + at + LANES], ones_four], axis=1
        )
        grad_pair = (att_grad[:, at : at + LANES].astype(f32) * inv_ref[:, at : at + LANES]).astype(
            bf16
        )
        product = grad_pair.astype(f32) * mixed_ref[:, at : at + LANES]
        high = product.astype(bf16)
        low = (product - high.astype(f32)).astype(bf16)
        inner = dot(jnp.concatenate([high, low], axis=1), gather)
        inner_high = inner.astype(bf16).astype(f32)
        tail = jnp.where(lane % 2 == 0, -inner_high, inner_high - inner)
        heads = []
        for half in range(2):
            grad_low = jnp.where(in_head(half, lane, False), grad_pair, 0.0).astype(bf16)
            tail_low = jnp.where(lane // 2 == half, tail, 0.0).astype(bf16)
            q_mine = jnp.where(in_head(half, lane, True), q_pair, 0.0).astype(bf16)
            low = half * (HD // 2)
            k_mine = jnp.concatenate(
                [k_turned[low : low + HD // 2], k_turned[HD + low : HD + low + HD // 2]], axis=0
            )
            heads.append(
                (jnp.concatenate([grad_low, tail_low], axis=1), grad_low, q_mine, k_mine)
            )
        return v_aug, heads

    prepared = {}

    def prob_grad_of(p, half, t):
        if p not in prepared:
            prepared[p] = operands(p)
        v_aug, heads = prepared[p]
        return dot(v_aug, heads[half][0][t * TILE : (t + 1) * TILE, :], RIGHT_T)

    order = [(p, half, t) for p in range(pairs) for half in range(2) for t in range(tiles)]
    value_grad = key_grad = None
    query_grad = {}
    prob_grad = prob_grad_of(*order[0])
    for n, (p, half, t) in enumerate(order):
        following = prob_grad_of(*order[n + 1]) if n + 1 < len(order) else None
        head = 2 * p + half
        cols = slice(t * TILE, (t + 1) * TILE)
        at = p * LANES
        _, grad_low, q_mine, k_mine = prepared[p][1][half]
        prob = prob_ref[head, :, cols]
        score_grad = prob.astype(f32) * prob_grad
        bias_acc[head : head + 1, cols] += jnp.sum(
            score_grad * block.same_ref[:, cols], axis=0, keepdims=True
        )
        score_low = score_grad.astype(bf16)
        part_v = dot(prob, grad_low[cols, :])
        part_k = dot(score_low, q_mine[cols, :])
        part_q = dot(k_mine, score_low)
        value_grad = part_v if value_grad is None else value_grad + part_v
        key_grad = part_k if key_grad is None else key_grad + part_k
        query_grad[t, half] = part_q
        if half == 1:
            one, two = query_grad.pop((t, 0)), query_grad.pop((t, 1))
            mid = HD // 2
            back = jnp.concatenate([one[:mid], two[:mid], one[mid:], two[mid:]], axis=0).T * HD**-0.5
            grads_ref[cols, at : at + LANES] = turn_back(
                back, block.cosine[cols, :], block.sine[cols, :]
            ).astype(bf16)
        if half == 1 and t == tiles - 1:
            grads_ref[:, width + at : width + at + LANES] = turn_back(
                key_grad, block.cosine, block.sine
            ).astype(bf16)
            grads_ref[:, 2 * width + at : 2 * width + at + LANES] = value_grad.astype(bf16)
            value_grad = key_grad = None
        prob_grad = following
    out_acc[...] += dot(mixed_ref[...].astype(bf16), mix_grad, LEFT_T)
    inverse = inverse_rms(hidden)
    normed = (hidden * inverse * gains).astype(bf16)
    normed_grad = dot(grads_ref[...], big_ref[:, : 3 * width], RIGHT_T)
    qkv_acc[...] += dot(normed, grads_ref[...], LEFT_T)
    scaled = normed_grad * gains
    gain_acc[...] += jnp.sum(normed_grad * hidden * inverse, axis=0, keepdims=True)
    return (
        middle_grad
        + inverse * scaled
        - hidden * (inverse * inverse * inverse) * jnp.mean(scaled * hidden, axis=1, keepdims=True)
    )


def column_tiles(acc_ref):
    return [acc_ref[:, at : at + LANES] for at in range(0, acc_ref.shape[1], LANES)]


class Packer:
    def __init__(self, stage_ref, sems, kept_refs, sent_refs):
        self.stage_ref, self.sems = stage_ref, sems
        self.kept_refs, self.sent_refs = kept_refs, sent_refs
        self.sent = []

    def copy(self, out_ref, slot, count):
        source = self.stage_ref.at[slot, pl.ds(0, count)]
        return pltpu.make_async_copy(source, out_ref, self.sems.at[slot])

    def send(self, keep, part, start, tiles):
        slot = len(self.sent) % 2
        if len(self.sent) >= 2:
            self.wait(2)
        at = 0
        for tile in tiles:
            self.stage_ref[slot, at : at + tile.shape[0], :] = tile.astype(bf16)
            at += tile.shape[0]
        where = pl.ds(start, at)

        @pl.when(keep)
        def _():
            self.copy(self.kept_refs[part].at[where], slot, at).start()

        @pl.when(jnp.logical_not(keep))
        def _():
            self.copy(self.sent_refs[part].at[where], slot, at).start()

        self.sent.append((self.kept_refs[part].at[where], slot, at))

    def wait(self, back):
        self.copy(*self.sent[-back]).wait()

    def finish(self):
        self.wait(2)
        self.wait(1)


def layers_body(
    sec_ref, x_ref, cotangent_ref, sid_ref, item_ref, var_ref, stats_ref, table_ref,
    own_small_ref, other_small_ref, *refs
):
    own_refs, other_refs, refs = refs[:7], refs[7:14], refs[14:]
    results_ref, grad_one_ref, grad_zero_ref, series_ref, small_ref = refs[:5]
    kept_refs, sent_refs, refs = refs[5:7], refs[7:9], refs[9:]
    big_ref, down_ref, refs = refs[0], refs[1], refs[2:]
    feed_accs, attention_accs, saved, refs = refs[:4], refs[4:8], refs[8:12], refs[12:]
    same_ref, grads_ref, hidden_ref, middle_ref, grad_ref, active_ref, stage_ref, *refs = refs
    sems, stage_sems = refs

    i = pl.program_id(0)
    last = i == pl.num_programs(0) - 1
    m = pl.num_programs(0) * sec_ref[0] + i
    weights = Weights(sec_ref[0], own_refs, other_refs, big_ref, down_ref, sems)

    @pl.when(i == 0)
    def _():
        for acc in feed_accs + attention_accs:
            acc[...] = jnp.zeros_like(acc)

    x = x_ref[0].astype(f32)
    rows, width = x.shape
    var_row = var_ref[pl.ds(m, 1), :]
    var_col = column(var_row)
    sid_col = column(sid_ref[pl.ds(m, 1), :])
    pieces = stats_ref.shape[-1] // LANES

    time = lax.broadcasted_iota(jnp.int32, (rows, LANES), 0).astype(f32) - var_col
    cosine = sine = jnp.zeros((rows, LANES), f32)
    for at in range(0, rows, LANES):
        hot = jnp.where(time == (lane_index(rows) + at).astype(f32), 1.0, 0.0).astype(bf16)
        found = dot(hot, table_ref[at : at + LANES, :])
        cosine = cosine + found[:, :LANES] + found[:, LANES : 2 * LANES]
        sine = sine + found[:, 2 * LANES : 3 * LANES] + found[:, 3 * LANES :]
    block = Block(cosine, sine, column(item_ref[pl.ds(m, 1), :]), var_col, var_row, same_ref)

    _, centre, scaling = centre_and_scale(stats_ref[0], width)
    centre_rows = scale_rows = 0.0
    for piece in range(pieces):
        hits = series_hits(sid_col, piece)
        part = slice(piece * LANES, (piece + 1) * LANES)
        centre_rows = centre_rows + rows_of(hits, centre[:, part])
        scale_rows = scale_rows + rows_of(hits, scaling[:, part])
    hidden_ref[0] = (x - centre_rows) / scale_rows
    grad_ref[...] = cotangent_ref[0]

    def small_row(layer, k):
        return jnp.where(
            sec_ref[0] == layer, own_small_ref[k : k + 1, :], other_small_ref[k : k + 1, :]
        )

    def forward(layer, _):
        middle = attention_forward(
            layer, hidden_ref[layer], small_row(layer, 0), block, small_row(layer, 2), weights,
            saved,
        )
        middle_ref[layer] = middle
        weights.wait_feed(layer)

        @pl.when(layer == 0)
        def _():
            result = feed_forward(layer, middle_ref[0], small_row(layer, 1), weights)
            results_ref[0, 0] = result
            hidden_ref[1] = result.astype(f32)

    def send(layer):
        packer = Packer(stage_ref, stage_sems, kept_refs, sent_refs)
        keep = sec_ref[0] == layer
        gate, up, down = (column_tiles(acc.at[layer]) for acc in feed_accs[:3])
        queries = column_tiles(attention_accs[0].at[layer])
        turned = [regroup(tile) for tile in queries[:6]]
        start = 0
        for tiles in (gate, up, down):
            packer.send(keep, 0, start, tiles)
            start += sum(tile.shape[0] for tile in tiles)
        packer.send(keep, 1, 0, turned)
        packer.send(keep, 1, width * 6, queries[6:] + column_tiles(attention_accs[1].at[layer]))
        packer.finish()

    def backward(step, _):
        layer = 1 - step
        middle_grad = feed_backward(
            layer, middle_ref[layer], small_row(layer, 1), grad_ref[...], weights, feed_accs,
            active_ref,
        )

        @pl.when(layer == 1)
        def _():
            total = middle_ref[1] + dot(active_ref[...], weights.down_ref[1])
            results_ref[1, 0] = total.astype(bf16)

        hidden_grad = attention_backward(
            layer, middle_grad, hidden_ref[layer], small_row(layer, 0), block, weights,
            saved, grads_ref, attention_accs,
        )
        grad_ref[...] = hidden_grad.astype(bf16)
        grad_zero_ref[0] = hidden_grad

        @pl.when(layer == 1)
        def _():
            grad_one_ref[0] = hidden_grad.astype(bf16)

        @pl.when(last)
        def _():
            send(layer)

    lax.fori_loop(0, 2, forward, None)
    lax.fori_loop(0, 2, backward, None)

    standard, hidden_grad = hidden_ref[0], grad_zero_ref[0]
    grad_rows = jnp.sum(hidden_grad, axis=1, keepdims=True)
    cross_rows = jnp.sum(hidden_grad * standard, axis=1, keepdims=True)
    standard_rows = jnp.sum(standard, axis=1, keepdims=True)
    series_ref[0] = jnp.zeros(series_ref.shape[1:], f32)
    for piece in range(pieces):
        hits = series_hits(sid_col, piece)
        part = slice(piece * LANES, (piece + 1) * LANES)
        series_ref[0, 0:1, part] = series_of(hits, grad_rows)
        series_ref[0, 1:2, part] = series_of(hits, cross_rows)
        series_ref[0, 2:3, part] = series_of(hits, standard_rows)

    @pl.when(last)
    def _():
        small_ref[...] = jnp.zeros_like(small_ref)
        for layer in range(2):
            base = 24 * layer
            for k in range(width // LANES):
                cols = slice(k * LANES, (k + 1) * LANES)
                small_ref[base + k : base + k + 1, :] = attention_accs[2][layer, :, cols]
                small_ref[base + 16 + k : base + 17 + k, :] = feed_accs[3][layer, :, cols]
            bias_sums = jnp.sum(attention_accs[3][layer], axis=1, keepdims=True)
            small_ref[base + 8 : base + 16, :] = jnp.broadcast_to(bias_sums, (8, LANES))


def final_body(
    sec_ref, x_ref, sid_ref, stats_ref, series_ref, own_first, own_second, other_grad,
    own_out, other_out, out_ref, grads_ref,
):
    i = pl.program_id(0)
    sec = sec_ref[0]
    own = (i // (pl.num_programs(0) // 2)) == sec
    grads_ref[0] = jnp.where(own, own_out[0], other_out[0])
    grad = jnp.where(
        own,
        jnp.where(sec == 0, own_first[0], own_second[0].astype(f32)),
        other_grad[0].astype(f32),
    )

    @pl.when(sec == 0)
    def _():
        x = x_ref[0].astype(f32)
        width = x.shape[1]
        entries, centre, scaling = centre_and_scale(stats_ref[0], width)
        sums = series_ref[0]
        cross = sums[1:2] * scaling
        spread_grad = -cross / (2.0 * scaling * scaling * scaling * entries)
        mean_grad = sums[0:1] / scaling + 2.0 * spread_grad * (sums[2:3] * scaling)
        tables = (centre, 1.0 / scaling, 2.0 * spread_grad, mean_grad / entries)
        sid_col = column(sid_ref[pl.ds(i, 1), :])
        looked = [0.0, 0.0, 0.0, 0.0]
        for piece in range(stats_ref.shape[-1] // LANES):
            hits = series_hits(sid_col, piece)
            part = slice(piece * LANES, (piece + 1) * LANES)
            for k in range(4):
                looked[k] = looked[k] + rows_of(hits, tables[k][:, part])
        out_ref[0] = grad * looked[1] + (x - looked[0]) * looked[2] - looked[3]

    @pl.when(sec != 0)
    def _():
        out_ref[0] = grad


def unpack_body(held, count, bit_ref, feed_ref, attention_ref, *refs):
    refs = refs[count:]
    gate, up, down, query, key, value, out = refs[:7]
    gate_at, up_at, down_at, one_at, two_at, sems = refs[7:]
    half_up = up_at.shape[1]

    def leave(k, source_ref, at, scratch_ref, target_ref):
        rows = scratch_ref.shape[0]
        for col in range(0, scratch_ref.shape[1], LANES):
            scratch_ref[:, col : col + LANES] = source_ref[at : at + rows, :].astype(f32)
            at += rows
        copy = pltpu.make_async_copy(scratch_ref, target_ref, sems.at[k])
        copy.start()
        return copy

    gate_rows = gate_at.shape[0] * gate_at.shape[1] // LANES
    up_rows = up_at.shape[0] * half_up // LANES
    one_rows = one_at.shape[0] * one_at.shape[1] // LANES

    def feed(low):
        if low:
            return [
                leave(0, feed_ref, 0, gate_at, gate),
                leave(1, feed_ref, gate_rows, up_at, up.at[:, pl.ds(0, half_up)]),
            ]
        return [
            leave(0, feed_ref, up_rows, down_at, down),
            leave(1, feed_ref, 0, up_at, up.at[:, pl.ds(half_up, half_up)]),
        ]

    def attention(low):
        first, second = (query, key) if low else (value, out)
        return [
            leave(2, attention_ref, 0, one_at, first),
            leave(3, attention_ref, one_rows, two_at, second),
        ]

    for feed_low in range(2):
        for attention_low in range(2):
            here = (bit_ref[0] == (1 - feed_low if held else feed_low)) & (
                bit_ref[1] == (1 - attention_low if held else attention_low)
            )

            @pl.when(here)
            def _(feed_low=feed_low, attention_low=attention_low):
                for copy in feed(feed_low) + attention(attention_low):
                    copy.wait()


def unpack_small_body(sec_ref, small_ref, attention_gain_ref, feed_gain_ref, bias_ref):
    base = 24 * sec_ref[0]
    for k in range(attention_gain_ref.shape[1] // LANES):
        cols = slice(k * LANES, (k + 1) * LANES)
        attention_gain_ref[:, cols] = small_ref[pl.ds(base + k, 1), :]
        feed_gain_ref[:, cols] = small_ref[pl.ds(base + 16 + k, 1), :]
    same = small_ref[pl.ds(base + 8, 8), :].T[0:1, : bias_ref.shape[1]]
    bias_ref[0:1, :] = same
    bias_ref[1:2, :] = -same


def swapped(x):
    return lax.ppermute(x, "section", [(0, 1), (1, 0)])


def to_section(x, section):
    return lax.ppermute(x, "section", [(1 - section, section)])


def exchange_steps(count):
    bits = []
    step = 1
    while step < count:
        bits.append(step)
        step *= 2
    other = list(bits)
    for k in range(0, len(bits) - 1, 2):
        other[k], other[k + 1] = bits[k + 1], bits[k]
    return bits, other


def partner(x, by_first, by_second, count):
    pairs = [(i, i ^ by_first) for i in range(count)]
    pairs += [(count + i, count + (i ^ by_second)) for i in range(count)]
    return lax.ppermute(x, ("section", "dp"), pairs)


def place(steps, section, index):
    step = jnp.where(section == 0, *steps)
    return (index // step) % 2


def halve(parts, orders, k, section, index, count, *more):
    keeps, sends = [], []
    for current, order in zip(parts, orders):
        bit = place(order[k], section, index)
        half = current.shape[0] // 2
        keeps.append(lax.dynamic_slice_in_dim(current, bit * half, half, 0))
        sends.append(lax.dynamic_slice_in_dim(current, (1 - bit) * half, half, 0))
    sends, keeps, more = lax.optimization_barrier((sends, keeps, more))
    got = [partner(send, *order[k], count) for send, order in zip(sends, orders)]
    parts = [(a.astype(f32) + b.astype(f32)).astype(bf16) for a, b in zip(keeps, got)]
    return (parts, *more)


def add_whole(parts, orders, k, count, *more):
    parts, more = lax.optimization_barrier((parts, more))
    got = [partner(part, *order[k], count) for part, order in zip(parts, orders)]
    parts = [(a.astype(f32) + b.astype(f32)).astype(bf16) for a, b in zip(parts, got)]
    return (parts, *more)


def double(parts, orders, k, section, index, count):
    parts = lax.optimization_barrier(parts)
    result = []
    for current, order in zip(parts, orders):
        bit = place(order[k], section, index)
        got = partner(current, *order[k], count)
        low = jnp.where(bit == 0, current, got)
        high = jnp.where(bit == 0, got, current)
        result.append(jnp.concatenate([low, high], axis=0))
    return result


HBM = pl.BlockSpec(memory_space=pl.ANY)
SCALARS = pl.BlockSpec(memory_space=pltpu.SMEM)


def whole_block(shape):
    return pl.BlockSpec(shape, lambda i, *_: (0,) * len(shape))


def by_step(shape):
    return pl.BlockSpec((1,) + shape, lambda i, *_: (i,) + (0,) * len(shape))


def by_batch(shape, own):
    return pl.BlockSpec((1,) + shape, lambda i, s: (own * s[0] + i,) + (0,) * len(shape))


def call(body, grid, in_specs, out_specs, out_shapes, scratch, flops, name):
    return pl.pallas_call(
        body,
        grid_spec=pltpu.PrefetchScalarGridSpec(
            num_scalar_prefetch=1,
            grid=(grid,),
            in_specs=in_specs,
            out_specs=out_specs,
            scratch_shapes=scratch,
        ),
        out_shape=out_shapes,
        compiler_params=pltpu.CompilerParams(vmem_limit_bytes=57 * 2**20),
        cost_estimate=pl.CostEstimate(flops=flops, bytes_accessed=2**22, transcendentals=0),
        name=name,
    )


def shape(*dims, dtype=f32):
    return jax.ShapeDtypeStruct(dims, dtype)


class Sizes:
    def __init__(self, inputs, heads, hidden, count):
        self.micro, self.rows, self.width = inputs.shape
        self.own = self.micro // 2
        self.heads, self.hidden, self.count = heads, hidden, count
        rows, width, own = self.rows, self.width, self.own
        self.stats = (8, -(-SER_DEV * count // LANES) * LANES)
        self.all_rows = whole_block((self.micro, rows))
        self.row = by_step((rows, width))
        self.row_batch = by_batch((rows, width), own)
        self.gain = whole_block((8, width))
        self.row_shape = shape(own, rows, width)
        self.low_shape = shape(own, rows, width, dtype=bf16)
        self.flops = 2 * rows * (4 * width * width + 3 * width * hidden) * own


def rotary_table(rows):
    lane = np.arange(LANES)
    frequency = np.float32(10000.0) ** (
        -(lane % (HD // 2)).astype(np.float32) * np.float32(2.0 / HD)
    )
    angle = np.arange(rows, dtype=np.float32)[:, None] * frequency[None, :].astype(np.float32)
    cosine = np.cos(angle.astype(np.float64))
    sine = np.sin(angle.astype(np.float64)) * np.where(lane < HD, -1.0, 1.0)
    parts = []
    for values in (cosine, sine):
        high = values.astype(jnp.bfloat16)
        parts += [high, (values - high.astype(np.float64)).astype(jnp.bfloat16)]
    return np.concatenate(parts, axis=1)


def series_stats(z, sec, inputs, series_id):
    return call(
        stats_body, 1,
        [pl.BlockSpec((z.own, z.rows, z.width), lambda i, s: (s[0], 0, 0)), z.all_rows],
        whole_block((z.own,) + z.stats), shape(z.own, *z.stats),
        [], 10**7, "series_stats",
    )(sec, inputs, series_id)


def layers(z, sec, inputs, cotangent, series_id, item, variate, stats, small, own, other):
    table = rotary_table(z.rows)
    rows, width, hidden = z.rows, z.width, z.hidden
    parts = [
        shape(3 * width * hidden // LANES, LANES, dtype=bf16),
        shape(4 * width * width // LANES, LANES, dtype=bf16),
    ]

    def both(*dims, dtype=f32):
        return pltpu.VMEM((2,) + dims, dtype)

    return call(
        layers_body, z.own,
        [z.row_batch, z.row_batch, z.all_rows, z.all_rows, z.all_rows, by_step(z.stats),
         whole_block(table.shape), whole_block((8, width)), whole_block((8, width))] + [HBM] * 14,
        [pl.BlockSpec((2, 1, rows, width), lambda i, *_: (0, i, 0, 0)), z.row, z.row,
         by_step(z.stats), whole_block((48, LANES))] + [HBM] * 4,
        [shape(2, z.own, rows, width, dtype=bf16), z.low_shape, z.row_shape,
         shape(z.own, *z.stats), shape(48, LANES)] + parts * 2,
        [both(width, 4 * width + 2 * hidden, dtype=bf16), both(hidden, width, dtype=bf16),
         both(width, hidden), both(width, hidden), both(hidden, width), both(1, width),
         both(width, 3 * width), both(width, width), both(1, width), both(8, rows),
         both(rows, 3 * width, dtype=bf16), both(z.heads, rows, rows, dtype=bf16),
         both(rows, width), both(rows, width),
         pltpu.VMEM((rows, rows), f32), pltpu.VMEM((rows, 3 * width), bf16),
         both(rows, width), both(rows, width), pltpu.VMEM((rows, width), bf16),
         pltpu.VMEM((rows, hidden), bf16),
         both(8 * width, LANES, dtype=bf16),
         pltpu.SemaphoreType.DMA((2, 7)), pltpu.SemaphoreType.DMA((2,))],
        12 * z.flops, "layers",
    )(sec, inputs, cotangent, series_id, item, variate, stats, jnp.asarray(table),
      *small, *own, *other)


def final(z, sec, inputs, series_id, stats, series, own_first, own_second, other_grad,
          own_out, other_out):
    own_count = z.own

    def own_step(i, s):
        return (jnp.clip(i - own_count * s[0], 0, own_count - 1), 0, 0)

    def other_step(i, s):
        return (jnp.clip(i - own_count * (1 - s[0]), 0, own_count - 1), 0, 0)

    own_spec = pl.BlockSpec((1, z.rows, z.width), own_step)
    other_spec = pl.BlockSpec((1, z.rows, z.width), other_step)
    return call(
        final_body, z.micro,
        [z.row, z.all_rows, by_step(z.stats), by_step(z.stats), own_spec, own_spec,
         other_spec, own_spec, other_spec],
        [z.row, z.row],
        [shape(z.micro, z.rows, z.width), shape(z.micro, z.rows, z.width, dtype=bf16)],
        [], 10**10, "final",
    )(sec, inputs, series_id, stats, series, own_first, own_second, other_grad, own_out, other_out)


def per_device(
    inputs,
    series_id,
    item_offset,
    variate_offset,
    cotangent,
    attention_gain,
    query_weight,
    key_weight,
    value_weight,
    out_weight,
    variate_bias,
    feed_gain,
    gate_weight,
    up_weight,
    down_weight,
):
    section = lax.axis_index("section")
    index = lax.axis_index("dp")
    count = lax.axis_size("dp")
    on_first = section == 0
    sec = section.astype(jnp.int32).reshape(1)
    heads = variate_bias.shape[1]
    z = Sizes(inputs, heads, down_weight.shape[1], count)
    width = z.width

    own_small = jnp.concatenate(
        [
            attention_gain,
            feed_gain,
            jnp.pad(variate_bias.reshape(1, 2 * heads), ((0, 0), (0, width - 2 * heads))),
        ],
        axis=0,
    ).astype(f32)
    own_small = jnp.pad(own_small, ((0, 5), (0, 0)))
    other_small = swapped(own_small)
    own = tuple(
        w[0]
        for w in (
            query_weight, key_weight, value_weight, out_weight, gate_weight, up_weight, down_weight
        )
    )
    other = tuple(swapped(w) for w in own)
    stats = series_stats(z, sec, inputs, series_id)
    steps = exchange_steps(count)[0]
    for k, step in enumerate(steps):
        if k == len(steps) - 1:
            stats, other, other_small = lax.optimization_barrier((stats, other, other_small))
        stats = merge_stats(stats, partner(stats, step, step, count), width)

    results, grad_one, standard_grad, series_sums, small_sums, *packs = layers(
        z, sec, inputs, cotangent, series_id, item_offset, variate_offset, stats,
        (own_small, other_small), own, other,
    )

    parts = [
        (k.astype(f32) + swapped(t).astype(f32)).astype(bf16)
        for k, t in zip(packs[:2], packs[2:])
    ]
    bits, turned = exchange_steps(count)
    near = list(zip(bits, turned))
    orders = (near, near[2:] + near[:2])
    rounds = len(bits)

    series_rows = z.own * z.stats[0] * z.stats[1] // LANES
    small = jnp.concatenate(
        [series_sums.reshape(-1, LANES), small_sums], axis=0
    )
    parts = halve(parts, orders, 0, section, index, count)[0]
    for k in range(1, rounds):
        if k < rounds - 1:
            parts, small = halve(parts, orders, k, section, index, count, small)
        else:
            parts, small = add_whole(parts, orders, k, count, small)
        small = small + partner(small, bits[rounds - k], bits[rounds - k], count)
    for k in reversed(range(1, rounds - 1)):
        if k == rounds - 2:
            parts, small = lax.optimization_barrier((parts, small))
            small = small + partner(small, bits[0], bits[0], count)
        if k == 1:
            parts, small, results, grad_one, standard_grad, stats = lax.optimization_barrier(
                (parts, small, results, grad_one, standard_grad, stats)
            )
            result_one, result_two = results[0], results[1]
            own_out = jnp.where(on_first, result_one, result_two)
            other_out = swapped(jnp.where(on_first, result_two, result_one))
            other_grad = swapped(jnp.where(on_first, grad_one, standard_grad.astype(bf16)))
            other_sums = swapped(small)
            other_stats = swapped(stats)
        parts = double(parts, orders, k, section, index, count)
    mine = small[:series_rows].reshape((z.own,) + z.stats)
    theirs = other_sums[:series_rows].reshape((z.own,) + z.stats)
    series_all = jnp.where(
        on_first, jnp.concatenate([mine, theirs]), jnp.concatenate([theirs, mine])
    )
    small = small[series_rows:] + other_sums[series_rows:]
    stats_all = jnp.where(
        on_first, jnp.concatenate([stats, other_stats]), jnp.concatenate([other_stats, stats])
    )
    sec_late, parts = lax.optimization_barrier((sec, parts))
    input_grads, section_output = final(
        z, sec_late, inputs, series_id, stats_all, series_all, standard_grad, grad_one, other_grad,
        own_out, other_out,
    )
    last_bits = jnp.stack([place(o[0], section, index) for o in orders]).astype(jnp.int32)
    others = [partner(p, *o[0], count) for p, o in zip(parts, orders)]
    vmem = pl.BlockSpec(memory_space=pltpu.VMEM)
    large = [shape(width, z.hidden)] * 2 + [shape(z.hidden, width)] + [shape(width, width)] * 4

    def unpack(held, halves, before):
        return pl.pallas_call(
            functools.partial(unpack_body, held, len(before)),
            in_specs=[SCALARS] + [vmem] * 2 + [HBM] * len(before),
            out_specs=[HBM] * 7,
            out_shape=large,
            input_output_aliases={3 + k: k for k in range(len(before))},
            scratch_shapes=[
                pltpu.VMEM((width, z.hidden), f32), pltpu.VMEM((width, z.hidden // 2), f32),
                pltpu.VMEM((z.hidden, width), f32), pltpu.VMEM((width, width), f32),
                pltpu.VMEM((width, width), f32), pltpu.SemaphoreType.DMA((4,)),
            ],
            compiler_params=pltpu.CompilerParams(vmem_limit_bytes=57 * 2**20),
            cost_estimate=pl.CostEstimate(flops=5 * 10**9, bytes_accessed=2**22, transcendentals=0),
            name="unpack",
        )(last_bits, *halves, *before)

    grad_gate, grad_up, grad_down, grad_query, grad_key, grad_value, grad_out = unpack(
        False, others, unpack(True, parts, ())
    )
    grad_attention_gain, grad_feed_gain, grad_bias = pl.pallas_call(
        unpack_small_body,
        in_specs=[SCALARS, vmem],
        out_shape=[shape(1, width)] * 2 + [shape(2, heads)],
        name="unpack_small",
    )(sec, small)
    return (
        section_output[None],
        input_grads[None],
        grad_attention_gain,
        grad_query[None],
        grad_key[None],
        grad_value[None],
        grad_out[None],
        grad_bias.T[None],
        grad_feed_gain,
        grad_gate[None],
        grad_up[None],
        grad_down[None],
    )


def solution(mesh):
    placed = (
        P(None, "dp", None),
        P(None, "dp"),
        P(None, "dp"),
        P(None, "dp"),
        P(None, "dp", None),
        P("section", None),
        P("section", None, None),
        P("section", None, None),
        P("section", None, None),
        P("section", None, None),
        P("section", None, None),
        P("section", None),
        P("section", None, None),
        P("section", None, None),
        P("section", None, None),
    )
    return jax.shard_map(
        per_device,
        mesh=mesh,
        in_specs=placed,
        out_specs=(
            P("section", None, "dp", None),
            P("section", None, "dp", None),
            P("section", None),
            P("section", None, None),
            P("section", None, None),
            P("section", None, None),
            P("section", None, None),
            P("section", None, None),
            P("section", None),
            P("section", None, None),
            P("section", None, None),
            P("section", None, None),
        ),
        check_vma=False,
    )
```

```python
import functools

import jax
import jax.numpy as jnp
import numpy as np
from jax import lax
from jax.experimental import pallas as pl
from jax.experimental.pallas import tpu as pltpu
from jax.sharding import PartitionSpec as P

HD = 64
BLOCK = 512
SER_DEV = 4
LANES = 128
CHUNK = 512
TILE = 256

norm_epsilon = 1e-05
scale_epsilon = 1e-05
masked_score = -1e30

f32 = jnp.float32
bf16 = jnp.bfloat16

AS_IS = (((1,), (0,)), ((), ()))
RIGHT_T = (((1,), (1,)), ((), ()))
LEFT_T = (((0,), (0,)), ((), ()))


def dot(left, right, dims=AS_IS):
    return lax.dot_general(left, right, dims, preferred_element_type=f32)


def column(row):
    return jnp.broadcast_to(row.astype(f32), (LANES, row.shape[1])).T


def lane_index(rows):
    return lax.broadcasted_iota(jnp.int32, (rows, LANES), 1)


def regroup(x):
    group = lane_index(x.shape[0]) // (HD // 2)
    return jnp.where(
        group == 1,
        pltpu.roll(x, LANES - HD // 2, 1),
        jnp.where(group == 2, pltpu.roll(x, HD // 2, 1), x),
    )


def turn(x, cosine, sine):
    return x * cosine + pltpu.roll(x, LANES // 2, 1) * sine


def turn_back(x, cosine, sine):
    return x * cosine - pltpu.roll(x, LANES // 2, 1) * sine


def inverse_rms(x):
    return lax.rsqrt(jnp.mean(x * x, axis=1, keepdims=True) + norm_epsilon)


def series_hits(sid_col, piece):
    return sid_col == (lane_index(sid_col.shape[0]) + piece * LANES).astype(f32)


def rows_of(hits, per_series):
    return jnp.sum(jnp.where(hits, per_series, 0.0), axis=1, keepdims=True)


def series_of(hits, per_row):
    return jnp.sum(jnp.where(hits, per_row, 0.0), axis=0, keepdims=True)


def stats_body(sec_ref, x_ref, sid_ref, out_ref):
    own, _, width = x_ref.shape
    pieces = out_ref.shape[-1] // LANES
    out_ref[...] = jnp.zeros_like(out_ref)
    for i in range(own):
        x = x_ref[i].astype(f32)
        sid_col = column(sid_ref[pl.ds(own * sec_ref[0] + i, 1), :])
        totals = jnp.sum(x, axis=1, keepdims=True)
        centre = jnp.zeros_like(totals)
        for piece in range(pieces):
            hits = series_hits(sid_col, piece)
            count = series_of(hits, 1.0)
            total = series_of(hits, totals)
            centre = centre + rows_of(hits, total / (jnp.maximum(count, 1.0) * width))
            out_ref[i, 0:1, piece * LANES : (piece + 1) * LANES] = count
            out_ref[i, 1:2, piece * LANES : (piece + 1) * LANES] = total
        centred = x - centre
        squares = jnp.sum(centred * centred, axis=1, keepdims=True)
        for piece in range(pieces):
            hits = series_hits(sid_col, piece)
            out_ref[i, 2:3, piece * LANES : (piece + 1) * LANES] = series_of(hits, squares)


def merge_stats(here, there, width):
    count_a, total_a, spread_a = here[:, 0:1], here[:, 1:2], here[:, 2:3]
    count_b, total_b, spread_b = there[:, 0:1], there[:, 1:2], there[:, 2:3]
    count = count_a + count_b
    gap = total_a / (jnp.maximum(count_a, 1.0) * width) - total_b / (
        jnp.maximum(count_b, 1.0) * width
    )
    weight = count_a * count_b * width / jnp.maximum(count, 1.0)
    row = lax.broadcasted_iota(jnp.int32, here.shape, 1)
    return jnp.where(
        row == 0,
        count,
        jnp.where(row == 1, total_a + total_b, spread_a + spread_b + gap * gap * weight),
    )


def centre_and_scale(stats, width):
    entries = jnp.maximum(stats[0:1], 1.0) * width
    centre = stats[1:2] / entries
    scaling = jnp.sqrt(stats[2:3] / entries + scale_epsilon)
    return entries, centre, scaling


class Weights:
    def __init__(self, section, own_refs, other_refs, big_ref, down_ref, sems):
        self.first_step = pl.program_id(0) == 0
        self.big_ref, self.down_ref = big_ref, down_ref
        self.own_refs, self.sems = own_refs, sems

        @pl.when(self.first_step)
        def _():
            for layer_of, refs in ((section, own_refs), (1 - section, other_refs)):
                for k, ref in enumerate(refs):
                    pltpu.make_async_copy(ref, self.target(layer_of, k), sems.at[layer_of, k]).start()

    def target(self, layer, k):
        if k == 6:
            return self.down_ref.at[layer]
        at = sum(ref.shape[1] for ref in self.own_refs[:k])
        return self.big_ref.at[layer, :, pl.ds(at, self.own_refs[k].shape[1])]

    def wait_here(self, layer, numbers):
        for k in numbers:
            pltpu.make_async_copy(
                self.own_refs[k], self.target(layer, k), self.sems.at[layer, k]
            ).wait()

    def wait_attention(self, layer):
        width = self.big_ref.shape[1]

        @pl.when(self.first_step)
        def _():
            self.wait_here(layer, (0, 1, 2, 3))
            for at in range(0, 2 * width, LANES):
                tile = self.big_ref[layer, :, at : at + LANES].astype(f32)
                self.big_ref[layer, :, at : at + LANES] = regroup(tile).astype(bf16)

    def wait_feed(self, layer):
        @pl.when(self.first_step)
        def _():
            self.wait_here(layer, (4, 5, 6))


def sigmoid(x):
    return 0.5 * jnp.tanh(0.5 * x) + 0.5


def in_head(half, lanes, grouped):
    if grouped:
        return (lanes % HD) // (HD // 2) == half
    return lanes // HD == half


def row_index(rows):
    return lax.broadcasted_iota(jnp.int32, (LANES, rows), 0)


class Block:
    def __init__(self, cosine, sine, item_col, var_col, var_row, same_ref):
        rows = cosine.shape[0]
        self.cosine, self.sine, self.same_ref = cosine, sine, same_ref
        row = var_row.astype(f32)
        for at in range(0, rows, LANES):
            same_ref[:, at : at + LANES] = jnp.where(var_col == row[:, at : at + LANES], 1.0, 0.0)
        lane = lane_index(rows)
        second = jnp.where(item_col > 0.0, 1.0, 0.0)
        self.item_q = jnp.where(
            lane == 0, second, jnp.where(lane == 1, 1.0 - second, 0.0)
        ).astype(bf16)
        self.item_k = jnp.where(
            lane == 0,
            (1.0 - second) * masked_score,
            jnp.where(lane == 1, second * masked_score, 0.0),
        ).astype(bf16)


def attention_forward(layer, hidden, gains, block, bias, weights, saved):
    qkv_ref, prob_ref, inv_ref, mixed_ref = (ref.at[layer] for ref in saved)
    rows, width = hidden.shape
    pairs = width // LANES
    tiles = rows // TILE
    big_ref = weights.big_ref.at[layer]
    normed = (hidden * inverse_rms(hidden) * gains).astype(bf16)
    weights.wait_attention(layer)
    lane = lane_index(rows)
    first_rows = row_index(rows) < HD
    extra = lax.broadcasted_iota(jnp.int32, (16, rows), 0)

    projected = dot(normed, big_ref[:, : 3 * width])

    def project(p):
        at = p * LANES
        q = turn(projected[:, at : at + LANES], block.cosine, block.sine)
        k = turn(projected[:, width + at : width + at + LANES], block.cosine, block.sine)
        v = projected[:, 2 * width + at : 2 * width + at + LANES]
        qkv_ref[:, at : at + LANES] = (q * HD**-0.5).astype(bf16)
        qkv_ref[:, width + at : width + at + LANES] = k.astype(bf16)
        qkv_ref[:, 2 * width + at : 2 * width + at + LANES] = v.astype(bf16)

    def operands(p):
        at = p * LANES
        q_pair = qkv_ref[:, at : at + LANES]
        k_aug = jnp.concatenate([qkv_ref[:, width + at : width + at + LANES], block.item_k], axis=1)
        v_turned = qkv_ref[:, 2 * width + at : 2 * width + at + LANES].T
        heads = []
        for half in range(2):
            q_aug = jnp.concatenate(
                [jnp.where(in_head(half, lane, True), q_pair, 0.0).astype(bf16), block.item_q],
                axis=1,
            )
            own_rows = first_rows if half == 0 else jnp.logical_not(first_rows)
            v_aug = jnp.concatenate(
                [
                    jnp.where(own_rows, v_turned, 0.0).astype(bf16),
                    jnp.where(extra == half, 1.0, 0.0).astype(bf16),
                ],
                axis=0,
            )
            heads.append((q_aug, v_aug))
        return k_aug, heads

    prepared = {}

    def scores_of(p, half, t):
        if p not in prepared:
            project(p)
            prepared[p] = operands(p)
        k_aug, heads = prepared[p]
        return dot(k_aug, heads[half][0][t * TILE : (t + 1) * TILE, :], RIGHT_T)

    order = [(p, half, t) for p in range(pairs) for half in range(2) for t in range(tiles)]
    attended = {}
    scores = scores_of(*order[0])
    for n, (p, half, t) in enumerate(order):
        following = scores_of(*order[n + 1]) if n + 1 < len(order) else None
        head = 2 * p + half
        cols = slice(t * TILE, (t + 1) * TILE)
        gap = bias[0:1, 2 * head : 2 * head + 1] - bias[0:1, 2 * head + 1 : 2 * head + 2]
        biased = scores + block.same_ref[:, cols] * gap
        peak = jnp.max(biased, axis=0, keepdims=True)
        prob = jnp.exp(biased - peak).astype(bf16)
        prob_ref[head, :, cols] = prob
        part = dot(prepared[p][1][half][1], prob)
        attended[p, t] = part if half == 0 else attended[p, t] + part
        if half == 1:
            sums = attended.pop((p, t))
            own_rows = row_index(TILE) < HD
            inv = jnp.where(
                own_rows, 1.0 / sums[LANES : LANES + 1], 1.0 / sums[LANES + 1 : LANES + 2]
            )
            inv_ref[cols, p * LANES : (p + 1) * LANES] = inv.T
            mixed_ref[cols, p * LANES : (p + 1) * LANES] = (sums[:LANES] * inv).T
        scores = following
    return hidden + dot(mixed_ref[...].astype(bf16), big_ref[:, 3 * width : 4 * width])


def feed_forward(layer, middle, gains, weights):
    big_ref, down_ref = weights.big_ref.at[layer], weights.down_ref.at[layer]
    width = middle.shape[1]
    hidden = down_ref.shape[0]
    feed = (middle * inverse_rms(middle) * gains).astype(bf16)
    total = middle
    for at in range(0, hidden, CHUNK):
        gate = dot(feed, big_ref[:, 4 * width + at : 4 * width + at + CHUNK])
        up = dot(feed, big_ref[:, 4 * width + hidden + at : 4 * width + hidden + at + CHUNK])
        active = (gate * sigmoid(gate) * up).astype(bf16)
        total = total + dot(active, down_ref[at : at + CHUNK, :])
    return total.astype(bf16)


def feed_backward(layer, middle, gains, grad_low, weights, accs, active_ref):
    gate_acc, up_acc, down_acc, gain_acc = (acc.at[layer] for acc in accs)
    big_ref, down_ref = weights.big_ref.at[layer], weights.down_ref.at[layer]
    width = middle.shape[1]
    hidden = down_ref.shape[0]
    inverse = inverse_rms(middle)
    feed = (middle * inverse * gains).astype(bf16)
    feed_t = feed.T
    feed_grad = jnp.zeros(middle.shape, f32)
    for at in range(0, hidden, CHUNK):
        gate_w = big_ref[:, 4 * width + at : 4 * width + at + CHUNK]
        up_w = big_ref[:, 4 * width + hidden + at : 4 * width + hidden + at + CHUNK]
        down_w = down_ref[at : at + CHUNK, :]
        gate = dot(feed, gate_w)
        up = dot(feed, up_w)
        act_grad = dot(grad_low, down_w, RIGHT_T)
        gated = sigmoid(gate)
        swish = gate * gated
        active = (swish * up).astype(bf16)
        active_ref[:, at : at + CHUNK] = active
        gate_grad = (act_grad * up * (gated + swish * (1.0 - gated))).astype(bf16)
        up_grad = (act_grad * swish).astype(bf16)
        feed_grad = feed_grad + dot(gate_grad, gate_w, RIGHT_T) + dot(up_grad, up_w, RIGHT_T)
        gate_acc[:, at : at + CHUNK] += dot(feed_t, gate_grad)
        up_acc[:, at : at + CHUNK] += dot(feed_t, up_grad)
        down_acc[at : at + CHUNK, :] += dot(active, grad_low, LEFT_T)
    scaled = feed_grad * gains
    gain_acc[...] += jnp.sum(feed_grad * middle * inverse, axis=0, keepdims=True)
    return (
        grad_low.astype(f32)
        + inverse * scaled
        - middle * (inverse * inverse * inverse) * jnp.mean(scaled * middle, axis=1, keepdims=True)
    )


def attention_backward(layer, middle_grad, hidden, gains, block, weights, saved, grads_ref, accs):
    qkv_ref, prob_ref, inv_ref, mixed_ref = (ref.at[layer] for ref in saved)
    qkv_acc, out_acc, gain_acc, bias_acc = (acc.at[layer] for acc in accs)
    rows, width = hidden.shape
    pairs = width // LANES
    tiles = rows // TILE
    big_ref = weights.big_ref.at[layer]
    mix_grad = middle_grad.astype(bf16)
    att_grad = dot(mix_grad, big_ref[:, 3 * width : 4 * width], RIGHT_T).astype(bf16)
    lane = lane_index(rows)
    ones_four = jnp.where(lane < 4, 1.0, 0.0).astype(bf16)
    source = lax.broadcasted_iota(jnp.int32, (2 * LANES, LANES), 0) % LANES // HD
    target = lax.broadcasted_iota(jnp.int32, (2 * LANES, LANES), 1)
    gather = jnp.where((target // 2 == source) & (target < 4), 1.0, 0.0).astype(bf16)

    def operands(p):
        at = p * LANES
        q_pair = qkv_ref[:, at : at + LANES]
        k_turned = qkv_ref[:, width + at : width + at + LANES].T
        v_aug = jnp.concatenate(
            [qkv_ref[:, 2 * width + at : 2 * width + at + LANES], ones_four], axis=1
        )
        grad_pair = (att_grad[:, at : at + LANES].astype(f32) * inv_ref[:, at : at + LANES]).astype(
            bf16
        )
        product = grad_pair.astype(f32) * mixed_ref[:, at : at + LANES]
        high = product.astype(bf16)
        low = (product - high.astype(f32)).astype(bf16)
        inner = dot(jnp.concatenate([high, low], axis=1), gather)
        inner_high = inner.astype(bf16).astype(f32)
        tail = jnp.where(lane % 2 == 0, -inner_high, inner_high - inner)
        heads = []
        for half in range(2):
            grad_low = jnp.where(in_head(half, lane, False), grad_pair, 0.0).astype(bf16)
            tail_low = jnp.where(lane // 2 == half, tail, 0.0).astype(bf16)
            q_mine = jnp.where(in_head(half, lane, True), q_pair, 0.0).astype(bf16)
            low = half * (HD // 2)
            k_mine = jnp.concatenate(
                [k_turned[low : low + HD // 2], k_turned[HD + low : HD + low + HD // 2]], axis=0
            )
            heads.append(
                (jnp.concatenate([grad_low, tail_low], axis=1), grad_low, q_mine, k_mine)
            )
        return v_aug, heads

    prepared = {}

    def prob_grad_of(p, half, t):
        if p not in prepared:
            prepared[p] = operands(p)
        v_aug, heads = prepared[p]
        return dot(v_aug, heads[half][0][t * TILE : (t + 1) * TILE, :], RIGHT_T)

    order = [(p, half, t) for p in range(pairs) for half in range(2) for t in range(tiles)]
    value_grad = key_grad = None
    query_grad = {}
    prob_grad = prob_grad_of(*order[0])
    for n, (p, half, t) in enumerate(order):
        following = prob_grad_of(*order[n + 1]) if n + 1 < len(order) else None
        head = 2 * p + half
        cols = slice(t * TILE, (t + 1) * TILE)
        at = p * LANES
        _, grad_low, q_mine, k_mine = prepared[p][1][half]
        prob = prob_ref[head, :, cols]
        score_grad = prob.astype(f32) * prob_grad
        bias_acc[head : head + 1, cols] += jnp.sum(
            score_grad * block.same_ref[:, cols], axis=0, keepdims=True
        )
        score_low = score_grad.astype(bf16)
        part_v = dot(prob, grad_low[cols, :])
        part_k = dot(score_low, q_mine[cols, :])
        part_q = dot(k_mine, score_low)
        value_grad = part_v if value_grad is None else value_grad + part_v
        key_grad = part_k if key_grad is None else key_grad + part_k
        query_grad[t, half] = part_q
        if half == 1:
            one, two = query_grad.pop((t, 0)), query_grad.pop((t, 1))
            mid = HD // 2
            back = jnp.concatenate([one[:mid], two[:mid], one[mid:], two[mid:]], axis=0).T * HD**-0.5
            grads_ref[cols, at : at + LANES] = turn_back(
                back, block.cosine[cols, :], block.sine[cols, :]
            ).astype(bf16)
        if half == 1 and t == tiles - 1:
            grads_ref[:, width + at : width + at + LANES] = turn_back(
                key_grad, block.cosine, block.sine
            ).astype(bf16)
            grads_ref[:, 2 * width + at : 2 * width + at + LANES] = value_grad.astype(bf16)
            value_grad = key_grad = None
        prob_grad = following
    out_acc[...] += dot(mixed_ref[...].astype(bf16), mix_grad, LEFT_T)
    inverse = inverse_rms(hidden)
    normed = (hidden * inverse * gains).astype(bf16)
    normed_grad = dot(grads_ref[...], big_ref[:, : 3 * width], RIGHT_T)
    qkv_acc[...] += dot(normed, grads_ref[...], LEFT_T)
    scaled = normed_grad * gains
    gain_acc[...] += jnp.sum(normed_grad * hidden * inverse, axis=0, keepdims=True)
    return (
        middle_grad
        + inverse * scaled
        - hidden * (inverse * inverse * inverse) * jnp.mean(scaled * hidden, axis=1, keepdims=True)
    )


def column_tiles(acc_ref):
    return [acc_ref[:, at : at + LANES] for at in range(0, acc_ref.shape[1], LANES)]


class Packer:
    def __init__(self, stage_ref, sems, kept_refs, sent_refs):
        self.stage_ref, self.sems = stage_ref, sems
        self.kept_refs, self.sent_refs = kept_refs, sent_refs
        self.sent = []

    def copy(self, out_ref, slot, count):
        source = self.stage_ref.at[slot, pl.ds(0, count)]
        return pltpu.make_async_copy(source, out_ref, self.sems.at[slot])

    def send(self, keep, part, start, tiles):
        slot = len(self.sent) % 2
        if len(self.sent) >= 2:
            self.wait(2)
        at = 0
        for tile in tiles:
            self.stage_ref[slot, at : at + tile.shape[0], :] = tile.astype(bf16)
            at += tile.shape[0]
        where = pl.ds(start, at)

        @pl.when(keep)
        def _():
            self.copy(self.kept_refs[part].at[where], slot, at).start()

        @pl.when(jnp.logical_not(keep))
        def _():
            self.copy(self.sent_refs[part].at[where], slot, at).start()

        self.sent.append((self.kept_refs[part].at[where], slot, at))

    def wait(self, back):
        self.copy(*self.sent[-back]).wait()

    def finish(self):
        self.wait(2)
        self.wait(1)


def layers_body(
    sec_ref, x_ref, cotangent_ref, sid_ref, item_ref, var_ref, stats_ref, table_ref,
    own_small_ref, other_small_ref, *refs
):
    own_refs, other_refs, refs = refs[:7], refs[7:14], refs[14:]
    results_ref, grad_one_ref, grad_zero_ref, series_ref, small_ref = refs[:5]
    kept_refs, sent_refs, refs = refs[5:7], refs[7:9], refs[9:]
    big_ref, down_ref, refs = refs[0], refs[1], refs[2:]
    feed_accs, attention_accs, saved, refs = refs[:4], refs[4:8], refs[8:12], refs[12:]
    same_ref, grads_ref, hidden_ref, middle_ref, grad_ref, active_ref, stage_ref, *refs = refs
    sems, stage_sems = refs

    i = pl.program_id(0)
    last = i == pl.num_programs(0) - 1
    m = pl.num_programs(0) * sec_ref[0] + i
    weights = Weights(sec_ref[0], own_refs, other_refs, big_ref, down_ref, sems)

    @pl.when(i == 0)
    def _():
        for acc in feed_accs + attention_accs:
            acc[...] = jnp.zeros_like(acc)

    x = x_ref[0].astype(f32)
    rows, width = x.shape
    var_row = var_ref[pl.ds(m, 1), :]
    var_col = column(var_row)
    sid_col = column(sid_ref[pl.ds(m, 1), :])
    pieces = stats_ref.shape[-1] // LANES

    time = lax.broadcasted_iota(jnp.int32, (rows, LANES), 0).astype(f32) - var_col
    cosine = sine = jnp.zeros((rows, LANES), f32)
    for at in range(0, rows, LANES):
        hot = jnp.where(time == (lane_index(rows) + at).astype(f32), 1.0, 0.0).astype(bf16)
        found = dot(hot, table_ref[at : at + LANES, :])
        cosine = cosine + found[:, :LANES] + found[:, LANES : 2 * LANES]
        sine = sine + found[:, 2 * LANES : 3 * LANES] + found[:, 3 * LANES :]
    block = Block(cosine, sine, column(item_ref[pl.ds(m, 1), :]), var_col, var_row, same_ref)

    _, centre, scaling = centre_and_scale(stats_ref[0], width)
    centre_rows = scale_rows = 0.0
    for piece in range(pieces):
        hits = series_hits(sid_col, piece)
        part = slice(piece * LANES, (piece + 1) * LANES)
        centre_rows = centre_rows + rows_of(hits, centre[:, part])
        scale_rows = scale_rows + rows_of(hits, scaling[:, part])
    hidden_ref[0] = (x - centre_rows) / scale_rows
    grad_ref[...] = cotangent_ref[0]

    def small_row(layer, k):
        return jnp.where(
            sec_ref[0] == layer, own_small_ref[k : k + 1, :], other_small_ref[k : k + 1, :]
        )

    def forward(layer, _):
        middle = attention_forward(
            layer, hidden_ref[layer], small_row(layer, 0), block, small_row(layer, 2), weights,
            saved,
        )
        middle_ref[layer] = middle
        weights.wait_feed(layer)

        @pl.when(layer == 0)
        def _():
            result = feed_forward(layer, middle_ref[0], small_row(layer, 1), weights)
            results_ref[0, 0] = result
            hidden_ref[1] = result.astype(f32)

    def send(layer):
        packer = Packer(stage_ref, stage_sems, kept_refs, sent_refs)
        keep = sec_ref[0] == layer
        gate, up, down = (column_tiles(acc.at[layer]) for acc in feed_accs[:3])
        queries = column_tiles(attention_accs[0].at[layer])
        turned = [regroup(tile) for tile in queries[:6]]
        start = 0
        for tiles in (gate, up, down):
            packer.send(keep, 0, start, tiles)
            start += sum(tile.shape[0] for tile in tiles)
        packer.send(keep, 1, 0, turned)
        packer.send(keep, 1, width * 6, queries[6:] + column_tiles(attention_accs[1].at[layer]))
        packer.finish()

    def backward(step, _):
        layer = 1 - step
        middle_grad = feed_backward(
            layer, middle_ref[layer], small_row(layer, 1), grad_ref[...], weights, feed_accs,
            active_ref,
        )

        @pl.when(layer == 1)
        def _():
            total = middle_ref[1] + dot(active_ref[...], weights.down_ref[1])
            results_ref[1, 0] = total.astype(bf16)

        hidden_grad = attention_backward(
            layer, middle_grad, hidden_ref[layer], small_row(layer, 0), block, weights,
            saved, grads_ref, attention_accs,
        )
        grad_ref[...] = hidden_grad.astype(bf16)
        grad_zero_ref[0] = hidden_grad

        @pl.when(layer == 1)
        def _():
            grad_one_ref[0] = hidden_grad.astype(bf16)

        @pl.when(last)
        def _():
            send(layer)

    lax.fori_loop(0, 2, forward, None)
    lax.fori_loop(0, 2, backward, None)

    standard, hidden_grad = hidden_ref[0], grad_zero_ref[0]
    grad_rows = jnp.sum(hidden_grad, axis=1, keepdims=True)
    cross_rows = jnp.sum(hidden_grad * standard, axis=1, keepdims=True)
    standard_rows = jnp.sum(standard, axis=1, keepdims=True)
    series_ref[0] = jnp.zeros(series_ref.shape[1:], f32)
    for piece in range(pieces):
        hits = series_hits(sid_col, piece)
        part = slice(piece * LANES, (piece + 1) * LANES)
        series_ref[0, 0:1, part] = series_of(hits, grad_rows)
        series_ref[0, 1:2, part] = series_of(hits, cross_rows)
        series_ref[0, 2:3, part] = series_of(hits, standard_rows)

    @pl.when(last)
    def _():
        small_ref[...] = jnp.zeros_like(small_ref)
        for layer in range(2):
            base = 24 * layer
            for k in range(width // LANES):
                cols = slice(k * LANES, (k + 1) * LANES)
                small_ref[base + k : base + k + 1, :] = attention_accs[2][layer, :, cols]
                small_ref[base + 16 + k : base + 17 + k, :] = feed_accs[3][layer, :, cols]
            bias_sums = jnp.sum(attention_accs[3][layer], axis=1, keepdims=True)
            small_ref[base + 8 : base + 16, :] = jnp.broadcast_to(bias_sums, (8, LANES))


def final_body(
    sec_ref, x_ref, sid_ref, stats_ref, series_ref, own_first, own_second, other_grad,
    own_out, other_out, out_ref, grads_ref,
):
    i = pl.program_id(0)
    sec = sec_ref[0]
    own = (i // (pl.num_programs(0) // 2)) == sec
    grads_ref[0] = jnp.where(own, own_out[0], other_out[0])
    grad = jnp.where(
        own,
        jnp.where(sec == 0, own_first[0], own_second[0].astype(f32)),
        other_grad[0].astype(f32),
    )

    @pl.when(sec == 0)
    def _():
        x = x_ref[0].astype(f32)
        width = x.shape[1]
        entries, centre, scaling = centre_and_scale(stats_ref[0], width)
        sums = series_ref[0]
        cross = sums[1:2] * scaling
        spread_grad = -cross / (2.0 * scaling * scaling * scaling * entries)
        mean_grad = sums[0:1] / scaling + 2.0 * spread_grad * (sums[2:3] * scaling)
        tables = (centre, 1.0 / scaling, 2.0 * spread_grad, mean_grad / entries)
        sid_col = column(sid_ref[pl.ds(i, 1), :])
        looked = [0.0, 0.0, 0.0, 0.0]
        for piece in range(stats_ref.shape[-1] // LANES):
            hits = series_hits(sid_col, piece)
            part = slice(piece * LANES, (piece + 1) * LANES)
            for k in range(4):
                looked[k] = looked[k] + rows_of(hits, tables[k][:, part])
        out_ref[0] = grad * looked[1] + (x - looked[0]) * looked[2] - looked[3]

    @pl.when(sec != 0)
    def _():
        out_ref[0] = grad


def unpack_body(held, count, bit_ref, feed_ref, attention_ref, *refs):
    refs = refs[count:]
    gate, up, down, query, key, value, out = refs[:7]
    gate_at, up_at, down_at, one_at, two_at, sems = refs[7:]
    half_up = up_at.shape[1]

    def leave(k, source_ref, at, scratch_ref, target_ref):
        rows = scratch_ref.shape[0]
        for col in range(0, scratch_ref.shape[1], LANES):
            scratch_ref[:, col : col + LANES] = source_ref[at : at + rows, :].astype(f32)
            at += rows
        copy = pltpu.make_async_copy(scratch_ref, target_ref, sems.at[k])
        copy.start()
        return copy

    gate_rows = gate_at.shape[0] * gate_at.shape[1] // LANES
    up_rows = up_at.shape[0] * half_up // LANES
    one_rows = one_at.shape[0] * one_at.shape[1] // LANES

    def feed(low):
        if low:
            return [
                leave(0, feed_ref, 0, gate_at, gate),
                leave(1, feed_ref, gate_rows, up_at, up.at[:, pl.ds(0, half_up)]),
            ]
        return [
            leave(0, feed_ref, up_rows, down_at, down),
            leave(1, feed_ref, 0, up_at, up.at[:, pl.ds(half_up, half_up)]),
        ]

    def attention(low):
        first, second = (query, key) if low else (value, out)
        return [
            leave(2, attention_ref, 0, one_at, first),
            leave(3, attention_ref, one_rows, two_at, second),
        ]

    for feed_low in range(2):
        for attention_low in range(2):
            here = (bit_ref[0] == (1 - feed_low if held else feed_low)) & (
                bit_ref[1] == (1 - attention_low if held else attention_low)
            )

            @pl.when(here)
            def _(feed_low=feed_low, attention_low=attention_low):
                for copy in feed(feed_low) + attention(attention_low):
                    copy.wait()


def unpack_small_body(sec_ref, small_ref, attention_gain_ref, feed_gain_ref, bias_ref):
    base = 24 * sec_ref[0]
    for k in range(attention_gain_ref.shape[1] // LANES):
        cols = slice(k * LANES, (k + 1) * LANES)
        attention_gain_ref[:, cols] = small_ref[pl.ds(base + k, 1), :]
        feed_gain_ref[:, cols] = small_ref[pl.ds(base + 16 + k, 1), :]
    same = small_ref[pl.ds(base + 8, 8), :].T[0:1, : bias_ref.shape[1]]
    bias_ref[0:1, :] = same
    bias_ref[1:2, :] = -same


def swapped(x):
    return lax.ppermute(x, "section", [(0, 1), (1, 0)])


def to_section(x, section):
    return lax.ppermute(x, "section", [(1 - section, section)])


def exchange_steps(count):
    bits = []
    step = 1
    while step < count:
        bits.append(step)
        step *= 2
    other = list(bits)
    for k in range(0, len(bits) - 1, 2):
        other[k], other[k + 1] = bits[k + 1], bits[k]
    return bits, other


def partner(x, by_first, by_second, count):
    pairs = [(i, i ^ by_first) for i in range(count)]
    pairs += [(count + i, count + (i ^ by_second)) for i in range(count)]
    return lax.ppermute(x, ("section", "dp"), pairs)


def place(steps, section, index):
    step = jnp.where(section == 0, *steps)
    return (index // step) % 2


def halve(parts, orders, k, section, index, count, *more):
    keeps, sends = [], []
    for current, order in zip(parts, orders):
        bit = place(order[k], section, index)
        half = current.shape[0] // 2
        keeps.append(lax.dynamic_slice_in_dim(current, bit * half, half, 0))
        sends.append(lax.dynamic_slice_in_dim(current, (1 - bit) * half, half, 0))
    sends, keeps, more = lax.optimization_barrier((sends, keeps, more))
    got = [partner(send, *order[k], count) for send, order in zip(sends, orders)]
    parts = [(a.astype(f32) + b.astype(f32)).astype(bf16) for a, b in zip(keeps, got)]
    return (parts, *more)


def add_whole(parts, orders, k, count, *more):
    parts, more = lax.optimization_barrier((parts, more))
    got = [partner(part, *order[k], count) for part, order in zip(parts, orders)]
    parts = [(a.astype(f32) + b.astype(f32)).astype(bf16) for a, b in zip(parts, got)]
    return (parts, *more)


def double(parts, orders, k, section, index, count):
    parts = lax.optimization_barrier(parts)
    result = []
    for current, order in zip(parts, orders):
        bit = place(order[k], section, index)
        got = partner(current, *order[k], count)
        low = jnp.where(bit == 0, current, got)
        high = jnp.where(bit == 0, got, current)
        result.append(jnp.concatenate([low, high], axis=0))
    return result


HBM = pl.BlockSpec(memory_space=pl.ANY)
SCALARS = pl.BlockSpec(memory_space=pltpu.SMEM)


def whole_block(shape):
    return pl.BlockSpec(shape, lambda i, *_: (0,) * len(shape))


def by_step(shape):
    return pl.BlockSpec((1,) + shape, lambda i, *_: (i,) + (0,) * len(shape))


def by_batch(shape, own):
    return pl.BlockSpec((1,) + shape, lambda i, s: (own * s[0] + i,) + (0,) * len(shape))


def call(body, grid, in_specs, out_specs, out_shapes, scratch, flops, name):
    return pl.pallas_call(
        body,
        grid_spec=pltpu.PrefetchScalarGridSpec(
            num_scalar_prefetch=1,
            grid=(grid,),
            in_specs=in_specs,
            out_specs=out_specs,
            scratch_shapes=scratch,
        ),
        out_shape=out_shapes,
        compiler_params=pltpu.CompilerParams(vmem_limit_bytes=57 * 2**20),
        cost_estimate=pl.CostEstimate(flops=flops, bytes_accessed=2**22, transcendentals=0),
        name=name,
    )


def shape(*dims, dtype=f32):
    return jax.ShapeDtypeStruct(dims, dtype)


class Sizes:
    def __init__(self, inputs, heads, hidden, count):
        self.micro, self.rows, self.width = inputs.shape
        self.own = self.micro // 2
        self.heads, self.hidden, self.count = heads, hidden, count
        rows, width, own = self.rows, self.width, self.own
        self.stats = (8, -(-SER_DEV * count // LANES) * LANES)
        self.all_rows = whole_block((self.micro, rows))
        self.row = by_step((rows, width))
        self.row_batch = by_batch((rows, width), own)
        self.gain = whole_block((8, width))
        self.row_shape = shape(own, rows, width)
        self.low_shape = shape(own, rows, width, dtype=bf16)
        self.flops = 2 * rows * (4 * width * width + 3 * width * hidden) * own


def rotary_table(rows):
    lane = np.arange(LANES)
    frequency = np.float32(10000.0) ** (
        -(lane % (HD // 2)).astype(np.float32) * np.float32(2.0 / HD)
    )
    angle = np.arange(rows, dtype=np.float32)[:, None] * frequency[None, :].astype(np.float32)
    cosine = np.cos(angle.astype(np.float64))
    sine = np.sin(angle.astype(np.float64)) * np.where(lane < HD, -1.0, 1.0)
    parts = []
    for values in (cosine, sine):
        high = values.astype(jnp.bfloat16)
        parts += [high, (values - high.astype(np.float64)).astype(jnp.bfloat16)]
    return np.concatenate(parts, axis=1)


def series_stats(z, sec, inputs, series_id):
    return call(
        stats_body, 1,
        [pl.BlockSpec((z.own, z.rows, z.width), lambda i, s: (s[0], 0, 0)), z.all_rows],
        whole_block((z.own,) + z.stats), shape(z.own, *z.stats),
        [], 10**7, "series_stats",
    )(sec, inputs, series_id)


def layers(z, sec, inputs, cotangent, series_id, item, variate, stats, small, own, other):
    table = rotary_table(z.rows)
    rows, width, hidden = z.rows, z.width, z.hidden
    parts = [
        shape(3 * width * hidden // LANES, LANES, dtype=bf16),
        shape(4 * width * width // LANES, LANES, dtype=bf16),
    ]

    def both(*dims, dtype=f32):
        return pltpu.VMEM((2,) + dims, dtype)

    return call(
        layers_body, z.own,
        [z.row_batch, z.row_batch, z.all_rows, z.all_rows, z.all_rows, by_step(z.stats),
         whole_block(table.shape), whole_block((8, width)), whole_block((8, width))] + [HBM] * 14,
        [pl.BlockSpec((2, 1, rows, width), lambda i, *_: (0, i, 0, 0)), z.row, z.row,
         by_step(z.stats), whole_block((48, LANES))] + [HBM] * 4,
        [shape(2, z.own, rows, width, dtype=bf16), z.low_shape, z.row_shape,
         shape(z.own, *z.stats), shape(48, LANES)] + parts * 2,
        [both(width, 4 * width + 2 * hidden, dtype=bf16), both(hidden, width, dtype=bf16),
         both(width, hidden), both(width, hidden), both(hidden, width), both(1, width),
         both(width, 3 * width), both(width, width), both(1, width), both(8, rows),
         both(rows, 3 * width, dtype=bf16), both(z.heads, rows, rows, dtype=bf16),
         both(rows, width), both(rows, width),
         pltpu.VMEM((rows, rows), f32), pltpu.VMEM((rows, 3 * width), bf16),
         both(rows, width), both(rows, width), pltpu.VMEM((rows, width), bf16),
         pltpu.VMEM((rows, hidden), bf16),
         both(8 * width, LANES, dtype=bf16),
         pltpu.SemaphoreType.DMA((2, 7)), pltpu.SemaphoreType.DMA((2,))],
        12 * z.flops, "layers",
    )(sec, inputs, cotangent, series_id, item, variate, stats, jnp.asarray(table),
      *small, *own, *other)


def final(z, sec, inputs, series_id, stats, series, own_first, own_second, other_grad,
          own_out, other_out):
    own_count = z.own

    def own_step(i, s):
        return (jnp.clip(i - own_count * s[0], 0, own_count - 1), 0, 0)

    def other_step(i, s):
        return (jnp.clip(i - own_count * (1 - s[0]), 0, own_count - 1), 0, 0)

    own_spec = pl.BlockSpec((1, z.rows, z.width), own_step)
    other_spec = pl.BlockSpec((1, z.rows, z.width), other_step)
    return call(
        final_body, z.micro,
        [z.row, z.all_rows, by_step(z.stats), by_step(z.stats), own_spec, own_spec,
         other_spec, own_spec, other_spec],
        [z.row, z.row],
        [shape(z.micro, z.rows, z.width), shape(z.micro, z.rows, z.width, dtype=bf16)],
        [], 10**10, "final",
    )(sec, inputs, series_id, stats, series, own_first, own_second, other_grad, own_out, other_out)


def per_device(
    inputs,
    series_id,
    item_offset,
    variate_offset,
    cotangent,
    attention_gain,
    query_weight,
    key_weight,
    value_weight,
    out_weight,
    variate_bias,
    feed_gain,
    gate_weight,
    up_weight,
    down_weight,
):
    section = lax.axis_index("section")
    index = lax.axis_index("dp")
    count = lax.axis_size("dp")
    on_first = section == 0
    sec = section.astype(jnp.int32).reshape(1)
    heads = variate_bias.shape[1]
    z = Sizes(inputs, heads, down_weight.shape[1], count)
    width = z.width

    own_small = jnp.concatenate(
        [
            attention_gain,
            feed_gain,
            jnp.pad(variate_bias.reshape(1, 2 * heads), ((0, 0), (0, width - 2 * heads))),
        ],
        axis=0,
    ).astype(f32)
    own_small = jnp.pad(own_small, ((0, 5), (0, 0)))
    other_small = swapped(own_small)
    own = tuple(
        w[0]
        for w in (
            query_weight, key_weight, value_weight, out_weight, gate_weight, up_weight, down_weight
        )
    )
    other = tuple(swapped(w) for w in own)
    stats = series_stats(z, sec, inputs, series_id)
    steps = exchange_steps(count)[0]
    for k, step in enumerate(steps):
        if k == len(steps) - 1:
            stats, other, other_small = lax.optimization_barrier((stats, other, other_small))
        stats = merge_stats(stats, partner(stats, step, step, count), width)

    results, grad_one, standard_grad, series_sums, small_sums, *packs = layers(
        z, sec, inputs, cotangent, series_id, item_offset, variate_offset, stats,
        (own_small, other_small), own, other,
    )

    parts = [
        (k.astype(f32) + swapped(t).astype(f32)).astype(bf16)
        for k, t in zip(packs[:2], packs[2:])
    ]
    bits, turned = exchange_steps(count)
    near = list(zip(bits, turned))
    orders = (near, near[2:] + near[:2])
    rounds = len(bits)

    series_rows = z.own * z.stats[0] * z.stats[1] // LANES
    small = jnp.concatenate(
        [series_sums.reshape(-1, LANES), small_sums], axis=0
    )
    parts = halve(parts, orders, 0, section, index, count)[0]
    for k in range(1, rounds):
        if k < rounds - 1:
            parts, small = halve(parts, orders, k, section, index, count, small)
        else:
            parts, stats = lax.optimization_barrier((parts, stats))
            parts, other_stats = lax.optimization_barrier((parts, swapped(stats)))
            parts, small = add_whole(parts, orders, k, count, small)
        small = small + partner(small, bits[rounds - k], bits[rounds - k], count)
    for k in reversed(range(1, rounds - 1)):
        if k == rounds - 2:
            parts, small = lax.optimization_barrier((parts, small))
            small = small + partner(small, bits[0], bits[0], count)
        if k == 1:
            parts, small, results, grad_one, standard_grad = lax.optimization_barrier(
                (parts, small, results, grad_one, standard_grad)
            )
            result_one, result_two = results[0], results[1]
            own_out = jnp.where(on_first, result_one, result_two)
            other_out = swapped(jnp.where(on_first, result_two, result_one))
            other_grad = swapped(jnp.where(on_first, grad_one, standard_grad.astype(bf16)))
            other_sums = swapped(small)
        parts = double(parts, orders, k, section, index, count)
    mine = small[:series_rows].reshape((z.own,) + z.stats)
    theirs = other_sums[:series_rows].reshape((z.own,) + z.stats)
    series_all = jnp.where(
        on_first, jnp.concatenate([mine, theirs]), jnp.concatenate([theirs, mine])
    )
    small = small[series_rows:] + other_sums[series_rows:]
    stats_all = jnp.where(
        on_first, jnp.concatenate([stats, other_stats]), jnp.concatenate([other_stats, stats])
    )
    sec_late, parts = lax.optimization_barrier((sec, parts))
    input_grads, section_output = final(
        z, sec_late, inputs, series_id, stats_all, series_all, standard_grad, grad_one, other_grad,
        own_out, other_out,
    )
    last_bits = jnp.stack([place(o[0], section, index) for o in orders]).astype(jnp.int32)
    others = [partner(p, *o[0], count) for p, o in zip(parts, orders)]
    vmem = pl.BlockSpec(memory_space=pltpu.VMEM)
    large = [shape(width, z.hidden)] * 2 + [shape(z.hidden, width)] + [shape(width, width)] * 4

    def unpack(held, halves, before):
        return pl.pallas_call(
            functools.partial(unpack_body, held, len(before)),
            in_specs=[SCALARS] + [vmem] * 2 + [HBM] * len(before),
            out_specs=[HBM] * 7,
            out_shape=large,
            input_output_aliases={3 + k: k for k in range(len(before))},
            scratch_shapes=[
                pltpu.VMEM((width, z.hidden), f32), pltpu.VMEM((width, z.hidden // 2), f32),
                pltpu.VMEM((z.hidden, width), f32), pltpu.VMEM((width, width), f32),
                pltpu.VMEM((width, width), f32), pltpu.SemaphoreType.DMA((4,)),
            ],
            compiler_params=pltpu.CompilerParams(vmem_limit_bytes=57 * 2**20),
            cost_estimate=pl.CostEstimate(flops=5 * 10**9, bytes_accessed=2**22, transcendentals=0),
            name="unpack",
        )(last_bits, *halves, *before)

    grad_gate, grad_up, grad_down, grad_query, grad_key, grad_value, grad_out = unpack(
        False, others, unpack(True, parts, ())
    )
    grad_attention_gain, grad_feed_gain, grad_bias = pl.pallas_call(
        unpack_small_body,
        in_specs=[SCALARS, vmem],
        out_shape=[shape(1, width)] * 2 + [shape(2, heads)],
        name="unpack_small",
    )(sec, small)
    return (
        section_output[None],
        input_grads[None],
        grad_attention_gain,
        grad_query[None],
        grad_key[None],
        grad_value[None],
        grad_out[None],
        grad_bias.T[None],
        grad_feed_gain,
        grad_gate[None],
        grad_up[None],
        grad_down[None],
    )


def solution(mesh):
    placed = (
        P(None, "dp", None),
        P(None, "dp"),
        P(None, "dp"),
        P(None, "dp"),
        P(None, "dp", None),
        P("section", None),
        P("section", None, None),
        P("section", None, None),
        P("section", None, None),
        P("section", None, None),
        P("section", None, None),
        P("section", None),
        P("section", None, None),
        P("section", None, None),
        P("section", None, None),
    )
    return jax.shard_map(
        per_device,
        mesh=mesh,
        in_specs=placed,
        out_specs=(
            P("section", None, "dp", None),
            P("section", None, "dp", None),
            P("section", None),
            P("section", None, None),
            P("section", None, None),
            P("section", None, None),
            P("section", None, None),
            P("section", None, None),
            P("section", None),
            P("section", None, None),
            P("section", None, None),
            P("section", None, None),
        ),
        check_vma=False,
    )
```

```python
import functools

import jax
import jax.numpy as jnp
import numpy as np
from jax import lax
from jax.experimental import pallas as pl
from jax.experimental.pallas import tpu as pltpu
from jax.sharding import PartitionSpec as P

HD = 64
BLOCK = 512
SER_DEV = 4
LANES = 128
CHUNK = 512
TILE = 256

norm_epsilon = 1e-05
scale_epsilon = 1e-05
masked_score = -1e30

f32 = jnp.float32
bf16 = jnp.bfloat16

AS_IS = (((1,), (0,)), ((), ()))
RIGHT_T = (((1,), (1,)), ((), ()))
LEFT_T = (((0,), (0,)), ((), ()))


def dot(left, right, dims=AS_IS):
    return lax.dot_general(left, right, dims, preferred_element_type=f32)


def column(row):
    return jnp.broadcast_to(row.astype(f32), (LANES, row.shape[1])).T


def lane_index(rows):
    return lax.broadcasted_iota(jnp.int32, (rows, LANES), 1)


def regroup(x):
    group = lane_index(x.shape[0]) // (HD // 2)
    return jnp.where(
        group == 1,
        pltpu.roll(x, LANES - HD // 2, 1),
        jnp.where(group == 2, pltpu.roll(x, HD // 2, 1), x),
    )


def turn(x, cosine, sine):
    return x * cosine + pltpu.roll(x, LANES // 2, 1) * sine


def turn_back(x, cosine, sine):
    return x * cosine - pltpu.roll(x, LANES // 2, 1) * sine


def inverse_rms(x):
    return lax.rsqrt(jnp.mean(x * x, axis=1, keepdims=True) + norm_epsilon)


def series_hits(sid_col, piece):
    return sid_col == (lane_index(sid_col.shape[0]) + piece * LANES).astype(f32)


def rows_of(hits, per_series):
    return jnp.sum(jnp.where(hits, per_series, 0.0), axis=1, keepdims=True)


def series_of(hits, per_row):
    return jnp.sum(jnp.where(hits, per_row, 0.0), axis=0, keepdims=True)


def stats_body(sec_ref, x_ref, sid_ref, out_ref):
    own, _, width = x_ref.shape
    pieces = out_ref.shape[-1] // LANES
    out_ref[...] = jnp.zeros_like(out_ref)
    for i in range(own):
        x = x_ref[i].astype(f32)
        sid_col = column(sid_ref[pl.ds(own * sec_ref[0] + i, 1), :])
        totals = jnp.sum(x, axis=1, keepdims=True)
        centre = jnp.zeros_like(totals)
        for piece in range(pieces):
            hits = series_hits(sid_col, piece)
            count = series_of(hits, 1.0)
            total = series_of(hits, totals)
            centre = centre + rows_of(hits, total / (jnp.maximum(count, 1.0) * width))
            out_ref[i, 0:1, piece * LANES : (piece + 1) * LANES] = count
            out_ref[i, 1:2, piece * LANES : (piece + 1) * LANES] = total
        centred = x - centre
        squares = jnp.sum(centred * centred, axis=1, keepdims=True)
        for piece in range(pieces):
            hits = series_hits(sid_col, piece)
            out_ref[i, 2:3, piece * LANES : (piece + 1) * LANES] = series_of(hits, squares)


def merge_stats(here, there, width):
    count_a, total_a, spread_a = here[:, 0:1], here[:, 1:2], here[:, 2:3]
    count_b, total_b, spread_b = there[:, 0:1], there[:, 1:2], there[:, 2:3]
    count = count_a + count_b
    gap = total_a / (jnp.maximum(count_a, 1.0) * width) - total_b / (
        jnp.maximum(count_b, 1.0) * width
    )
    weight = count_a * count_b * width / jnp.maximum(count, 1.0)
    row = lax.broadcasted_iota(jnp.int32, here.shape, 1)
    return jnp.where(
        row == 0,
        count,
        jnp.where(row == 1, total_a + total_b, spread_a + spread_b + gap * gap * weight),
    )


def centre_and_scale(stats, width):
    entries = jnp.maximum(stats[0:1], 1.0) * width
    centre = stats[1:2] / entries
    scaling = jnp.sqrt(stats[2:3] / entries + scale_epsilon)
    return entries, centre, scaling


class Weights:
    def __init__(self, section, own_refs, other_refs, big_ref, down_ref, sems):
        self.first_step = pl.program_id(0) == 0
        self.big_ref, self.down_ref = big_ref, down_ref
        self.own_refs, self.sems = own_refs, sems

        @pl.when(self.first_step)
        def _():
            for layer_of, refs in ((section, own_refs), (1 - section, other_refs)):
                for k, ref in enumerate(refs):
                    pltpu.make_async_copy(ref, self.target(layer_of, k), sems.at[layer_of, k]).start()

    def target(self, layer, k):
        if k == 6:
            return self.down_ref.at[layer]
        at = sum(ref.shape[1] for ref in self.own_refs[:k])
        return self.big_ref.at[layer, :, pl.ds(at, self.own_refs[k].shape[1])]

    def wait_here(self, layer, numbers):
        for k in numbers:
            pltpu.make_async_copy(
                self.own_refs[k], self.target(layer, k), self.sems.at[layer, k]
            ).wait()

    def wait_attention(self, layer):
        width = self.big_ref.shape[1]

        @pl.when(self.first_step)
        def _():
            self.wait_here(layer, (0, 1, 2, 3))
            for at in range(0, 2 * width, LANES):
                tile = self.big_ref[layer, :, at : at + LANES].astype(f32)
                self.big_ref[layer, :, at : at + LANES] = regroup(tile).astype(bf16)

    def wait_feed(self, layer):
        @pl.when(self.first_step)
        def _():
            self.wait_here(layer, (4, 5, 6))


def sigmoid(x):
    return 0.5 * jnp.tanh(0.5 * x) + 0.5


def in_head(half, lanes, grouped):
    if grouped:
        return (lanes % HD) // (HD // 2) == half
    return lanes // HD == half


def row_index(rows):
    return lax.broadcasted_iota(jnp.int32, (LANES, rows), 0)


class Block:
    def __init__(self, cosine, sine, item_col, var_col, var_row, same_ref):
        rows = cosine.shape[0]
        self.cosine, self.sine, self.same_ref = cosine, sine, same_ref
        row = var_row.astype(f32)
        for at in range(0, rows, LANES):
            same_ref[:, at : at + LANES] = jnp.where(var_col == row[:, at : at + LANES], 1.0, 0.0)
        lane = lane_index(rows)
        second = jnp.where(item_col > 0.0, 1.0, 0.0)
        self.item_q = jnp.where(
            lane == 0, second, jnp.where(lane == 1, 1.0 - second, 0.0)
        ).astype(bf16)
        self.item_k = jnp.where(
            lane == 0,
            (1.0 - second) * masked_score,
            jnp.where(lane == 1, second * masked_score, 0.0),
        ).astype(bf16)


def attention_forward(layer, hidden, gains, block, bias, weights, saved):
    qkv_ref, prob_ref, inv_ref, mixed_ref = (ref.at[layer] for ref in saved)
    rows, width = hidden.shape
    pairs = width // LANES
    tiles = rows // TILE
    big_ref = weights.big_ref.at[layer]
    normed = (hidden * inverse_rms(hidden) * gains).astype(bf16)
    weights.wait_attention(layer)
    lane = lane_index(rows)
    first_rows = row_index(rows) < HD
    extra = lax.broadcasted_iota(jnp.int32, (16, rows), 0)

    projected = dot(normed, big_ref[:, : 3 * width])

    def project(p):
        at = p * LANES
        q = turn(projected[:, at : at + LANES], block.cosine, block.sine)
        k = turn(projected[:, width + at : width + at + LANES], block.cosine, block.sine)
        v = projected[:, 2 * width + at : 2 * width + at + LANES]
        qkv_ref[:, at : at + LANES] = (q * HD**-0.5).astype(bf16)
        qkv_ref[:, width + at : width + at + LANES] = k.astype(bf16)
        qkv_ref[:, 2 * width + at : 2 * width + at + LANES] = v.astype(bf16)

    def operands(p):
        at = p * LANES
        q_pair = qkv_ref[:, at : at + LANES]
        k_aug = jnp.concatenate([qkv_ref[:, width + at : width + at + LANES], block.item_k], axis=1)
        v_turned = qkv_ref[:, 2 * width + at : 2 * width + at + LANES].T
        heads = []
        for half in range(2):
            q_aug = jnp.concatenate(
                [jnp.where(in_head(half, lane, True), q_pair, 0.0).astype(bf16), block.item_q],
                axis=1,
            )
            own_rows = first_rows if half == 0 else jnp.logical_not(first_rows)
            v_aug = jnp.concatenate(
                [
                    jnp.where(own_rows, v_turned, 0.0).astype(bf16),
                    jnp.where(extra == half, 1.0, 0.0).astype(bf16),
                ],
                axis=0,
            )
            heads.append((q_aug, v_aug))
        return k_aug, heads

    prepared = {}

    def scores_of(p, half, t):
        if p not in prepared:
            project(p)
            prepared[p] = operands(p)
        k_aug, heads = prepared[p]
        return dot(k_aug, heads[half][0][t * TILE : (t + 1) * TILE, :], RIGHT_T)

    order = [(p, half, t) for p in range(pairs) for half in range(2) for t in range(tiles)]
    attended = {}
    scores = scores_of(*order[0])
    for n, (p, half, t) in enumerate(order):
        following = scores_of(*order[n + 1]) if n + 1 < len(order) else None
        head = 2 * p + half
        cols = slice(t * TILE, (t + 1) * TILE)
        gap = bias[0:1, 2 * head : 2 * head + 1] - bias[0:1, 2 * head + 1 : 2 * head + 2]
        biased = scores + block.same_ref[:, cols] * gap
        peak = jnp.max(biased, axis=0, keepdims=True)
        prob = jnp.exp(biased - peak).astype(bf16)
        prob_ref[head, :, cols] = prob
        part = dot(prepared[p][1][half][1], prob)
        attended[p, t] = part if half == 0 else attended[p, t] + part
        if half == 1:
            sums = attended.pop((p, t))
            own_rows = row_index(TILE) < HD
            inv = jnp.where(
                own_rows, 1.0 / sums[LANES : LANES + 1], 1.0 / sums[LANES + 1 : LANES + 2]
            )
            inv_ref[cols, p * LANES : (p + 1) * LANES] = inv.T
            mixed_ref[cols, p * LANES : (p + 1) * LANES] = (sums[:LANES] * inv).T
        scores = following
    return hidden + dot(mixed_ref[...].astype(bf16), big_ref[:, 3 * width : 4 * width])


def feed_forward(layer, middle, gains, weights):
    big_ref, down_ref = weights.big_ref.at[layer], weights.down_ref.at[layer]
    width = middle.shape[1]
    hidden = down_ref.shape[0]
    feed = (middle * inverse_rms(middle) * gains).astype(bf16)
    total = middle
    for at in range(0, hidden, CHUNK):
        gate = dot(feed, big_ref[:, 4 * width + at : 4 * width + at + CHUNK])
        up = dot(feed, big_ref[:, 4 * width + hidden + at : 4 * width + hidden + at + CHUNK])
        active = (gate * sigmoid(gate) * up).astype(bf16)
        total = total + dot(active, down_ref[at : at + CHUNK, :])
    return total.astype(bf16)


def feed_backward(layer, middle, gains, grad_low, weights, accs, active_ref):
    gate_acc, up_acc, down_acc, gain_acc = (acc.at[layer] for acc in accs)
    big_ref, down_ref = weights.big_ref.at[layer], weights.down_ref.at[layer]
    width = middle.shape[1]
    hidden = down_ref.shape[0]
    inverse = inverse_rms(middle)
    feed = (middle * inverse * gains).astype(bf16)
    feed_t = feed.T
    feed_grad = jnp.zeros(middle.shape, f32)
    for at in range(0, hidden, CHUNK):
        gate_w = big_ref[:, 4 * width + at : 4 * width + at + CHUNK]
        up_w = big_ref[:, 4 * width + hidden + at : 4 * width + hidden + at + CHUNK]
        down_w = down_ref[at : at + CHUNK, :]
        gate = dot(feed, gate_w)
        up = dot(feed, up_w)
        act_grad = dot(grad_low, down_w, RIGHT_T)
        gated = sigmoid(gate)
        swish = gate * gated
        active = (swish * up).astype(bf16)
        active_ref[:, at : at + CHUNK] = active
        gate_grad = (act_grad * up * (gated + swish * (1.0 - gated))).astype(bf16)
        up_grad = (act_grad * swish).astype(bf16)
        feed_grad = feed_grad + dot(gate_grad, gate_w, RIGHT_T) + dot(up_grad, up_w, RIGHT_T)
        gate_acc[:, at : at + CHUNK] += dot(feed_t, gate_grad)
        up_acc[:, at : at + CHUNK] += dot(feed_t, up_grad)
        down_acc[at : at + CHUNK, :] += dot(active, grad_low, LEFT_T)
    scaled = feed_grad * gains
    gain_acc[...] += jnp.sum(feed_grad * middle * inverse, axis=0, keepdims=True)
    return (
        grad_low.astype(f32)
        + inverse * scaled
        - middle * (inverse * inverse * inverse) * jnp.mean(scaled * middle, axis=1, keepdims=True)
    )


def attention_backward(layer, middle_grad, hidden, gains, block, weights, saved, grads_ref, accs):
    qkv_ref, prob_ref, inv_ref, mixed_ref = (ref.at[layer] for ref in saved)
    qkv_acc, out_acc, gain_acc, bias_acc = (acc.at[layer] for acc in accs)
    rows, width = hidden.shape
    pairs = width // LANES
    tiles = rows // TILE
    big_ref = weights.big_ref.at[layer]
    mix_grad = middle_grad.astype(bf16)
    att_grad = dot(mix_grad, big_ref[:, 3 * width : 4 * width], RIGHT_T).astype(bf16)
    lane = lane_index(rows)
    ones_four = jnp.where(lane < 4, 1.0, 0.0).astype(bf16)
    source = lax.broadcasted_iota(jnp.int32, (2 * LANES, LANES), 0) % LANES // HD
    target = lax.broadcasted_iota(jnp.int32, (2 * LANES, LANES), 1)
    gather = jnp.where((target // 2 == source) & (target < 4), 1.0, 0.0).astype(bf16)

    def operands(p):
        at = p * LANES
        q_pair = qkv_ref[:, at : at + LANES]
        k_turned = qkv_ref[:, width + at : width + at + LANES].T
        v_aug = jnp.concatenate(
            [qkv_ref[:, 2 * width + at : 2 * width + at + LANES], ones_four], axis=1
        )
        grad_pair = (att_grad[:, at : at + LANES].astype(f32) * inv_ref[:, at : at + LANES]).astype(
            bf16
        )
        product = grad_pair.astype(f32) * mixed_ref[:, at : at + LANES]
        high = product.astype(bf16)
        low = (product - high.astype(f32)).astype(bf16)
        inner = dot(jnp.concatenate([high, low], axis=1), gather)
        inner_high = inner.astype(bf16).astype(f32)
        tail = jnp.where(lane % 2 == 0, -inner_high, inner_high - inner)
        heads = []
        for half in range(2):
            grad_low = jnp.where(in_head(half, lane, False), grad_pair, 0.0).astype(bf16)
            tail_low = jnp.where(lane // 2 == half, tail, 0.0).astype(bf16)
            q_mine = jnp.where(in_head(half, lane, True), q_pair, 0.0).astype(bf16)
            low = half * (HD // 2)
            k_mine = jnp.concatenate(
                [k_turned[low : low + HD // 2], k_turned[HD + low : HD + low + HD // 2]], axis=0
            )
            heads.append(
                (jnp.concatenate([grad_low, tail_low], axis=1), grad_low, q_mine, k_mine)
            )
        return v_aug, heads

    prepared = {}

    def prob_grad_of(p, half, t):
        if p not in prepared:
            prepared[p] = operands(p)
        v_aug, heads = prepared[p]
        return dot(v_aug, heads[half][0][t * TILE : (t + 1) * TILE, :], RIGHT_T)

    order = [(p, half, t) for p in range(pairs) for half in range(2) for t in range(tiles)]
    value_grad = key_grad = None
    query_grad = {}
    prob_grad = prob_grad_of(*order[0])
    for n, (p, half, t) in enumerate(order):
        following = prob_grad_of(*order[n + 1]) if n + 1 < len(order) else None
        head = 2 * p + half
        cols = slice(t * TILE, (t + 1) * TILE)
        at = p * LANES
        _, grad_low, q_mine, k_mine = prepared[p][1][half]
        prob = prob_ref[head, :, cols]
        score_grad = prob.astype(f32) * prob_grad
        bias_acc[head : head + 1, cols] += jnp.sum(
            score_grad * block.same_ref[:, cols], axis=0, keepdims=True
        )
        score_low = score_grad.astype(bf16)
        part_v = dot(prob, grad_low[cols, :])
        part_k = dot(score_low, q_mine[cols, :])
        part_q = dot(k_mine, score_low)
        value_grad = part_v if value_grad is None else value_grad + part_v
        key_grad = part_k if key_grad is None else key_grad + part_k
        query_grad[t, half] = part_q
        if half == 1:
            one, two = query_grad.pop((t, 0)), query_grad.pop((t, 1))
            mid = HD // 2
            back = jnp.concatenate([one[:mid], two[:mid], one[mid:], two[mid:]], axis=0).T * HD**-0.5
            grads_ref[cols, at : at + LANES] = turn_back(
                back, block.cosine[cols, :], block.sine[cols, :]
            ).astype(bf16)
        if half == 1 and t == tiles - 1:
            grads_ref[:, width + at : width + at + LANES] = turn_back(
                key_grad, block.cosine, block.sine
            ).astype(bf16)
            grads_ref[:, 2 * width + at : 2 * width + at + LANES] = value_grad.astype(bf16)
            value_grad = key_grad = None
        prob_grad = following
    out_acc[...] += dot(mixed_ref[...].astype(bf16), mix_grad, LEFT_T)
    inverse = inverse_rms(hidden)
    normed = (hidden * inverse * gains).astype(bf16)
    normed_grad = dot(grads_ref[...], big_ref[:, : 3 * width], RIGHT_T)
    qkv_acc[...] += dot(normed, grads_ref[...], LEFT_T)
    scaled = normed_grad * gains
    gain_acc[...] += jnp.sum(normed_grad * hidden * inverse, axis=0, keepdims=True)
    return (
        middle_grad
        + inverse * scaled
        - hidden * (inverse * inverse * inverse) * jnp.mean(scaled * hidden, axis=1, keepdims=True)
    )


def column_tiles(acc_ref):
    return [acc_ref[:, at : at + LANES] for at in range(0, acc_ref.shape[1], LANES)]


class Packer:
    def __init__(self, stage_ref, sems, kept_refs, sent_refs):
        self.stage_ref, self.sems = stage_ref, sems
        self.kept_refs, self.sent_refs = kept_refs, sent_refs
        self.sent = []

    def copy(self, out_ref, slot, count):
        source = self.stage_ref.at[slot, pl.ds(0, count)]
        return pltpu.make_async_copy(source, out_ref, self.sems.at[slot])

    def send(self, keep, part, start, tiles):
        slot = len(self.sent) % 2
        if len(self.sent) >= 2:
            self.wait(2)
        at = 0
        for tile in tiles:
            self.stage_ref[slot, at : at + tile.shape[0], :] = tile.astype(bf16)
            at += tile.shape[0]
        where = pl.ds(start, at)

        @pl.when(keep)
        def _():
            self.copy(self.kept_refs[part].at[where], slot, at).start()

        @pl.when(jnp.logical_not(keep))
        def _():
            self.copy(self.sent_refs[part].at[where], slot, at).start()

        self.sent.append((self.kept_refs[part].at[where], slot, at))

    def wait(self, back):
        self.copy(*self.sent[-back]).wait()

    def finish(self):
        self.wait(2)
        self.wait(1)


def layers_body(
    sec_ref, x_ref, cotangent_ref, sid_ref, item_ref, var_ref, stats_ref, table_ref,
    own_small_ref, other_small_ref, *refs
):
    own_refs, other_refs, refs = refs[:7], refs[7:14], refs[14:]
    results_ref, grad_one_ref, grad_zero_ref, series_ref, small_ref = refs[:5]
    kept_refs, sent_refs, refs = refs[5:7], refs[7:9], refs[9:]
    big_ref, down_ref, refs = refs[0], refs[1], refs[2:]
    feed_accs, attention_accs, saved, refs = refs[:4], refs[4:8], refs[8:12], refs[12:]
    same_ref, grads_ref, hidden_ref, middle_ref, grad_ref, active_ref, stage_ref, *refs = refs
    sems, stage_sems = refs

    i = pl.program_id(0)
    last = i == pl.num_programs(0) - 1
    m = pl.num_programs(0) * sec_ref[0] + i
    weights = Weights(sec_ref[0], own_refs, other_refs, big_ref, down_ref, sems)

    @pl.when(i == 0)
    def _():
        for acc in feed_accs + attention_accs:
            acc[...] = jnp.zeros_like(acc)

    x = x_ref[0].astype(f32)
    rows, width = x.shape
    var_row = var_ref[pl.ds(m, 1), :]
    var_col = column(var_row)
    sid_col = column(sid_ref[pl.ds(m, 1), :])
    pieces = stats_ref.shape[-1] // LANES

    time = lax.broadcasted_iota(jnp.int32, (rows, LANES), 0).astype(f32) - var_col
    cosine = sine = jnp.zeros((rows, LANES), f32)
    for at in range(0, rows, LANES):
        hot = jnp.where(time == (lane_index(rows) + at).astype(f32), 1.0, 0.0).astype(bf16)
        found = dot(hot, table_ref[at : at + LANES, :])
        cosine = cosine + found[:, :LANES] + found[:, LANES : 2 * LANES]
        sine = sine + found[:, 2 * LANES : 3 * LANES] + found[:, 3 * LANES :]
    block = Block(cosine, sine, column(item_ref[pl.ds(m, 1), :]), var_col, var_row, same_ref)

    _, centre, scaling = centre_and_scale(stats_ref[0], width)
    centre_rows = scale_rows = 0.0
    for piece in range(pieces):
        hits = series_hits(sid_col, piece)
        part = slice(piece * LANES, (piece + 1) * LANES)
        centre_rows = centre_rows + rows_of(hits, centre[:, part])
        scale_rows = scale_rows + rows_of(hits, scaling[:, part])
    hidden_ref[0] = (x - centre_rows) / scale_rows
    grad_ref[...] = cotangent_ref[0]

    def small_row(layer, k):
        return jnp.where(
            sec_ref[0] == layer, own_small_ref[k : k + 1, :], other_small_ref[k : k + 1, :]
        )

    def forward(layer, _):
        middle = attention_forward(
            layer, hidden_ref[layer], small_row(layer, 0), block, small_row(layer, 2), weights,
            saved,
        )
        middle_ref[layer] = middle
        weights.wait_feed(layer)

        @pl.when(layer == 0)
        def _():
            result = feed_forward(layer, middle_ref[0], small_row(layer, 1), weights)
            results_ref[0, 0] = result
            hidden_ref[1] = result.astype(f32)

    def send(layer):
        packer = Packer(stage_ref, stage_sems, kept_refs, sent_refs)
        keep = sec_ref[0] == layer
        gate, up, down = (column_tiles(acc.at[layer]) for acc in feed_accs[:3])
        queries = column_tiles(attention_accs[0].at[layer])
        turned = [regroup(tile) for tile in queries[:6]]
        start = 0
        for tiles in (gate, up, down):
            packer.send(keep, 0, start, tiles)
            start += sum(tile.shape[0] for tile in tiles)
        packer.send(keep, 1, 0, turned)
        packer.send(keep, 1, width * 6, queries[6:] + column_tiles(attention_accs[1].at[layer]))
        packer.finish()

    def backward(step, _):
        layer = 1 - step
        middle_grad = feed_backward(
            layer, middle_ref[layer], small_row(layer, 1), grad_ref[...], weights, feed_accs,
            active_ref,
        )

        @pl.when(layer == 1)
        def _():
            total = middle_ref[1] + dot(active_ref[...], weights.down_ref[1])
            results_ref[1, 0] = total.astype(bf16)

        hidden_grad = attention_backward(
            layer, middle_grad, hidden_ref[layer], small_row(layer, 0), block, weights,
            saved, grads_ref, attention_accs,
        )
        grad_ref[...] = hidden_grad.astype(bf16)
        grad_zero_ref[0] = hidden_grad

        @pl.when(layer == 1)
        def _():
            grad_one_ref[0] = hidden_grad.astype(bf16)

        @pl.when(last)
        def _():
            send(layer)

    lax.fori_loop(0, 2, forward, None)
    lax.fori_loop(0, 2, backward, None)

    standard, hidden_grad = hidden_ref[0], grad_zero_ref[0]
    grad_rows = jnp.sum(hidden_grad, axis=1, keepdims=True)
    cross_rows = jnp.sum(hidden_grad * standard, axis=1, keepdims=True)
    standard_rows = jnp.sum(standard, axis=1, keepdims=True)
    series_ref[0] = jnp.zeros(series_ref.shape[1:], f32)
    for piece in range(pieces):
        hits = series_hits(sid_col, piece)
        part = slice(piece * LANES, (piece + 1) * LANES)
        series_ref[0, 0:1, part] = series_of(hits, grad_rows)
        series_ref[0, 1:2, part] = series_of(hits, cross_rows)
        series_ref[0, 2:3, part] = series_of(hits, standard_rows)

    @pl.when(last)
    def _():
        small_ref[...] = jnp.zeros_like(small_ref)
        for layer in range(2):
            base = 24 * layer
            for k in range(width // LANES):
                cols = slice(k * LANES, (k + 1) * LANES)
                small_ref[base + k : base + k + 1, :] = attention_accs[2][layer, :, cols]
                small_ref[base + 16 + k : base + 17 + k, :] = feed_accs[3][layer, :, cols]
            bias_sums = jnp.sum(attention_accs[3][layer], axis=1, keepdims=True)
            small_ref[base + 8 : base + 16, :] = jnp.broadcast_to(bias_sums, (8, LANES))


def final_body(
    sec_ref, x_ref, sid_ref, stats_ref, series_ref, own_first, own_second, other_grad,
    own_out, other_out, out_ref, grads_ref,
):
    i = pl.program_id(0)
    sec = sec_ref[0]
    own = (i // (pl.num_programs(0) // 2)) == sec
    grads_ref[0] = jnp.where(own, own_out[0], other_out[0])
    grad = jnp.where(
        own,
        jnp.where(sec == 0, own_first[0], own_second[0].astype(f32)),
        other_grad[0].astype(f32),
    )

    @pl.when(sec == 0)
    def _():
        x = x_ref[0].astype(f32)
        width = x.shape[1]
        entries, centre, scaling = centre_and_scale(stats_ref[0], width)
        sums = series_ref[0]
        cross = sums[1:2] * scaling
        spread_grad = -cross / (2.0 * scaling * scaling * scaling * entries)
        mean_grad = sums[0:1] / scaling + 2.0 * spread_grad * (sums[2:3] * scaling)
        tables = (centre, 1.0 / scaling, 2.0 * spread_grad, mean_grad / entries)
        sid_col = column(sid_ref[pl.ds(i, 1), :])
        looked = [0.0, 0.0, 0.0, 0.0]
        for piece in range(stats_ref.shape[-1] // LANES):
            hits = series_hits(sid_col, piece)
            part = slice(piece * LANES, (piece + 1) * LANES)
            for k in range(4):
                looked[k] = looked[k] + rows_of(hits, tables[k][:, part])
        out_ref[0] = grad * looked[1] + (x - looked[0]) * looked[2] - looked[3]

    @pl.when(sec != 0)
    def _():
        out_ref[0] = grad


def unpack_body(held, count, bit_ref, feed_ref, attention_ref, *refs):
    refs = refs[count:]
    gate, up, down, query, key, value, out = refs[:7]
    gate_at, up_at, down_at, one_at, two_at, sems = refs[7:]
    half_up = up_at.shape[1]

    def leave(k, source_ref, at, scratch_ref, target_ref):
        rows = scratch_ref.shape[0]
        for col in range(0, scratch_ref.shape[1], LANES):
            scratch_ref[:, col : col + LANES] = source_ref[at : at + rows, :].astype(f32)
            at += rows
        copy = pltpu.make_async_copy(scratch_ref, target_ref, sems.at[k])
        copy.start()
        return copy

    gate_rows = gate_at.shape[0] * gate_at.shape[1] // LANES
    up_rows = up_at.shape[0] * half_up // LANES
    one_rows = one_at.shape[0] * one_at.shape[1] // LANES

    def feed(low):
        if low:
            return [
                leave(0, feed_ref, 0, gate_at, gate),
                leave(1, feed_ref, gate_rows, up_at, up.at[:, pl.ds(0, half_up)]),
            ]
        return [
            leave(0, feed_ref, up_rows, down_at, down),
            leave(1, feed_ref, 0, up_at, up.at[:, pl.ds(half_up, half_up)]),
        ]

    def attention(low):
        first, second = (query, key) if low else (value, out)
        return [
            leave(2, attention_ref, 0, one_at, first),
            leave(3, attention_ref, one_rows, two_at, second),
        ]

    for feed_low in range(2):
        for attention_low in range(2):
            here = (bit_ref[0] == (1 - feed_low if held else feed_low)) & (
                bit_ref[1] == (1 - attention_low if held else attention_low)
            )

            @pl.when(here)
            def _(feed_low=feed_low, attention_low=attention_low):
                for copy in feed(feed_low) + attention(attention_low):
                    copy.wait()


def unpack_small_body(sec_ref, small_ref, attention_gain_ref, feed_gain_ref, bias_ref):
    base = 24 * sec_ref[0]
    for k in range(attention_gain_ref.shape[1] // LANES):
        cols = slice(k * LANES, (k + 1) * LANES)
        attention_gain_ref[:, cols] = small_ref[pl.ds(base + k, 1), :]
        feed_gain_ref[:, cols] = small_ref[pl.ds(base + 16 + k, 1), :]
    same = small_ref[pl.ds(base + 8, 8), :].T[0:1, : bias_ref.shape[1]]
    bias_ref[0:1, :] = same
    bias_ref[1:2, :] = -same


def swapped(x):
    return lax.ppermute(x, "section", [(0, 1), (1, 0)])


def to_section(x, section):
    return lax.ppermute(x, "section", [(1 - section, section)])


def exchange_steps(count):
    bits = []
    step = 1
    while step < count:
        bits.append(step)
        step *= 2
    other = list(bits)
    for k in range(0, len(bits) - 1, 2):
        other[k], other[k + 1] = bits[k + 1], bits[k]
    return bits, other


def partner(x, by_first, by_second, count):
    pairs = [(i, i ^ by_first) for i in range(count)]
    pairs += [(count + i, count + (i ^ by_second)) for i in range(count)]
    return lax.ppermute(x, ("section", "dp"), pairs)


def place(steps, section, index):
    step = jnp.where(section == 0, *steps)
    return (index // step) % 2


def halve(parts, orders, k, section, index, count, *more):
    keeps, sends = [], []
    for current, order in zip(parts, orders):
        bit = place(order[k], section, index)
        half = current.shape[0] // 2
        keeps.append(lax.dynamic_slice_in_dim(current, bit * half, half, 0))
        sends.append(lax.dynamic_slice_in_dim(current, (1 - bit) * half, half, 0))
    sends, keeps, more = lax.optimization_barrier((sends, keeps, more))
    got = [partner(send, *order[k], count) for send, order in zip(sends, orders)]
    parts = [(a.astype(f32) + b.astype(f32)).astype(bf16) for a, b in zip(keeps, got)]
    return (parts, *more)


def add_whole(parts, orders, k, count, *more):
    parts, more = lax.optimization_barrier((parts, more))
    got = [partner(part, *order[k], count) for part, order in zip(parts, orders)]
    parts = [(a.astype(f32) + b.astype(f32)).astype(bf16) for a, b in zip(parts, got)]
    return (parts, *more)


def double(parts, orders, k, section, index, count):
    parts = lax.optimization_barrier(parts)
    result = []
    for current, order in zip(parts, orders):
        bit = place(order[k], section, index)
        got = partner(current, *order[k], count)
        low = jnp.where(bit == 0, current, got)
        high = jnp.where(bit == 0, got, current)
        result.append(jnp.concatenate([low, high], axis=0))
    return result


HBM = pl.BlockSpec(memory_space=pl.ANY)
SCALARS = pl.BlockSpec(memory_space=pltpu.SMEM)


def whole_block(shape):
    return pl.BlockSpec(shape, lambda i, *_: (0,) * len(shape))


def by_step(shape):
    return pl.BlockSpec((1,) + shape, lambda i, *_: (i,) + (0,) * len(shape))


def by_batch(shape, own):
    return pl.BlockSpec((1,) + shape, lambda i, s: (own * s[0] + i,) + (0,) * len(shape))


def call(body, grid, in_specs, out_specs, out_shapes, scratch, flops, name, vmem=28):
    return pl.pallas_call(
        body,
        grid_spec=pltpu.PrefetchScalarGridSpec(
            num_scalar_prefetch=1,
            grid=(grid,),
            in_specs=in_specs,
            out_specs=out_specs,
            scratch_shapes=scratch,
        ),
        out_shape=out_shapes,
        compiler_params=pltpu.CompilerParams(vmem_limit_bytes=vmem * 2**20),
        cost_estimate=pl.CostEstimate(flops=flops, bytes_accessed=2**22, transcendentals=0),
        name=name,
    )


def shape(*dims, dtype=f32):
    return jax.ShapeDtypeStruct(dims, dtype)


class Sizes:
    def __init__(self, inputs, heads, hidden, count):
        self.micro, self.rows, self.width = inputs.shape
        self.own = self.micro // 2
        self.heads, self.hidden, self.count = heads, hidden, count
        rows, width, own = self.rows, self.width, self.own
        self.stats = (8, -(-SER_DEV * count // LANES) * LANES)
        self.all_rows = whole_block((self.micro, rows))
        self.row = by_step((rows, width))
        self.row_batch = by_batch((rows, width), own)
        self.gain = whole_block((8, width))
        self.row_shape = shape(own, rows, width)
        self.low_shape = shape(own, rows, width, dtype=bf16)
        self.flops = 2 * rows * (4 * width * width + 3 * width * hidden) * own


def rotary_table(rows):
    lane = np.arange(LANES)
    frequency = np.float32(10000.0) ** (
        -(lane % (HD // 2)).astype(np.float32) * np.float32(2.0 / HD)
    )
    angle = np.arange(rows, dtype=np.float32)[:, None] * frequency[None, :].astype(np.float32)
    cosine = np.cos(angle.astype(np.float64))
    sine = np.sin(angle.astype(np.float64)) * np.where(lane < HD, -1.0, 1.0)
    parts = []
    for values in (cosine, sine):
        high = values.astype(jnp.bfloat16)
        parts += [high, (values - high.astype(np.float64)).astype(jnp.bfloat16)]
    return np.concatenate(parts, axis=1)


def series_stats(z, sec, inputs, series_id):
    return call(
        stats_body, 1,
        [pl.BlockSpec((z.own, z.rows, z.width), lambda i, s: (s[0], 0, 0)), z.all_rows],
        whole_block((z.own,) + z.stats), shape(z.own, *z.stats),
        [], 10**7, "series_stats",
    )(sec, inputs, series_id)


def layers(z, sec, inputs, cotangent, series_id, item, variate, stats, small, own, other):
    table = rotary_table(z.rows)
    rows, width, hidden = z.rows, z.width, z.hidden
    parts = [
        shape(3 * width * hidden // LANES, LANES, dtype=bf16),
        shape(4 * width * width // LANES, LANES, dtype=bf16),
    ]

    def both(*dims, dtype=f32):
        return pltpu.VMEM((2,) + dims, dtype)

    return call(
        layers_body, z.own,
        [z.row_batch, z.row_batch, z.all_rows, z.all_rows, z.all_rows, by_step(z.stats),
         whole_block(table.shape), whole_block((8, width)), whole_block((8, width))] + [HBM] * 14,
        [pl.BlockSpec((2, 1, rows, width), lambda i, *_: (0, i, 0, 0)), z.row, z.row,
         by_step(z.stats), whole_block((48, LANES))] + [HBM] * 4,
        [shape(2, z.own, rows, width, dtype=bf16), z.low_shape, z.row_shape,
         shape(z.own, *z.stats), shape(48, LANES)] + parts * 2,
        [both(width, 4 * width + 2 * hidden, dtype=bf16), both(hidden, width, dtype=bf16),
         both(width, hidden), both(width, hidden), both(hidden, width), both(1, width),
         both(width, 3 * width), both(width, width), both(1, width), both(8, rows),
         both(rows, 3 * width, dtype=bf16), both(z.heads, rows, rows, dtype=bf16),
         both(rows, width), both(rows, width),
         pltpu.VMEM((rows, rows), f32), pltpu.VMEM((rows, 3 * width), bf16),
         both(rows, width), both(rows, width), pltpu.VMEM((rows, width), bf16),
         pltpu.VMEM((rows, hidden), bf16),
         both(8 * width, LANES, dtype=bf16),
         pltpu.SemaphoreType.DMA((2, 7)), pltpu.SemaphoreType.DMA((2,))],
        12 * z.flops, "layers", 57,
    )(sec, inputs, cotangent, series_id, item, variate, stats, jnp.asarray(table),
      *small, *own, *other)


def final(z, sec, inputs, series_id, stats, series, own_first, own_second, other_grad,
          own_out, other_out):
    own_count = z.own

    def own_step(i, s):
        return (jnp.clip(i - own_count * s[0], 0, own_count - 1), 0, 0)

    def other_step(i, s):
        return (jnp.clip(i - own_count * (1 - s[0]), 0, own_count - 1), 0, 0)

    own_spec = pl.BlockSpec((1, z.rows, z.width), own_step)
    other_spec = pl.BlockSpec((1, z.rows, z.width), other_step)
    return call(
        final_body, z.micro,
        [z.row, z.all_rows, by_step(z.stats), by_step(z.stats), own_spec, own_spec,
         other_spec, own_spec, other_spec],
        [z.row, z.row],
        [shape(z.micro, z.rows, z.width), shape(z.micro, z.rows, z.width, dtype=bf16)],
        [], 10**10, "final",
    )(sec, inputs, series_id, stats, series, own_first, own_second, other_grad, own_out, other_out)


def per_device(
    inputs,
    series_id,
    item_offset,
    variate_offset,
    cotangent,
    attention_gain,
    query_weight,
    key_weight,
    value_weight,
    out_weight,
    variate_bias,
    feed_gain,
    gate_weight,
    up_weight,
    down_weight,
):
    section = lax.axis_index("section")
    index = lax.axis_index("dp")
    count = lax.axis_size("dp")
    on_first = section == 0
    sec = section.astype(jnp.int32).reshape(1)
    heads = variate_bias.shape[1]
    z = Sizes(inputs, heads, down_weight.shape[1], count)
    width = z.width

    own_small = jnp.concatenate(
        [
            attention_gain,
            feed_gain,
            jnp.pad(variate_bias.reshape(1, 2 * heads), ((0, 0), (0, width - 2 * heads))),
        ],
        axis=0,
    ).astype(f32)
    own_small = jnp.pad(own_small, ((0, 5), (0, 0)))
    other_small = swapped(own_small)
    own = tuple(
        w[0]
        for w in (
            query_weight, key_weight, value_weight, out_weight, gate_weight, up_weight, down_weight
        )
    )
    other = tuple(swapped(w) for w in own)
    stats = series_stats(z, sec, inputs, series_id)
    steps = exchange_steps(count)[0]
    for k, step in enumerate(steps):
        if k == len(steps) - 1:
            stats, other, other_small = lax.optimization_barrier((stats, other, other_small))
        stats = merge_stats(stats, partner(stats, step, step, count), width)

    results, grad_one, standard_grad, series_sums, small_sums, *packs = layers(
        z, sec, inputs, cotangent, series_id, item_offset, variate_offset, stats,
        (own_small, other_small), own, other,
    )

    parts = [
        (k.astype(f32) + swapped(t).astype(f32)).astype(bf16)
        for k, t in zip(packs[:2], packs[2:])
    ]
    bits, turned = exchange_steps(count)
    near = list(zip(bits, turned))
    orders = (near, near[2:] + near[:2])
    rounds = len(bits)

    series_rows = z.own * z.stats[0] * z.stats[1] // LANES
    small = jnp.concatenate(
        [series_sums.reshape(-1, LANES), small_sums], axis=0
    )
    parts = halve(parts, orders, 0, section, index, count)[0]
    for k in range(1, rounds):
        if k < rounds - 1:
            parts, small = halve(parts, orders, k, section, index, count, small)
        else:
            parts, stats = lax.optimization_barrier((parts, stats))
            parts, other_stats = lax.optimization_barrier((parts, swapped(stats)))
            parts, small = add_whole(parts, orders, k, count, small)
        small = small + partner(small, bits[rounds - k], bits[rounds - k], count)
    for k in reversed(range(1, rounds - 1)):
        if k == rounds - 2:
            parts, small = lax.optimization_barrier((parts, small))
            small = small + partner(small, bits[0], bits[0], count)
        if k == 1:
            parts, small, results, grad_one, standard_grad = lax.optimization_barrier(
                (parts, small, results, grad_one, standard_grad)
            )
            result_one, result_two = results[0], results[1]
            own_out = jnp.where(on_first, result_one, result_two)
            other_out = swapped(jnp.where(on_first, result_two, result_one))
            other_grad = swapped(jnp.where(on_first, grad_one, standard_grad.astype(bf16)))
            other_sums = swapped(small)
        parts = double(parts, orders, k, section, index, count)
    mine = small[:series_rows].reshape((z.own,) + z.stats)
    theirs = other_sums[:series_rows].reshape((z.own,) + z.stats)
    series_all = jnp.where(
        on_first, jnp.concatenate([mine, theirs]), jnp.concatenate([theirs, mine])
    )
    small = small[series_rows:] + other_sums[series_rows:]
    stats_all = jnp.where(
        on_first, jnp.concatenate([stats, other_stats]), jnp.concatenate([other_stats, stats])
    )
    sec_late, parts = lax.optimization_barrier((sec, parts))
    input_grads, section_output = final(
        z, sec_late, inputs, series_id, stats_all, series_all, standard_grad, grad_one, other_grad,
        own_out, other_out,
    )
    last_bits = jnp.stack([place(o[0], section, index) for o in orders]).astype(jnp.int32)
    others = [partner(p, *o[0], count) for p, o in zip(parts, orders)]
    vmem = pl.BlockSpec(memory_space=pltpu.VMEM)
    large = [shape(width, z.hidden)] * 2 + [shape(z.hidden, width)] + [shape(width, width)] * 4

    def unpack(held, halves, before):
        return pl.pallas_call(
            functools.partial(unpack_body, held, len(before)),
            in_specs=[SCALARS] + [vmem] * 2 + [HBM] * len(before),
            out_specs=[HBM] * 7,
            out_shape=large,
            input_output_aliases={3 + k: k for k in range(len(before))},
            scratch_shapes=[
                pltpu.VMEM((width, z.hidden), f32), pltpu.VMEM((width, z.hidden // 2), f32),
                pltpu.VMEM((z.hidden, width), f32), pltpu.VMEM((width, width), f32),
                pltpu.VMEM((width, width), f32), pltpu.SemaphoreType.DMA((4,)),
            ],
            compiler_params=pltpu.CompilerParams(vmem_limit_bytes=24 * 2**20),
            cost_estimate=pl.CostEstimate(flops=5 * 10**9, bytes_accessed=2**22, transcendentals=0),
            name="unpack",
        )(last_bits, *halves, *before)

    grad_gate, grad_up, grad_down, grad_query, grad_key, grad_value, grad_out = unpack(
        False, others, unpack(True, parts, ())
    )
    grad_attention_gain, grad_feed_gain, grad_bias = pl.pallas_call(
        unpack_small_body,
        in_specs=[SCALARS, vmem],
        out_shape=[shape(1, width)] * 2 + [shape(2, heads)],
        name="unpack_small",
    )(sec, small)
    return (
        section_output[None],
        input_grads[None],
        grad_attention_gain,
        grad_query[None],
        grad_key[None],
        grad_value[None],
        grad_out[None],
        grad_bias.T[None],
        grad_feed_gain,
        grad_gate[None],
        grad_up[None],
        grad_down[None],
    )


def solution(mesh):
    placed = (
        P(None, "dp", None),
        P(None, "dp"),
        P(None, "dp"),
        P(None, "dp"),
        P(None, "dp", None),
        P("section", None),
        P("section", None, None),
        P("section", None, None),
        P("section", None, None),
        P("section", None, None),
        P("section", None, None),
        P("section", None),
        P("section", None, None),
        P("section", None, None),
        P("section", None, None),
    )
    return jax.shard_map(
        per_device,
        mesh=mesh,
        in_specs=placed,
        out_specs=(
            P("section", None, "dp", None),
            P("section", None, "dp", None),
            P("section", None),
            P("section", None, None),
            P("section", None, None),
            P("section", None, None),
            P("section", None, None),
            P("section", None, None),
            P("section", None),
            P("section", None, None),
            P("section", None, None),
            P("section", None, None),
        ),
        check_vma=False,
    )
```
